32 devices in a mesh: dp: 8 (over z, x), tensor: 4 (over y, core).
Axes of the slice: x: 2, y: 2, z: 4, core: 2. Of those that a mesh axis runs over, the one named last changes fastest.
Arguments:
- tokens: bfloat16 [16, 4, 128, 1024], P(None, 'tensor', 'dp'), may hold values from -6 to 6
- grad_output: bfloat16 [16, 4, 128, 1024], P(None, 'tensor', 'dp'), may hold values from -6 to 6
- query_weight: bfloat16 [1024, 1024], P('dp', 'tensor'), may hold values from -0.1875 to 0.1875
- key_weight: bfloat16 [1024, 1024], P('dp', 'tensor'), may hold values from -0.1875 to 0.1875
- value_weight: bfloat16 [1024, 1024], P('dp', 'tensor'), may hold values from -0.1875 to 0.1875
- rates_weight: bfloat16 [1024, 24], P('dp', 'tensor'), may hold values from -0.1875 to 0.1875
- out_weight: bfloat16 [1024, 1024], P('dp', 'tensor'), may hold values from -0.75 to 0.75
- gate_weight: bfloat16 [1024, 2816], P('dp', 'tensor'), may hold values from -0.1875 to 0.1875
- up_weight: bfloat16 [1024, 2816], P('dp', 'tensor'), may hold values from -0.1875 to 0.1875
- down_weight: bfloat16 [1024, 2816], P('dp', 'tensor'), may hold values from -0.109375 to 0.109375
- norm1_gain: bfloat16 [1024], P('dp'), may hold values from 0.5 to 1.5
- norm2_gain: bfloat16 [1024], P('dp'), may hold values from 0.5 to 1.5
- persist_key: bfloat16 [8, 16, 128], P('tensor'), may hold values from -5 to 5
- persist_value: bfloat16 [8, 16, 128], P('tensor'), may hold values from -5 to 5
- memory_first: float32 [8, 128, 128], P('tensor'), may hold values from -0.5 to 0.5
- memory_second: float32 [8, 128, 128], P('tensor'), may hold values from -0.5 to 0.5
- seq_lengths: int32 [16], replicated, may hold values from 256 to 512, as said below
- deal: int32 [16], replicated, may hold values from 0 to 15, each once
Outputs:
- layer_out: bfloat16 [16, 4, 128, 1024], P(None, 'tensor', 'dp')
- grad_tokens: bfloat16 [16, 4, 128, 1024], P(None, 'tensor', 'dp')
- grad_query: float32 [1024, 1024], P('dp', 'tensor')
- grad_key: float32 [1024, 1024], P('dp', 'tensor')
- grad_value: float32 [1024, 1024], P('dp', 'tensor')
- grad_rates: float32 [1024, 24], P('dp', 'tensor')
- grad_out: float32 [1024, 1024], P('dp', 'tensor')
- grad_gate: float32 [1024, 2816], P('dp', 'tensor')
- grad_up: float32 [1024, 2816], P('dp', 'tensor')
- grad_down: float32 [1024, 2816], P('dp', 'tensor')
- grad_norm1: float32 [1024], replicated
- grad_norm2: float32 [1024], replicated
- grad_persist_key: float32 [8, 16, 128], P('tensor')
- grad_persist_value: float32 [8, 16, 128], P('tensor')
- grad_memory_first: float32 [8, 128, 128], P('tensor')
- grad_memory_second: float32 [8, 128, 128], P('tensor')
The draws below stay inside these ranges and needn't reach their ends.
Inputs may be any that keep to these rules, and one draw needn't show every extreme that they name: `seq_lengths`: at least one sequence has 512 tokens; slots at and past a sequence's length are padding. A permutation; sequence s is in micro-batch deal[s] // 8 and is handled by dp device deal[s] % 8.
All inputs are finite; a program needn't handle non-finite values.
Results may differ from the reference program's by a relative error of at most 0.017.
Values may be sent and summed in bfloat16 or wider, within the bound.
No kernel may reach another device: no remote copies, remote signals or barrier semaphores. Data moves between devices by JAX's collectives and lax.ppermute only.
A program may use at most 192 MiB of HBM per device.

```python
from functools import partial
import jax
import jax.numpy as jnp
from jax import lax

HEADS = 8
HEAD_DIM = 128
D = 1024
FF = 2816
MEM_HIDDEN = 128
PERSIST = 16
CH = 64
WINDOW = 256
QB = 512
LMAX = 512
LMIN = 256
MB = 2
SEQS = 16
QUART = 128
N_DP = 8
N_TENSOR = 4


def draw_seq_lengths(key, part):
    key = jax.random.fold_in(key, 11)
    length_key, pick_key = jax.random.split(key)
    lengths = jax.random.randint(length_key, (SEQS,), LMIN, LMAX + 1)
    longest = jax.random.randint(pick_key, (), 0, SEQS)
    return jnp.where(jnp.arange(SEQS) == longest, LMAX, lengths).astype(jnp.int32)


def level_of(rng, shape, cuts, low, largest):
    loudness, own = 1.0, jax.random.fold_in(rng, 6)
    for position, blocks in cuts:
        steps = jnp.exp(jax.random.uniform(jax.random.fold_in(own, position), (blocks,), jnp.float32, low / len(cuts), largest / len(cuts)))
        loudness = loudness * jnp.repeat(steps, shape[position] // blocks).reshape([-1 if axis == position else 1 for axis in range(len(shape))])
    return loudness


def centred(key, dims, deviation, bound, shards=(), held_as=jnp.bfloat16):
    values = jax.random.normal(key, dims, jnp.float32) * deviation
    if len(shards) > 0:
        values = level_of(key, dims, shards, -0.22, 0.18) * values
    return jnp.clip(values, min=-bound, max=bound).astype(held_as)


def setup_inputs(seed: int = 0) -> dict:
    streams_of = jax.random.split(jax.random.key(seed), 19)
    tokens = centred(streams_of[0], (SEQS, N_TENSOR, QUART, D), 1.0, 6.0, ((1, 4), (2, 8)))
    grad_output = centred(streams_of[1], (SEQS, N_TENSOR, QUART, D), 1.0, 6.0, ((1, 4), (2, 8)))
    query_weight = centred(streams_of[2], (D, D), D ** -0.5, 0.1875, ((0, 8), (1, 4)))
    key_weight = centred(streams_of[3], (D, D), D ** -0.5, 0.1875, ((0, 8), (1, 4)))
    value_weight = centred(streams_of[4], (D, D), D ** -0.5, 0.1875, ((0, 8), (1, 4)))
    rates_weight = centred(streams_of[5], (D, 3 * HEADS), D ** -0.5, 0.1875, ((0, 8), (1, 4)))
    out_weight = centred(streams_of[6], (D, D), (D // 16) ** -0.5, 0.75, ((0, 8), (1, 4)))
    gate_weight = centred(streams_of[7], (D, FF), D ** -0.5, 0.1875, ((0, 8), (1, 4)))
    up_weight = centred(streams_of[8], (D, FF), D ** -0.5, 0.1875, ((0, 8), (1, 4)))
    down_weight = centred(streams_of[9], (D, FF), FF ** -0.5, 0.109375, ((0, 8), (1, 4)))
    norm1_gain = jnp.clip(1.0 + 0.1 * jax.random.normal(streams_of[10], (D,), jnp.float32), 0.5, 1.5).astype(jnp.bfloat16)
    norm2_gain = jnp.clip(1.0 + 0.1 * jax.random.normal(streams_of[11], (D,), jnp.float32), 0.5, 1.5).astype(jnp.bfloat16)
    persist_key = centred(streams_of[12], (HEADS, PERSIST, HEAD_DIM), 1.0, 5.0, ((0, 4),))
    persist_value = centred(streams_of[13], (HEADS, PERSIST, HEAD_DIM), 1.0, 5.0, ((0, 4),))
    memory_first = centred(streams_of[14], (HEADS, HEAD_DIM, MEM_HIDDEN), HEAD_DIM ** -0.5, 0.5, ((0, 4),), jnp.float32)
    memory_second = centred(streams_of[15], (HEADS, MEM_HIDDEN, HEAD_DIM), MEM_HIDDEN ** -0.5, 0.5, ((0, 4),), jnp.float32)
    seq_lengths = draw_seq_lengths(jax.random.fold_in(streams_of[18], 71), 0)
    deal = jax.random.permutation(streams_of[17], SEQS).astype(jnp.int32)
    return {"tokens": tokens, "grad_output": grad_output, "query_weight": query_weight, "key_weight": key_weight, "value_weight": value_weight, "rates_weight": rates_weight, "out_weight": out_weight, "gate_weight": gate_weight, "up_weight": up_weight, "down_weight": down_weight, "norm1_gain": norm1_gain, "norm2_gain": norm2_gain, "persist_key": persist_key, "persist_value": persist_value, "memory_first": memory_first, "memory_second": memory_second, "seq_lengths": seq_lengths, "deal": deal}


@jax.custom_vjp
def low(v):
    return lax.optimization_barrier(v.astype(jnp.bfloat16)).astype(jnp.float32)

@jax.custom_vjp
def low_back(v):
    return v

def low_keep(v):
    return (low(v), None)

def low_pass(kept, grad):
    return (grad,)

def back_keep(v):
    return (v, None)

def back_low(kept, grad):
    return (low(grad),)
low.defvjp(low_keep, low_pass)
low_back.defvjp(back_keep, back_low)

def highest(left, right):
    return jnp.dot(left, right, precision=lax.Precision.HIGHEST, preferred_element_type=jnp.float32)

def row_norm(values_in):
    return values_in * lax.rsqrt(lax.optimization_barrier(jnp.mean(values_in * values_in, axis=-1, keepdims=True)) + 1e-06)

def memory_span(carry_in, pieces):
    first_layer, second_layer, moment_first, moment_second = carry_in
    span_keys, span_values, span_queries, span_rates, span_live = pieces
    recalled = highest(jax.nn.silu(highest(span_queries, first_layer)), second_layer)
    pre_act = highest(span_keys, first_layer)
    sigmoid_pre = jax.nn.sigmoid(pre_act)
    activated = pre_act * sigmoid_pre
    mismatch = highest(activated, second_layer) - span_values
    weighting = 2.0 * span_rates[:, 0] * span_live / (span_live.shape[0] * span_keys.shape[1])
    mismatch_grad = mismatch * weighting[:, None]
    grad_second = highest(activated.T, mismatch_grad)
    grad_pre = highest(mismatch_grad, second_layer.T) * sigmoid_pre * (1.0 + pre_act * (1.0 - sigmoid_pre))
    grad_first = highest(span_keys.T, grad_pre)
    momentum = jnp.mean(span_rates[:, 1])
    forget = 0.5 * jnp.mean(span_rates[:, 2])
    moment_first = momentum * moment_first - grad_first
    moment_second = momentum * moment_second - grad_second
    first_layer = (1.0 - forget) * first_layer + moment_first
    second_layer = (1.0 - forget) * second_layer + moment_second
    return ((first_layer, second_layer, moment_first, moment_second), recalled)

def head_mix(queries, keys, values, rates, persist_keys, persist_values, first_layer, second_layer, length, span_len, window, block_rows):
    row_total = queries.shape[0]
    spans = row_total // span_len
    live_rows = (jnp.arange(row_total, dtype=jnp.int32) < length).astype(jnp.float32)

    def grouped(tensor_in):
        return tensor_in.reshape((spans, span_len) + tensor_in.shape[1:])
    blank_first = jnp.zeros_like(first_layer)
    blank_second = jnp.zeros_like(second_layer)
    carried, recalled = lax.scan(jax.checkpoint(memory_span), (first_layer, second_layer, blank_first, blank_second), (grouped(row_norm(keys)), grouped(values), grouped(row_norm(queries)), grouped(rates), grouped(live_rows)))
    recalled = recalled.reshape(row_total, -1)
    padded_keys = jnp.pad(keys, ((window, 0), (0, 0)))
    padded_values = jnp.pad(values, ((window, 0), (0, 0)))
    starts = (jnp.arange(row_total // block_rows) * block_rows).astype(jnp.int32)
    groups = block_rows // span_len

    def attend(block_start):
        scaled = lax.dynamic_slice_in_dim(queries, block_start, block_rows, 0) * queries.shape[1] ** (-0.5)
        near_keys = lax.dynamic_slice_in_dim(padded_keys, block_start, block_rows + window, 0)
        near_values = lax.dynamic_slice_in_dim(padded_values, block_start, block_rows + window, 0)
        near_recalled = lax.dynamic_slice_in_dim(recalled, block_start, block_rows, 0).reshape(groups, span_len, -1)
        positions = block_start + jnp.arange(block_rows, dtype=jnp.int32)
        key_positions = block_start - window + jnp.arange(block_rows + window, dtype=jnp.int32)
        near_ok = (key_positions[None, :] <= positions[:, None]) & (key_positions[None, :] > positions[:, None] - window) & (key_positions[None, :] >= 0)
        recall_ok = (positions < length).reshape(groups, 1, span_len)
        persist_scores = highest(scaled, persist_keys.T)
        near_scores = jnp.where(near_ok, highest(scaled, near_keys.T), -1e+30)
        recall_scores = jnp.where(recall_ok, jnp.einsum('gqd,gkd->gqk', scaled.reshape(groups, span_len, -1), near_recalled, precision=lax.Precision.HIGHEST), -1e+30)
        top_rows = jnp.maximum(jnp.maximum(lax.optimization_barrier(jnp.max(persist_scores, axis=1)), lax.optimization_barrier(jnp.max(near_scores, axis=1))), lax.optimization_barrier(jnp.max(recall_scores, axis=2)).reshape(block_rows))
        persist_exp = jnp.exp(persist_scores - top_rows[:, None])
        near_exp = jnp.exp(near_scores - top_rows[:, None])
        recall_exp = jnp.exp(recall_scores - top_rows.reshape(groups, span_len, 1))
        denominator = lax.optimization_barrier(jnp.sum(persist_exp, axis=1)) + lax.optimization_barrier(jnp.sum(near_exp, axis=1)) + lax.optimization_barrier(jnp.sum(recall_exp, axis=2)).reshape(block_rows)
        weighted = highest(persist_exp, persist_values) + highest(near_exp, near_values)
        weighted = weighted + jnp.einsum('gqk,gkd->gqd', recall_exp, near_recalled, precision=lax.Precision.HIGHEST).reshape(block_rows, -1)
        return weighted / denominator[:, None]
    return lax.map(jax.checkpoint(attend), starts).reshape(row_total, -1)

def mix_heads(queries, keys, values, logits, persist_keys, persist_values, first_layer, second_layer, length, span_len, window, block_rows):
    row_total = queries.shape[0]
    head_count = persist_keys.shape[0]

    def by_head(tensor_in):
        return tensor_in.reshape(row_total, head_count, -1).transpose(1, 0, 2)
    per_head = partial(head_mix, length=length, span_len=span_len, window=window, block_rows=block_rows)
    outputs = jax.vmap(per_head)(by_head(queries), by_head(keys), by_head(values), by_head(jax.nn.sigmoid(logits)), persist_keys, persist_values, first_layer, second_layer)
    return outputs.transpose(1, 0, 2).reshape(row_total, -1)

def layer_forward(token_rows, params, length):
    query_weight, key_weight, value_weight, rates_weight, out_weight, gate_weight, up_weight, down_weight, norm1_gain, norm2_gain, persist_key, persist_value, memory_first, memory_second = params
    row_total = token_rows.shape[0]
    live_mask = (jnp.arange(row_total, dtype=jnp.int32) < length).astype(jnp.float32)[:, None]
    normed_first = low(row_norm(token_rows) * norm1_gain)
    queries = low_back(highest(normed_first, query_weight))
    keys = low_back(highest(normed_first, key_weight))
    values = low_back(highest(normed_first, value_weight))
    rate_logits = low_back(highest(normed_first, rates_weight))
    mixed = low(mix_heads(queries, keys, values, rate_logits, persist_key, persist_value, memory_first, memory_second, length, CH, WINDOW, QB))
    attended = low_back(highest(mixed, out_weight.T))
    residual = token_rows + attended
    normed_second = low(row_norm(residual) * norm2_gain)
    gate_pre = low_back(highest(normed_second, gate_weight))
    up_pre = low_back(highest(normed_second, up_weight))
    hidden = low(jax.nn.silu(gate_pre) * up_pre)
    feed_rows = low_back(highest(hidden, down_weight.T))
    return live_mask * (residual + feed_rows)

def reference(tokens, grad_output, query_weight, key_weight, value_weight, rates_weight, out_weight, gate_weight, up_weight, down_weight, norm1_gain, norm2_gain, persist_key, persist_value, memory_first, memory_second, seq_lengths, deal):
    params = (query_weight.astype(jnp.float32), key_weight.astype(jnp.float32), value_weight.astype(jnp.float32), rates_weight.astype(jnp.float32), out_weight.astype(jnp.float32), gate_weight.astype(jnp.float32), up_weight.astype(jnp.float32), down_weight.astype(jnp.float32), norm1_gain.astype(jnp.float32), norm2_gain.astype(jnp.float32), persist_key.astype(jnp.float32), persist_value.astype(jnp.float32), memory_first.astype(jnp.float32), memory_second.astype(jnp.float32))
    batch_of = deal // N_DP
    in_batch = batch_of[None, :] == jnp.arange(MB, dtype=jnp.int32)[:, None]
    batch_tokens = lax.optimization_barrier(jnp.sum(jnp.where(in_batch, seq_lengths[None, :], 0), axis=1)).astype(jnp.float32)
    batch_scale = jnp.sum(seq_lengths).astype(jnp.float32) / (MB * batch_tokens)
    seq_scale = lax.optimization_barrier(jnp.sum(jnp.where(in_batch, batch_scale[:, None], 0.0), axis=0))
    token_seqs = tokens.astype(jnp.float32).reshape(SEQS, LMAX, D)
    cot_seqs = grad_output.astype(jnp.float32).reshape(SEQS, LMAX, D)
    zero_grads = jax.tree.map(jnp.zeros_like, params)

    def one_sequence(totals, inputs):
        token_rows, cot_rows, length, scaling = inputs

        def forward(rows_in, weights_in):
            return layer_forward(rows_in, weights_in, length)
        outputs, pullback = jax.vjp(forward, token_rows, params)
        row_grads, weight_grads = pullback(cot_rows * scaling)
        return (jax.tree.map(jnp.add, totals, weight_grads), (outputs, row_grads))
    totals, (outputs, row_grads) = lax.scan(one_sequence, zero_grads, (token_seqs, cot_seqs, seq_lengths, seq_scale))
    return (outputs.reshape(tokens.shape).astype(jnp.bfloat16), row_grads.reshape(tokens.shape).astype(jnp.bfloat16), totals[0], totals[1], totals[2], totals[3], totals[4], totals[5], totals[6], totals[7], totals[8], totals[9], totals[10], totals[11], totals[12], totals[13])
```

```python
from functools import partial

import jax
import jax.numpy as jnp
from jax import lax
from jax.experimental import pallas as pl
from jax.experimental.pallas import tpu as pltpu
from jax.sharding import Mesh
from jax.sharding import PartitionSpec as P

CH = 64
WINDOW = 256
EPS = 1e-06
NEG = -1e30
BF = jnp.bfloat16
F32 = jnp.float32


def _nn(a, b):
    return lax.dot_general(a, b, (((1,), (0,)), ((), ())), preferred_element_type=F32)


def _nt(a, b):
    return lax.dot_general(a, b, (((1,), (1,)), ((), ())), preferred_element_type=F32)


def _tn(a, b):
    return lax.dot_general(a, b, (((0,), (0,)), ((), ())), preferred_element_type=F32)


def _sig(v):
    return 1.0 / (1.0 + jnp.exp(-v))


def _scale_of(v):
    return lax.rsqrt(jnp.mean(v * v, axis=-1, keepdims=True) + EPS)


def _lane(shape, dim):
    return lax.broadcasted_iota(jnp.int32, shape, dim)


def _masks():
    rows = _lane((128, 128), 0)
    cols = _lane((128, 128), 1)
    return cols > rows, cols <= rows, (rows // CH) == (cols // CH)


def _scores(qs, near_keys, read_b, pkey, block, length, masks):
    older, newer, same_span = masks
    read_ok = same_span & (block * 128 + _lane((128, 128), 1) < length)
    parts = [_nt(qs, pkey), jnp.where(read_ok, _nt(qs, read_b), NEG)]
    for back, keys in near_keys:
        part = _nt(qs, keys)
        if back == 2:
            part = jnp.where(older, part, NEG)
        elif back == 0:
            part = jnp.where(newer, part, NEG)
        parts.append(part)
    return parts


def _spot(place, quarter):
    there = place ^ quarter
    return pl.multiple_of((((there & 1) << 1) | (there >> 1)) * 128, 128)


def _load_rows(place, length, qkv_ref, heads, qn_s, kn_s, qs_s, kb_s, v_s, vb_s, w_s, r_s):
    width = heads * 128
    for quarter in range(4):
        source = pl.ds(_spot(place, quarter), 128)
        here = pl.ds(quarter * 128, 128)
        live = (quarter * 128 + _lane((128, 1), 0) < length).astype(F32)
        rates = _sig(qkv_ref[source, 3 * width : 3 * width + 128])
        r_s[here, :] = rates
        for head in range(heads):
            at = slice(head * 128, (head + 1) * 128)
            q = qkv_ref[source, head * 128 : (head + 1) * 128]
            k = qkv_ref[source, width + head * 128 : width + (head + 1) * 128]
            v = qkv_ref[source, 2 * width + head * 128 : 2 * width + (head + 1) * 128]
            qn_s[here, at] = (q * _scale_of(q)).astype(BF)
            kn_s[here, at] = (k * _scale_of(k)).astype(BF)
            qs_s[here, at] = (q * (128 ** (-0.5))).astype(BF)
            kb_s[here, at] = k.astype(BF)
            v_s[here, at] = v
            vb_s[here, at] = v.astype(BF)
            weighting = rates[:, 3 * head : 3 * head + 1] * live * (2.0 / (CH * 128))
            w_s[here, at] = jnp.broadcast_to(weighting, (128, 128))


def _fwd_kernel(
    heads,
    where_ref,
    qkv_ref,
    pk_ref,
    pv_ref,
    m1_ref,
    m2_ref,
    mixed_ref,
    reads_ref,
    lse_ref,
    states_ref,
    qn_s,
    kn_s,
    qs_s,
    kb_s,
    v_s,
    vb_s,
    w_s,
    r_s,
):
    place = where_ref[0]
    length = where_ref[1]
    _load_rows(place, length, qkv_ref, heads, qn_s, kn_s, qs_s, kb_s, v_s, vb_s, w_s, r_s)
    carry = [
        [m1_ref[h], m2_ref[h], jnp.zeros((128, 128), F32), jnp.zeros((128, 128), F32)]
        for h in range(heads)
    ]
    for span in range(8):
        rows = slice(span * CH, (span + 1) * CH)
        means = jnp.mean(r_s[rows, :], axis=0, keepdims=True)
        for head in range(heads):
            at = slice(head * 128, (head + 1) * 128)
            first, second, s1, s2 = carry[head]
            first_b, second_b = first.astype(BF), second.astype(BF)
            states_ref[span, 0, head] = first_b
            states_ref[span, 1, head] = second_b
            states_ref[span, 2, head] = s1.astype(BF)
            states_ref[span, 3, head] = s2.astype(BF)
            kn = kn_s[rows, at]
            qn = qn_s[rows, at]
            both = _nn(jnp.concatenate([kn, qn], axis=0), first_b)
            both = both * _sig(both) if span == 7 else both
            if span < 7:
                pre = both[:CH]
                sig = _sig(both)
                act_both = both * sig
                sig_k = sig[:CH]
            else:
                act_both = both
            out_both = _nn(act_both.astype(BF), second_b)
            reads_ref[rows, at] = out_both[CH:].astype(BF)
            if span < 7:
                act = act_both[:CH]
                miss = (out_both[:CH] - v_s[rows, at]) * w_s[rows, at]
                miss_b = miss.astype(BF)
                grad_second = _tn(act.astype(BF), miss_b)
                grad_pre = _nt(miss_b, second_b) * sig_k * (1.0 + pre * (1.0 - sig_k))
                grad_first = _tn(kn, grad_pre.astype(BF))
                eta = means[:, 3 * head + 1 : 3 * head + 2]
                keep = 1.0 - 0.5 * means[:, 3 * head + 2 : 3 * head + 3]
                s1 = eta * s1 - grad_first
                s2 = eta * s2 - grad_second
                carry[head] = [keep * first + s1, keep * second + s2, s1, s2]
    masks = _masks()
    for block in range(4):
        rows = slice(block * 128, (block + 1) * 128)
        target = pl.ds(_spot(place, block), 128)
        lse_all = jnp.zeros((128, 128), F32)
        for head in range(heads):
            at = slice(head * 128, (head + 1) * 128)
            qs = qs_s[rows, at]
            near = [
                (back, slice((block - back) * 128, (block - back + 1) * 128))
                for back in (2, 1, 0)
                if block - back >= 0
            ]
            read_b = reads_ref[rows, at]
            parts = _scores(
                qs, [(b, kb_s[r, at]) for b, r in near], read_b, pk_ref[head], block, length, masks
            )
            top = jnp.max(parts[0], axis=1, keepdims=True)
            wide = parts[1]
            for part in parts[2:]:
                wide = jnp.maximum(wide, part)
            top = jnp.maximum(top, jnp.max(wide, axis=1, keepdims=True))
            exps = [jnp.exp(part - top) for part in parts]
            wide = exps[1]
            for part in exps[2:]:
                wide = wide + part
            total = jnp.sum(exps[0], axis=1, keepdims=True) + jnp.sum(wide, axis=1, keepdims=True)
            acc = _nn(exps[0].astype(BF), pv_ref[head]) + _nn(exps[1].astype(BF), read_b)
            for (_, r), part in zip(near, exps[2:]):
                acc = acc + _nn(part.astype(BF), vb_s[r, at])
            mixed_ref[target, at] = (acc / total).astype(BF)
            lse_all = jnp.where(
                _lane((128, 128), 1) == head, jnp.broadcast_to(top + jnp.log(total), (128, 128)), lse_all
            )
        lse_ref[rows, :] = lse_all


def _bwd_kernel(
    heads,
    where_ref,
    qkv_ref,
    pk_ref,
    pv_ref,
    mixed_ref,
    reads_ref,
    lse_ref,
    states_ref,
    dmix_ref,
    dqkv_ref,
    dz_ref,
    dpk_ref,
    dpv_ref,
    dm1_ref,
    dm2_ref,
    qn_s,
    kn_s,
    qs_s,
    kb_s,
    v_s,
    vb_s,
    w_s,
    r_s,
    dq_s,
    dk_s,
    dv_s,
    dr_s,
    dqn_s,
    dkn_s,
    dz_s,
):
    place = where_ref[0]
    length = where_ref[1]
    width = heads * 128
    _load_rows(place, length, qkv_ref, heads, qn_s, kn_s, qs_s, kb_s, v_s, vb_s, w_s, r_s)
    masks = _masks()
    scale = 128 ** (-0.5)
    for head in range(heads):
        at = slice(head * 128, (head + 1) * 128)
        dpk = jnp.zeros((16, 128), F32)
        dpv = jnp.zeros((16, 128), F32)
        dk = [jnp.zeros((128, 128), F32)] * 4
        dv = [jnp.zeros((128, 128), F32)] * 4
        for block in range(4):
            rows = slice(block * 128, (block + 1) * 128)
            source = pl.ds(_spot(place, block), 128)
            qs = qs_s[rows, at]
            near = [
                (back, slice((block - back) * 128, (block - back + 1) * 128))
                for back in (2, 1, 0)
                if block - back >= 0
            ]
            read_b = reads_ref[rows, at]
            parts = _scores(
                qs, [(b, kb_s[r, at]) for b, r in near], read_b, pk_ref[head], block, length, masks
            )
            lse = lse_ref[rows, head : head + 1]
            probs = [jnp.exp(part - lse) for part in parts]
            dout = dmix_ref[source, at]
            dout_b = dout.astype(BF)
            dot = jnp.sum(dout * mixed_ref[source, at].astype(F32), axis=1, keepdims=True)
            values = [pv_ref[head], read_b] + [vb_s[r, at] for _, r in near]
            keys = [pk_ref[head], read_b] + [kb_s[r, at] for _, r in near]
            ds_b = [
                (p * (_nt(dout_b, val) - dot)).astype(BF) for p, val in zip(probs, values)
            ]
            probs_b = [p.astype(BF) for p in probs]
            dq = _nn(ds_b[0], keys[0])
            for d, key in zip(ds_b[1:], keys[1:]):
                dq = dq + _nn(d, key)
            dq_s[rows, at] = dq * scale
            dpk = dpk + _tn(ds_b[0], qs)
            dpv = dpv + _tn(probs_b[0], dout_b)
            dr_s[rows, at] = _tn(ds_b[1], qs) + _tn(probs_b[1], dout_b)
            for (back, _), d, p in zip(near, ds_b[2:], probs_b[2:]):
                dk[block - back] = dk[block - back] + _tn(d, qs)
                dv[block - back] = dv[block - back] + _tn(p, dout_b)
            if block >= 2:
                dk_s[(block - 2) * 128 : (block - 1) * 128, at] = dk[block - 2]
                dv_s[(block - 2) * 128 : (block - 1) * 128, at] = dv[block - 2]
        for block in (2, 3):
            rows = slice(block * 128, (block + 1) * 128)
            dk_s[rows, at] = dk[block]
            dv_s[rows, at] = dv[block]
        dpk_ref[head] = dpk
        dpv_ref[head] = dpv
    zero = jnp.zeros((128, 128), F32)
    carry = [[zero, zero, zero, zero] for _ in range(heads)]
    lanes = _lane((CH, 128), 1)
    for span in range(7, -1, -1):
        rows = slice(span * CH, (span + 1) * CH)
        means = jnp.mean(r_s[rows, :], axis=0, keepdims=True)
        dr_row = jnp.zeros((CH, 128), F32)
        live = (span * CH + _lane((CH, 1), 0) < length).astype(F32)
        for head in range(heads):
            at = slice(head * 128, (head + 1) * 128)
            a1, a2, b1, b2 = carry[head]
            first_b = states_ref[span, 0, head]
            second_b = states_ref[span, 1, head]
            kn = kn_s[rows, at]
            qn = qn_s[rows, at]
            dread_b = dr_s[rows, at].astype(BF)
            both = _nn(jnp.concatenate([kn, qn], axis=0), first_b)
            sig_both = _sig(both)
            act_both = both * sig_both
            slope_both = sig_both * (1.0 + both * (1.0 - sig_both))
            act_b = act_both.astype(BF)
            db_b = (_nt(dread_b, second_b) * slope_both[CH:]).astype(BF)
            if span == 7:
                dqn_s[rows, at] = _nt(db_b, first_b)
                dkn_s[rows, at] = jnp.zeros((CH, 128), F32)
                carry[head] = [_tn(qn, db_b), _tn(act_b[CH:], dread_b), zero, zero]
                continue
            eta = means[:, 3 * head + 1 : 3 * head + 2]
            keep = 1.0 - 0.5 * means[:, 3 * head + 2 : 3 * head + 3]
            pre, sig, slope = both[:CH], sig_both[:CH], slope_both[:CH]
            bend = sig * (1.0 - sig) * (2.0 + pre * (1.0 - 2.0 * sig))
            u_b = act_b[:CH]
            w = w_s[rows, at]
            e = _nn(u_b, second_b) - v_s[rows, at]
            m_b = (e * w).astype(BF)
            p = _nt(m_b, second_b)
            g_b = (p * slope).astype(BF)
            ds1 = b1 + a1
            ds2 = b2 + a2
            dg1_b = (-ds1).astype(BF)
            dg2_b = (-ds2).astype(BF)
            x1 = _nn(kn, dg1_b)
            dp_b = (x1 * slope).astype(BF)
            dm = _nn(dp_b, second_b) + _nn(u_b, dg2_b)
            de = dm * w
            de_b = de.astype(BF)
            du = _nt(m_b, dg2_b) + _nt(de_b, second_b)
            da = x1 * p * bend + du * slope
            da_b = da.astype(BF)
            back = _nt(jnp.concatenate([da_b, db_b], axis=0), first_b)
            dkn_s[rows, at] = _nt(g_b, dg1_b) + back[:CH]
            dqn_s[rows, at] = back[CH:]
            dv_s[rows, at] = dv_s[rows, at] - de
            new1 = keep * a1 + _tn(
                jnp.concatenate([kn, qn], axis=0), jnp.concatenate([da_b, db_b], axis=0)
            )
            new2 = (
                keep * a2
                + _tn(act_b, jnp.concatenate([de_b, dread_b], axis=0))
                + _tn(dp_b, m_b)
            )
            prev1 = states_ref[span, 2, head].astype(F32)
            prev2 = states_ref[span, 3, head].astype(F32)
            deta = jnp.sum(
                jnp.sum(ds1 * prev1 + ds2 * prev2, axis=0, keepdims=True), axis=1, keepdims=True
            )
            dkeep = jnp.sum(
                jnp.sum(a1 * first_b.astype(F32) + a2 * second_b.astype(F32), axis=0, keepdims=True),
                axis=1,
                keepdims=True,
            )
            dw = jnp.sum(dm * e, axis=1, keepdims=True) * live * (2.0 / (CH * 128))
            dr_row = jnp.where(lanes == 3 * head, jnp.broadcast_to(dw, (CH, 128)), dr_row)
            dr_row = jnp.where(
                lanes == 3 * head + 1, jnp.broadcast_to(deta * (1.0 / CH), (CH, 128)), dr_row
            )
            dr_row = jnp.where(
                lanes == 3 * head + 2, jnp.broadcast_to(dkeep * (-0.5 / CH), (CH, 128)), dr_row
            )
            carry[head] = [new1, new2, eta * ds1, eta * ds2]
        rates = r_s[rows, :]
        dz_s[rows, :] = dr_row * rates * (1.0 - rates)
    for head in range(heads):
        dm1_ref[head] = carry[head][0]
        dm2_ref[head] = carry[head][1]
    for quarter in range(4):
        source = pl.ds(_spot(place, quarter), 128)
        here = slice(quarter * 128, (quarter + 1) * 128)
        dz_ref[source, :] = dz_s[here, :].astype(BF)
        for head in range(heads):
            at = slice(head * 128, (head + 1) * 128)
            for part, grad_s, norm_s in ((0, dq_s, dqn_s), (1, dk_s, dkn_s)):
                col = slice(part * width + head * 128, part * width + (head + 1) * 128)
                raw = qkv_ref[source, col]
                inverse = _scale_of(raw)
                normed = raw * inverse
                dn = norm_s[here, at]
                inner = jnp.mean(dn * normed, axis=-1, keepdims=True)
                dqkv_ref[source, col] = (
                    grad_s[here, at] + inverse * (dn - normed * inner)
                ).astype(BF)
            col = slice(2 * width + head * 128, 2 * width + (head + 1) * 128)
            dqkv_ref[source, col] = dv_s[here, at].astype(BF)


def _row_scratch(heads):
    wide = heads * 128
    return [
        pltpu.VMEM((512, wide), BF),
        pltpu.VMEM((512, wide), BF),
        pltpu.VMEM((512, wide), BF),
        pltpu.VMEM((512, wide), BF),
        pltpu.VMEM((512, wide), F32),
        pltpu.VMEM((512, wide), BF),
        pltpu.VMEM((512, wide), F32),
        pltpu.VMEM((512, 128), F32),
    ]


_VM = pl.BlockSpec(memory_space=pltpu.VMEM)
_SM = pl.BlockSpec(memory_space=pltpu.SMEM)


def mix_forward(where, qkv, pk, pv, m1, m2):
    heads = pk.shape[0]
    wide = heads * 128
    return pl.pallas_call(
        partial(_fwd_kernel, heads),
        out_shape=(
            jax.ShapeDtypeStruct((512, wide), BF),
            jax.ShapeDtypeStruct((512, wide), BF),
            jax.ShapeDtypeStruct((512, 128), F32),
            jax.ShapeDtypeStruct((8, 4, heads, 128, 128), BF),
        ),
        in_specs=[_SM] + [_VM] * 5,
        out_specs=(_VM,) * 4,
        scratch_shapes=_row_scratch(heads),
        compiler_params=pltpu.CompilerParams(vmem_limit_bytes=48 * 1024 * 1024),
    )(where, qkv, pk, pv, m1, m2)


def mix_backward(where, qkv, pk, pv, mixed, reads, lse, states, dmix):
    heads = pk.shape[0]
    wide = heads * 128
    return pl.pallas_call(
        partial(_bwd_kernel, heads),
        out_shape=(
            jax.ShapeDtypeStruct((512, 3 * wide), BF),
            jax.ShapeDtypeStruct((512, 128), BF),
            jax.ShapeDtypeStruct((heads, 16, 128), F32),
            jax.ShapeDtypeStruct((heads, 16, 128), F32),
            jax.ShapeDtypeStruct((heads, 128, 128), F32),
            jax.ShapeDtypeStruct((heads, 128, 128), F32),
        ),
        in_specs=[_SM] + [_VM] * 8,
        out_specs=(_VM,) * 6,
        scratch_shapes=_row_scratch(heads)
        + [pltpu.VMEM((512, wide), F32)] * 6
        + [pltpu.VMEM((512, 128), F32)],
        compiler_params=pltpu.CompilerParams(vmem_limit_bytes=48 * 1024 * 1024),
    )(where, qkv, pk, pv, mixed, reads, lse, states, dmix)


DP = ("z", "x")


def _swap(value, axis):
    return lax.ppermute(value, axis, [(0, 1), (1, 0)])


PAIR = [(0, 1), (1, 0), (2, 3), (3, 2)]
MIDDLE = [(1, 2), (2, 1)]
OUTWARD = [(1, 0), (2, 3)]
INWARD = [(0, 1), (3, 2)]


def _line():
    return lax.axis_size("z") == 4


def _block_ids():
    depth = lax.axis_size("z")
    z = lax.axis_index("z")
    x = lax.axis_index("x")
    if not _line():
        return jnp.arange(2 * depth, dtype=jnp.int32)
    low_half = z < 2
    zs = jnp.stack([z, z ^ 1, jnp.where(low_half, 2, 1), jnp.where(low_half, 3, 0)])
    return jnp.concatenate([2 * zs + x, 2 * zs + (x ^ 1)]).astype(jnp.int32)


def _gather_rows(own):
    if not _line():
        return lax.all_gather(own, DP, axis=0)
    middle = (lax.axis_index("z") + 1) // 2 == 1
    pair = lax.ppermute(own, "z", PAIR)
    near = jnp.stack([own, pair])
    crossed = lax.ppermute(near, "z", MIDDLE)
    passed = lax.ppermute(crossed, "z", OUTWARD)
    far = jnp.where(middle, crossed, passed)
    return jnp.concatenate([near, far, _swap(near, "x"), _swap(far, "x")])


def _scatter_rows(keep, send):
    if not _line():
        whole = jnp.concatenate([keep, send.astype(F32)])
        return lax.psum_scatter(whole.astype(BF), DP, scatter_dimension=0).astype(F32)
    total = keep + _swap(send, "x").astype(F32)
    far = total[2:] + lax.ppermute(total[2:].astype(BF), "z", INWARD).astype(F32)
    crossed = lax.ppermute(far.astype(BF), "z", MIDDLE).astype(F32)
    pair = lax.ppermute((total[1] + crossed[1]).astype(BF), "z", PAIR).astype(F32)
    return total[0] + crossed[0] + pair


def _sum_all(value, axes):
    for axis in axes:
        size = lax.axis_size(axis)
        step = 1
        while step < size:
            value = value + lax.ppermute(value, axis, [(i, i ^ step) for i in range(size)])
            step *= 2
    return value


def _gather_slots(own):
    column = jnp.concatenate([own, _swap(own, "y")])
    return jnp.concatenate([column, _swap(column, "c")])


def _scatter_slots(keep, send):
    half = keep.shape[0] // 2
    total = keep + _swap(send, "c").astype(F32)
    return total[:half] + _swap(total[half:].astype(BF), "y").astype(F32)


def _dot(a, b, out=F32):
    return lax.dot_general(a, b, (((1,), (0,)), ((), ())), preferred_element_type=out)


def _dot_t(a, b, out=F32):
    return lax.dot_general(a, b, (((1,), (1,)), ((), ())), preferred_element_type=out)


def _dot_r(a, b, out=F32):
    return lax.dot_general(a, b, (((0,), (0,)), ((), ())), preferred_element_type=out)


def per_device(
    tokens,
    grad_output,
    query_weight,
    key_weight,
    value_weight,
    rates_weight,
    out_weight,
    gate_weight,
    up_weight,
    down_weight,
    norm1_gain,
    norm2_gain,
    persist_key,
    persist_value,
    memory_first,
    memory_second,
    seq_lengths,
    deal,
):
    devices = lax.axis_size("z") * lax.axis_size("x")
    dp_index = lax.axis_index("z") * lax.axis_size("x") + lax.axis_index("x")
    place = lax.axis_index("y") * 2 + lax.axis_index("c")
    seq_count = seq_lengths.shape[0]
    batches = seq_count // devices
    local_rows = tokens.shape[2]
    width = tokens.shape[3]
    quarter = local_rows * devices
    rows_of = query_weight.shape[0]
    head_cols = query_weight.shape[1]
    heads = persist_key.shape[0]
    rate_cols = rates_weight.shape[1]
    hidden_cols = gate_weight.shape[1]
    half = width // 2

    batch_of = deal // devices
    batch_ids = jnp.arange(batches, dtype=jnp.int32)
    batch_tokens = jnp.sum(
        jnp.where(batch_of[None, :] == batch_ids[:, None], seq_lengths[None, :], 0), axis=1
    ).astype(F32)
    batch_scale = jnp.sum(seq_lengths).astype(F32) / (batches * batch_tokens)
    my_seqs = [b * devices + dp_index for b in range(batches)]
    lengths = [seq_lengths[s] for s in my_seqs]
    scales = [batch_scale[batch_of[s]] for s in my_seqs]
    positions = place * quarter + jnp.arange(quarter, dtype=jnp.int32)
    lives = [(positions < n).astype(F32)[:, None] for n in lengths]

    ids = _block_ids()
    order = (ids[:, None] * rows_of + jnp.arange(rows_of, dtype=jnp.int32)[None, :]).reshape(width)
    shuffle = (jnp.arange(width, dtype=jnp.int32)[:, None] == order[None, :]).astype(BF)

    def deal_in(array, b):
        part = array[b * devices : (b + 1) * devices, 0]
        return lax.all_to_all(part, DP, split_axis=0, concat_axis=0, tiled=True).reshape(
            quarter, width
        )

    def deal_out(rows):
        plain = _dot_t(rows.astype(BF), shuffle, BF)
        return lax.all_to_all(
            plain.reshape(devices, local_rows, width), DP, split_axis=0, concat_axis=0, tiled=True
        )

    got_tokens = [deal_in(tokens, b) for b in range(batches)]

    extra = jnp.zeros((16, 3 * head_cols), BF)
    extra = extra.at[0, : rate_cols * rows_of].set(rates_weight.T.reshape(rate_cols * rows_of))
    extra = extra.at[1, :rows_of].set(norm1_gain).at[1, rows_of : 2 * rows_of].set(norm2_gain)
    packed = _gather_rows(
        jnp.concatenate(
            [jnp.concatenate([query_weight, key_weight, value_weight], axis=1), extra], axis=0
        )
    )
    rates_full = (
        packed[:, rows_of, : rate_cols * rows_of]
        .reshape(devices, rate_cols, rows_of)
        .transpose(0, 2, 1)
        .reshape(width, rate_cols)
    )
    project = jnp.concatenate(
        [
            packed[:, :rows_of].reshape(width, 3 * head_cols),
            jnp.pad(rates_full, ((0, 0), (0, 128 - rate_cols))),
        ],
        axis=1,
    )
    gain_one = packed[:, rows_of + 1, :rows_of].reshape(width).astype(F32)
    gain_two = packed[:, rows_of + 1, rows_of : 2 * rows_of].reshape(width).astype(F32)
    out_full = _gather_rows(out_weight).reshape(width, head_cols)
    gate_full = _gather_rows(gate_weight).reshape(width, hidden_cols)
    up_full = _gather_rows(up_weight).reshape(width, hidden_cols)
    down_full = _gather_rows(down_weight).reshape(width, hidden_cols)

    got_cots = [deal_in(grad_output, b) for b in range(batches)]

    span = range(batches)
    token_rows = [_dot(got_tokens[b], shuffle) for b in span]
    inverse_one = [lax.rsqrt(jnp.mean(t * t, axis=-1, keepdims=True) + EPS) for t in token_rows]
    normed_one = [t * i for t, i in zip(token_rows, inverse_one)]
    first = [_gather_slots((n * gain_one).astype(BF)) for n in normed_one]
    where = [jnp.stack([place, lengths[b]]).astype(jnp.int32) for b in span]
    projected = [_dot(first[b], project) for b in span]
    mixes = [
        mix_forward(where[b], projected[b], persist_key, persist_value, memory_first, memory_second)
        for b in span
    ]
    mixed = [m[0] for m in mixes]
    attended = [
        _scatter_slots(
            _dot_t(mixed[b][: 2 * quarter], out_full), _dot_t(mixed[b][2 * quarter :], out_full, BF)
        )
        for b in span
    ]
    residual = [token_rows[b] + attended[b] for b in span]
    inverse_two = [lax.rsqrt(jnp.mean(r * r, axis=-1, keepdims=True) + EPS) for r in residual]
    normed_two = [r * i for r, i in zip(residual, inverse_two)]
    second = [_gather_slots((n * gain_two).astype(BF)) for n in normed_two]
    cot_rows = [
        _dot(got_cots[b], shuffle) * scales[b] * lives[b] for b in span
    ]
    cot_full = [_gather_slots(c.astype(BF)) for c in cot_rows]

    gate_grad, up_grad, hidden = [], [], []
    for b in span:
        gate_pre = _dot(second[b], gate_full)
        up_pre = _dot(second[b], up_full)
        hidden_grad = _dot(cot_full[b], down_full)
        gate_sig = jax.nn.sigmoid(gate_pre)
        hidden.append((gate_pre * gate_sig * up_pre).astype(BF))
        gate_grad.append(
            (hidden_grad * up_pre * gate_sig * (1.0 + gate_pre * (1.0 - gate_sig))).astype(BF)
        )
        up_grad.append((hidden_grad * gate_pre * gate_sig).astype(BF))
    two_grad = [
        _scatter_slots(
            _dot_t(gate_grad[b][: 2 * quarter], gate_full)
            + _dot_t(up_grad[b][: 2 * quarter], up_full),
            (
                _dot_t(gate_grad[b][2 * quarter :], gate_full)
                + _dot_t(up_grad[b][2 * quarter :], up_full)
            ).astype(BF),
        )
        for b in span
    ]
    scaled_two = [g * gain_two for g in two_grad]
    residual_grad = [
        cot_rows[b]
        + inverse_two[b]
        * (
            scaled_two[b]
            - normed_two[b] * jnp.mean(scaled_two[b] * normed_two[b], axis=-1, keepdims=True)
        )
        for b in span
    ]
    mixer_cot = [_gather_slots(r.astype(BF)) for r in residual_grad]
    mixed_grad = [_dot(mixer_cot[b], out_full) for b in span]
    backs = [
        mix_backward(
            where[b], projected[b], persist_key, persist_value, *mixes[b], mixed_grad[b]
        )
        for b in span
    ]
    feed = [
        _scatter_slots(
            _dot_t(hidden[b][: 2 * quarter], down_full),
            _dot_t(hidden[b][2 * quarter :], down_full, BF),
        )
        for b in span
    ]
    layer_out = [deal_out(lives[b] * (residual[b] + feed[b])) for b in span]

    def weight_grad(rows, grads):
        rows = jnp.concatenate(rows)
        grads = jnp.concatenate(grads)
        cols = grads.shape[1]
        keep = _dot_r(rows[:, :half], grads).reshape(devices // 2, rows_of, cols)
        send = _dot_r(rows[:, half:], grads, BF).reshape(devices // 2, rows_of, cols)
        return _scatter_rows(keep, send)

    down_total = weight_grad(cot_full, hidden)
    gate_total = weight_grad(second, gate_grad)
    up_total = weight_grad(second, up_grad)
    out_total = weight_grad(mixer_cot, mixed)

    one_grad = [
        _scatter_slots(
            _dot_t(backs[b][0][: 2 * quarter], project[:, : 3 * head_cols])
            + _dot_t(backs[b][1][: 2 * quarter], project[:, 3 * head_cols :]),
            (
                _dot_t(backs[b][0][2 * quarter :], project[:, : 3 * head_cols])
                + _dot_t(backs[b][1][2 * quarter :], project[:, 3 * head_cols :])
            ).astype(BF),
        )
        for b in span
    ]
    scaled_one = [g * gain_one for g in one_grad]
    token_grad = [
        residual_grad[b]
        + inverse_one[b]
        * (
            scaled_one[b]
            - normed_one[b] * jnp.mean(scaled_one[b] * normed_one[b], axis=-1, keepdims=True)
        )
        for b in span
    ]
    grad_tokens = [deal_out(t) for t in token_grad]

    rows = jnp.concatenate(first)
    project_grad = jnp.concatenate([backs[b][0] for b in span])
    rate_grad = jnp.concatenate([backs[b][1] for b in span])
    rate_total = (
        _dot_r(rate_grad, rows)[:rate_cols]
        .reshape(rate_cols, devices, rows_of)
        .transpose(1, 0, 2)
        .reshape(devices, 1, rate_cols * rows_of)
    )
    rate_total = jnp.pad(
        rate_total, ((0, 0), (0, 15), (0, 3 * head_cols - rate_cols * rows_of))
    )
    keep = _dot_r(rows[:, :half], project_grad).reshape(devices // 2, rows_of, 3 * head_cols)
    send = _dot_r(rows[:, half:], project_grad, BF).reshape(devices // 2, rows_of, 3 * head_cols)
    packed_total = _scatter_rows(
        jnp.concatenate([keep, rate_total[: devices // 2]], axis=1),
        jnp.concatenate([send, rate_total[devices // 2 :].astype(BF)], axis=1),
    )
    project_total = packed_total[:rows_of]
    rates_total = (
        packed_total[rows_of, : rate_cols * rows_of].reshape(rate_cols, rows_of).transpose(1, 0)
    )

    memory = [sum(backs[b][i] for b in span) for i in (2, 3, 4, 5)]
    flat = jnp.concatenate([m.reshape(-1, 128) for m in memory])
    flat = _sum_all(flat, ("x", "z"))
    memory_out = []
    start = 0
    for m in memory:
        size = m.size // 128
        memory_out.append(flat[start : start + size].reshape(m.shape))
        start += size

    gains = jnp.stack(
        [
            sum(jnp.sum(one_grad[b] * normed_one[b], axis=0) for b in span),
            sum(jnp.sum(two_grad[b] * normed_two[b], axis=0) for b in span),
        ]
    ).reshape(2, devices, rows_of)
    place_of = (ids[:, None] == jnp.arange(devices, dtype=jnp.int32)[None, :]).astype(F32)
    gains = jnp.sum(gains[:, :, None, :] * place_of[None, :, :, None], axis=1)
    gains = _sum_all(gains.reshape(2 * devices, rows_of), ("c", "y", "x", "z")).reshape(2, width)

    return (
        jnp.concatenate(layer_out)[:, None],
        jnp.concatenate(grad_tokens)[:, None],
        project_total[:, :head_cols],
        project_total[:, head_cols : 2 * head_cols],
        project_total[:, 2 * head_cols :],
        rates_total,
        out_total,
        gate_total,
        up_total,
        down_total,
        gains[0],
        gains[1],
        memory_out[0],
        memory_out[1],
        memory_out[2],
        memory_out[3],
    )


def solution(mesh):
    sizes = mesh.devices.shape
    fine = Mesh(mesh.devices.reshape(sizes[0] // 2, 2, 2, sizes[1] // 2), ("z", "x", "y", "c"))
    tensor = ("y", "c")
    return jax.shard_map(
        per_device,
        mesh=fine,
        in_specs=(
            P(None, tensor, DP, None),
            P(None, tensor, DP, None),
            P(DP, tensor),
            P(DP, tensor),
            P(DP, tensor),
            P(DP, tensor),
            P(DP, tensor),
            P(DP, tensor),
            P(DP, tensor),
            P(DP, tensor),
            P(DP),
            P(DP),
            P(tensor, None, None),
            P(tensor, None, None),
            P(tensor, None, None),
            P(tensor, None, None),
            P(),
            P(),
        ),
        out_specs=(
            P(None, tensor, DP, None),
            P(None, tensor, DP, None),
            P(DP, tensor),
            P(DP, tensor),
            P(DP, tensor),
            P(DP, tensor),
            P(DP, tensor),
            P(DP, tensor),
            P(DP, tensor),
            P(DP, tensor),
            P(),
            P(),
            P(tensor, None, None),
            P(tensor, None, None),
            P(tensor, None, None),
            P(tensor, None, None),
        ),
        check_vma=False,
    )
```

```python
from functools import partial

import jax
import jax.numpy as jnp
from jax import lax
from jax.experimental import pallas as pl
from jax.experimental.pallas import tpu as pltpu
from jax.sharding import Mesh
from jax.sharding import PartitionSpec as P

CH = 64
WINDOW = 256
EPS = 1e-06
NEG = -1e30
BF = jnp.bfloat16
F32 = jnp.float32


def _nn(a, b):
    return lax.dot_general(a, b, (((1,), (0,)), ((), ())), preferred_element_type=F32)


def _nt(a, b):
    return lax.dot_general(a, b, (((1,), (1,)), ((), ())), preferred_element_type=F32)


def _tn(a, b):
    return lax.dot_general(a, b, (((0,), (0,)), ((), ())), preferred_element_type=F32)


def _sig(v):
    return 1.0 / (1.0 + jnp.exp(-v))


def _scale_of(v):
    return lax.rsqrt(jnp.mean(v * v, axis=-1, keepdims=True) + EPS)


def _lane(shape, dim):
    return lax.broadcasted_iota(jnp.int32, shape, dim)


def _masks():
    rows = _lane((128, 128), 0)
    cols = _lane((128, 128), 1)
    return cols > rows, cols <= rows, (rows // CH) == (cols // CH)


def _scores(qs, near_keys, read_b, pkey, block, length, masks):
    older, newer, same_span = masks
    read_ok = same_span & (block * 128 + _lane((128, 128), 1) < length)
    parts = [_nt(qs, pkey), jnp.where(read_ok, _nt(qs, read_b), NEG)]
    for back, keys in near_keys:
        part = _nt(qs, keys)
        if back == 2:
            part = jnp.where(older, part, NEG)
        elif back == 0:
            part = jnp.where(newer, part, NEG)
        parts.append(part)
    return parts


def _spot(place, quarter):
    there = place ^ quarter
    return pl.multiple_of((((there & 1) << 1) | (there >> 1)) * 128, 128)


def _load_rows(place, length, qkv_ref, heads, qn_s, kn_s, qs_s, kb_s, v_s, vb_s, w_s, r_s):
    width = heads * 128
    for quarter in range(4):
        source = pl.ds(_spot(place, quarter), 128)
        here = pl.ds(quarter * 128, 128)
        live = (quarter * 128 + _lane((128, 1), 0) < length).astype(F32)
        rates = _sig(qkv_ref[source, 3 * width : 3 * width + 128])
        r_s[here, :] = rates
        for head in range(heads):
            at = slice(head * 128, (head + 1) * 128)
            q = qkv_ref[source, head * 128 : (head + 1) * 128]
            k = qkv_ref[source, width + head * 128 : width + (head + 1) * 128]
            v = qkv_ref[source, 2 * width + head * 128 : 2 * width + (head + 1) * 128]
            qn_s[here, at] = (q * _scale_of(q)).astype(BF)
            kn_s[here, at] = (k * _scale_of(k)).astype(BF)
            qs_s[here, at] = (q * (128 ** (-0.5))).astype(BF)
            kb_s[here, at] = k.astype(BF)
            v_s[here, at] = v
            vb_s[here, at] = v.astype(BF)
            weighting = rates[:, 3 * head : 3 * head + 1] * live * (2.0 / (CH * 128))
            w_s[here, at] = jnp.broadcast_to(weighting, (128, 128))


def _copies(blocks, rows, cols, target, sems):
    made = []
    for k, block in enumerate(blocks):
        copy = pltpu.make_async_copy(
            block.at[rows, cols],
            target.at[pl.ds(k * rows.size, rows.size), :],
            sems.at[k],
        )
        copy.start()
        made.append(copy)
    return made


def _fwd_kernel(
    heads,
    blocks,
    batch,
    where_ref,
    own_ref,
    ypart_ref,
    cpart_ref,
    far_ref,
    pk_ref,
    pv_ref,
    m1_ref,
    m2_ref,
    *rest,
):
    weight_refs = rest[:blocks]
    (
        first_ref,
        extra_ref,
        token_ref,
        qkv_ref,
        mixed_ref,
        reads_ref,
        lse_ref,
        states_ref,
        keep_ref,
        send_ref,
        project_s,
        rates_s,
        out_s,
        sems,
    ) = rest[blocks : blocks + 14]
    scratch = rest[blocks + 14 :]
    step = weight_refs[0].shape[0] - 16
    wide = heads * 128
    every = pl.ds(0, step)
    rates_s[16:128, :] = jnp.zeros((112, rates_s.shape[1]), BF)
    extra = []
    for k, block in enumerate(weight_refs):
        copy = pltpu.make_async_copy(
            block.at[pl.ds(step, 16), pl.ds(0, step)],
            rates_s.at[pl.ds(0, 16), pl.ds(k * step, step)],
            sems.at[2, k],
        )
        copy.start()
        extra.append(copy)
    project_copies = _copies(weight_refs, every, pl.ds(0, 3 * wide), project_s, sems.at[0])
    out_copies = _copies(weight_refs, every, pl.ds(3 * wide, wide), out_s, sems.at[1])
    for copy in extra:
        copy.wait()
    extra_rows = rates_s[0:16, :].astype(F32)
    extra_ref[...] = extra_rows
    gain = extra_rows[3 * heads : 3 * heads + 1, :]
    width = blocks * step
    for quarter, ref in enumerate((own_ref, ypart_ref, cpart_ref, far_ref)):
        raw = ref[:, batch].reshape(128, width).astype(F32)
        inverse = _scale_of(raw)
        for k in range(blocks):
            source = pl.ds(pl.multiple_of(where_ref[2 + k] * step, step), step)
            piece = ref[:, batch, :, source].reshape(128, step).astype(F32)
            at = slice(k * step, (k + 1) * step)
            if quarter == 0:
                token_ref[:, at] = piece
            first_ref[quarter * 128 : (quarter + 1) * 128, at] = (
                piece * inverse * gain[:, at]
            ).astype(BF)
    for copy in project_copies:
        copy.wait()
    for quarter in range(4):
        rows = slice(quarter * 128, (quarter + 1) * 128)
        left = first_ref[rows, :]
        qkv_ref[rows, : 3 * wide] = _nn(left, project_s[...])
        qkv_ref[rows, 3 * wide :] = _nt(left, rates_s[...])
    _mix_forward(
        heads,
        where_ref,
        qkv_ref,
        pk_ref,
        pv_ref,
        m1_ref,
        m2_ref,
        mixed_ref,
        reads_ref,
        lse_ref,
        states_ref,
        *scratch,
    )
    for copy in out_copies:
        copy.wait()
    for part in range(2):
        rows = slice(part * 128, (part + 1) * 128)
        send_ref[rows, :] = _nt(mixed_ref[256 + part * 128 : 384 + part * 128, :], out_s[...]).astype(BF)
        keep_ref[rows, :] = _nt(mixed_ref[rows, :], out_s[...])


def _mix_forward(
    heads,
    where_ref,
    qkv_ref,
    pk_ref,
    pv_ref,
    m1_ref,
    m2_ref,
    mixed_ref,
    reads_ref,
    lse_ref,
    states_ref,
    qn_s,
    kn_s,
    qs_s,
    kb_s,
    v_s,
    vb_s,
    w_s,
    r_s,
):
    place = where_ref[0]
    length = where_ref[1]
    _load_rows(place, length, qkv_ref, heads, qn_s, kn_s, qs_s, kb_s, v_s, vb_s, w_s, r_s)
    carry = [
        [m1_ref[h], m2_ref[h], jnp.zeros((128, 128), F32), jnp.zeros((128, 128), F32)]
        for h in range(heads)
    ]
    for span in range(8):
        rows = slice(span * CH, (span + 1) * CH)
        means = jnp.mean(r_s[rows, :], axis=0, keepdims=True)
        for head in range(heads):
            at = slice(head * 128, (head + 1) * 128)
            first, second, s1, s2 = carry[head]
            first_b, second_b = first.astype(BF), second.astype(BF)
            states_ref[span, 0, head] = first_b
            states_ref[span, 1, head] = second_b
            states_ref[span, 2, head] = s1.astype(BF)
            states_ref[span, 3, head] = s2.astype(BF)
            kn = kn_s[rows, at]
            qn = qn_s[rows, at]
            both = _nn(jnp.concatenate([kn, qn], axis=0), first_b)
            both = both * _sig(both) if span == 7 else both
            if span < 7:
                pre = both[:CH]
                sig = _sig(both)
                act_both = both * sig
                sig_k = sig[:CH]
            else:
                act_both = both
            out_both = _nn(act_both.astype(BF), second_b)
            reads_ref[rows, at] = out_both[CH:].astype(BF)
            if span < 7:
                act = act_both[:CH]
                miss = (out_both[:CH] - v_s[rows, at]) * w_s[rows, at]
                miss_b = miss.astype(BF)
                grad_second = _tn(act.astype(BF), miss_b)
                grad_pre = _nt(miss_b, second_b) * sig_k * (1.0 + pre * (1.0 - sig_k))
                grad_first = _tn(kn, grad_pre.astype(BF))
                eta = means[:, 3 * head + 1 : 3 * head + 2]
                keep = 1.0 - 0.5 * means[:, 3 * head + 2 : 3 * head + 3]
                s1 = eta * s1 - grad_first
                s2 = eta * s2 - grad_second
                carry[head] = [keep * first + s1, keep * second + s2, s1, s2]
    masks = _masks()
    for block in range(4):
        rows = slice(block * 128, (block + 1) * 128)
        target = pl.ds(_spot(place, block), 128)
        lse_all = jnp.zeros((128, 128), F32)
        for head in range(heads):
            at = slice(head * 128, (head + 1) * 128)
            qs = qs_s[rows, at]
            near = [
                (back, slice((block - back) * 128, (block - back + 1) * 128))
                for back in (2, 1, 0)
                if block - back >= 0
            ]
            read_b = reads_ref[rows, at]
            parts = _scores(
                qs, [(b, kb_s[r, at]) for b, r in near], read_b, pk_ref[head], block, length, masks
            )
            top = jnp.max(parts[0], axis=1, keepdims=True)
            wide = parts[1]
            for part in parts[2:]:
                wide = jnp.maximum(wide, part)
            top = jnp.maximum(top, jnp.max(wide, axis=1, keepdims=True))
            exps = [jnp.exp(part - top) for part in parts]
            wide = exps[1]
            for part in exps[2:]:
                wide = wide + part
            total = jnp.sum(exps[0], axis=1, keepdims=True) + jnp.sum(wide, axis=1, keepdims=True)
            acc = _nn(exps[0].astype(BF), pv_ref[head]) + _nn(exps[1].astype(BF), read_b)
            for (_, r), part in zip(near, exps[2:]):
                acc = acc + _nn(part.astype(BF), vb_s[r, at])
            mixed_ref[target, at] = (acc / total).astype(BF)
            lse_all = jnp.where(
                _lane((128, 128), 1) == head, jnp.broadcast_to(top + jnp.log(total), (128, 128)), lse_all
            )
        lse_ref[rows, :] = lse_all


def _bwd_kernel(heads, blocks, where_ref, *rest):
    cots = rest[:4]
    saved = rest[4:11]
    weight_refs = rest[11 : 11 + blocks]
    rest = rest[11 + blocks :]
    dqkv_ref, dpk_ref, dpv_ref, dm1_ref, dm2_ref, keep_ref, send_ref = rest[:7]
    dmix_s, project_s, rates_s, out_s, sems = rest[7:12]
    scratch = rest[12:]
    step = weight_refs[0].shape[0] - 16
    wide = heads * 128
    every = pl.ds(0, step)
    out_copies = _copies(weight_refs, every, pl.ds(3 * wide, wide), out_s, sems.at[1])
    project_copies = _copies(weight_refs, every, pl.ds(0, 3 * wide), project_s, sems.at[0])
    rates_s[16:128, :] = jnp.zeros((112, rates_s.shape[1]), BF)
    for k, block in enumerate(weight_refs):
        copy = pltpu.make_async_copy(
            block.at[pl.ds(step, 16), pl.ds(0, step)],
            rates_s.at[pl.ds(0, 16), pl.ds(k * step, step)],
            sems.at[2, k],
        )
        copy.start()
        project_copies.append(copy)
    for copy in out_copies:
        copy.wait()
    for quarter, ref in enumerate(cots):
        dmix_s[quarter * 128 : (quarter + 1) * 128, :] = _nn(ref[...], out_s[...])
    _mix_backward(
        heads,
        where_ref,
        *saved,
        dmix_s,
        dqkv_ref,
        dpk_ref,
        dpv_ref,
        dm1_ref,
        dm2_ref,
        *scratch,
    )
    for copy in project_copies:
        copy.wait()
    for quarter in (2, 3, 0, 1):
        rows = slice(quarter * 128, (quarter + 1) * 128)
        grad = _nt(dqkv_ref[rows, : 3 * wide], project_s[...])
        grad = grad + _nn(dqkv_ref[rows, 3 * wide :], rates_s[...])
        if quarter >= 2:
            send_ref[(quarter - 2) * 128 : (quarter - 1) * 128, :] = grad.astype(BF)
        else:
            keep_ref[rows, :] = grad


def _mix_backward(
    heads,
    where_ref,
    qkv_ref,
    pk_ref,
    pv_ref,
    mixed_ref,
    reads_ref,
    lse_ref,
    states_ref,
    dmix_ref,
    dqkv_ref,
    dpk_ref,
    dpv_ref,
    dm1_ref,
    dm2_ref,
    qn_s,
    kn_s,
    qs_s,
    kb_s,
    v_s,
    vb_s,
    w_s,
    r_s,
    dq_s,
    dk_s,
    dv_s,
    dr_s,
    dqn_s,
    dkn_s,
    dz_s,
):
    place = where_ref[0]
    length = where_ref[1]
    width = heads * 128
    _load_rows(place, length, qkv_ref, heads, qn_s, kn_s, qs_s, kb_s, v_s, vb_s, w_s, r_s)
    masks = _masks()
    scale = 128 ** (-0.5)
    for head in range(heads):
        at = slice(head * 128, (head + 1) * 128)
        dpk = jnp.zeros((16, 128), F32)
        dpv = jnp.zeros((16, 128), F32)
        dk = [jnp.zeros((128, 128), F32)] * 4
        dv = [jnp.zeros((128, 128), F32)] * 4
        for block in range(4):
            rows = slice(block * 128, (block + 1) * 128)
            source = pl.ds(_spot(place, block), 128)
            qs = qs_s[rows, at]
            near = [
                (back, slice((block - back) * 128, (block - back + 1) * 128))
                for back in (2, 1, 0)
                if block - back >= 0
            ]
            read_b = reads_ref[rows, at]
            parts = _scores(
                qs, [(b, kb_s[r, at]) for b, r in near], read_b, pk_ref[head], block, length, masks
            )
            lse = lse_ref[rows, head : head + 1]
            probs = [jnp.exp(part - lse) for part in parts]
            dout = dmix_ref[source, at]
            dout_b = dout.astype(BF)
            dot = jnp.sum(dout * mixed_ref[source, at].astype(F32), axis=1, keepdims=True)
            values = [pv_ref[head], read_b] + [vb_s[r, at] for _, r in near]
            keys = [pk_ref[head], read_b] + [kb_s[r, at] for _, r in near]
            ds_b = [
                (p * (_nt(dout_b, val) - dot)).astype(BF) for p, val in zip(probs, values)
            ]
            probs_b = [p.astype(BF) for p in probs]
            dq = _nn(ds_b[0], keys[0])
            for d, key in zip(ds_b[1:], keys[1:]):
                dq = dq + _nn(d, key)
            dq_s[rows, at] = dq * scale
            dpk = dpk + _tn(ds_b[0], qs)
            dpv = dpv + _tn(probs_b[0], dout_b)
            dr_s[rows, at] = _tn(ds_b[1], qs) + _tn(probs_b[1], dout_b)
            for (back, _), d, p in zip(near, ds_b[2:], probs_b[2:]):
                dk[block - back] = dk[block - back] + _tn(d, qs)
                dv[block - back] = dv[block - back] + _tn(p, dout_b)
            if block >= 2:
                dk_s[(block - 2) * 128 : (block - 1) * 128, at] = dk[block - 2]
                dv_s[(block - 2) * 128 : (block - 1) * 128, at] = dv[block - 2]
        for block in (2, 3):
            rows = slice(block * 128, (block + 1) * 128)
            dk_s[rows, at] = dk[block]
            dv_s[rows, at] = dv[block]
        dpk_ref[head] = dpk
        dpv_ref[head] = dpv
    zero = jnp.zeros((128, 128), F32)
    carry = [[zero, zero, zero, zero] for _ in range(heads)]
    lanes = _lane((CH, 128), 1)
    for span in range(7, -1, -1):
        rows = slice(span * CH, (span + 1) * CH)
        means = jnp.mean(r_s[rows, :], axis=0, keepdims=True)
        dr_row = jnp.zeros((CH, 128), F32)
        live = (span * CH + _lane((CH, 1), 0) < length).astype(F32)
        for head in range(heads):
            at = slice(head * 128, (head + 1) * 128)
            a1, a2, b1, b2 = carry[head]
            first_b = states_ref[span, 0, head]
            second_b = states_ref[span, 1, head]
            kn = kn_s[rows, at]
            qn = qn_s[rows, at]
            dread_b = dr_s[rows, at].astype(BF)
            both = _nn(jnp.concatenate([kn, qn], axis=0), first_b)
            sig_both = _sig(both)
            act_both = both * sig_both
            slope_both = sig_both * (1.0 + both * (1.0 - sig_both))
            act_b = act_both.astype(BF)
            db_b = (_nt(dread_b, second_b) * slope_both[CH:]).astype(BF)
            if span == 7:
                dqn_s[rows, at] = _nt(db_b, first_b)
                dkn_s[rows, at] = jnp.zeros((CH, 128), F32)
                carry[head] = [_tn(qn, db_b), _tn(act_b[CH:], dread_b), zero, zero]
                continue
            eta = means[:, 3 * head + 1 : 3 * head + 2]
            keep = 1.0 - 0.5 * means[:, 3 * head + 2 : 3 * head + 3]
            pre, sig, slope = both[:CH], sig_both[:CH], slope_both[:CH]
            bend = sig * (1.0 - sig) * (2.0 + pre * (1.0 - 2.0 * sig))
            u_b = act_b[:CH]
            w = w_s[rows, at]
            e = _nn(u_b, second_b) - v_s[rows, at]
            m_b = (e * w).astype(BF)
            p = _nt(m_b, second_b)
            g_b = (p * slope).astype(BF)
            ds1 = b1 + a1
            ds2 = b2 + a2
            dg1_b = (-ds1).astype(BF)
            dg2_b = (-ds2).astype(BF)
            x1 = _nn(kn, dg1_b)
            dp_b = (x1 * slope).astype(BF)
            dm = _nn(dp_b, second_b) + _nn(u_b, dg2_b)
            de = dm * w
            de_b = de.astype(BF)
            du = _nt(m_b, dg2_b) + _nt(de_b, second_b)
            da = x1 * p * bend + du * slope
            da_b = da.astype(BF)
            back = _nt(jnp.concatenate([da_b, db_b], axis=0), first_b)
            dkn_s[rows, at] = _nt(g_b, dg1_b) + back[:CH]
            dqn_s[rows, at] = back[CH:]
            dv_s[rows, at] = dv_s[rows, at] - de
            new1 = keep * a1 + _tn(
                jnp.concatenate([kn, qn], axis=0), jnp.concatenate([da_b, db_b], axis=0)
            )
            new2 = (
                keep * a2
                + _tn(act_b, jnp.concatenate([de_b, dread_b], axis=0))
                + _tn(dp_b, m_b)
            )
            prev1 = states_ref[span, 2, head].astype(F32)
            prev2 = states_ref[span, 3, head].astype(F32)
            deta = jnp.sum(
                jnp.sum(ds1 * prev1 + ds2 * prev2, axis=0, keepdims=True), axis=1, keepdims=True
            )
            dkeep = jnp.sum(
                jnp.sum(a1 * first_b.astype(F32) + a2 * second_b.astype(F32), axis=0, keepdims=True),
                axis=1,
                keepdims=True,
            )
            dw = jnp.sum(dm * e, axis=1, keepdims=True) * live * (2.0 / (CH * 128))
            dr_row = jnp.where(lanes == 3 * head, jnp.broadcast_to(dw, (CH, 128)), dr_row)
            dr_row = jnp.where(
                lanes == 3 * head + 1, jnp.broadcast_to(deta * (1.0 / CH), (CH, 128)), dr_row
            )
            dr_row = jnp.where(
                lanes == 3 * head + 2, jnp.broadcast_to(dkeep * (-0.5 / CH), (CH, 128)), dr_row
            )
            carry[head] = [new1, new2, eta * ds1, eta * ds2]
        rates = r_s[rows, :]
        dz_s[rows, :] = dr_row * rates * (1.0 - rates)
    for head in range(heads):
        dm1_ref[head] = carry[head][0]
        dm2_ref[head] = carry[head][1]
    for quarter in range(4):
        source = pl.ds(_spot(place, quarter), 128)
        here = slice(quarter * 128, (quarter + 1) * 128)
        dqkv_ref[source, 3 * width :] = dz_s[here, :].astype(BF)
        for head in range(heads):
            at = slice(head * 128, (head + 1) * 128)
            for part, grad_s, norm_s in ((0, dq_s, dqn_s), (1, dk_s, dkn_s)):
                col = slice(part * width + head * 128, part * width + (head + 1) * 128)
                raw = qkv_ref[source, col]
                inverse = _scale_of(raw)
                normed = raw * inverse
                dn = norm_s[here, at]
                inner = jnp.mean(dn * normed, axis=-1, keepdims=True)
                dqkv_ref[source, col] = (
                    grad_s[here, at] + inverse * (dn - normed * inner)
                ).astype(BF)
            col = slice(2 * width + head * 128, 2 * width + (head + 1) * 128)
            dqkv_ref[source, col] = dv_s[here, at].astype(BF)


def _row_scratch(heads):
    wide = heads * 128
    return [
        pltpu.VMEM((512, wide), BF),
        pltpu.VMEM((512, wide), BF),
        pltpu.VMEM((512, wide), BF),
        pltpu.VMEM((512, wide), BF),
        pltpu.VMEM((512, wide), F32),
        pltpu.VMEM((512, wide), BF),
        pltpu.VMEM((512, wide), F32),
        pltpu.VMEM((512, 128), F32),
    ]


_VM = pl.BlockSpec(memory_space=pltpu.VMEM)
_SM = pl.BlockSpec(memory_space=pltpu.SMEM)


def _any(count):
    return [pl.BlockSpec(memory_space=pl.ANY)] * count


def mix_forward(where, quarters, batch, weights, pk, pv, m1, m2):
    heads = pk.shape[0]
    wide = heads * 128
    blocks = len(weights)
    step = weights[0].shape[0] - 16
    width = blocks * step
    return pl.pallas_call(
        partial(_fwd_kernel, heads, blocks, batch),
        out_shape=(
            jax.ShapeDtypeStruct((512, width), BF),
            jax.ShapeDtypeStruct((16, width), F32),
            jax.ShapeDtypeStruct((128, width), F32),
            jax.ShapeDtypeStruct((512, 3 * wide + 128), F32),
            jax.ShapeDtypeStruct((512, wide), BF),
            jax.ShapeDtypeStruct((512, wide), BF),
            jax.ShapeDtypeStruct((512, 128), F32),
            jax.ShapeDtypeStruct((8, 4, heads, 128, 128), BF),
            jax.ShapeDtypeStruct((256, width), F32),
            jax.ShapeDtypeStruct((256, width), BF),
        ),
        in_specs=[_SM] + [_VM] * 8 + _any(blocks),
        out_specs=(_VM,) * 10,
        scratch_shapes=[
            pltpu.VMEM((width, 3 * wide), BF),
            pltpu.VMEM((128, width), BF),
            pltpu.VMEM((width, wide), BF),
            pltpu.SemaphoreType.DMA((3, blocks)),
        ]
        + _row_scratch(heads),
        compiler_params=pltpu.CompilerParams(vmem_limit_bytes=48 * 1024 * 1024),
        cost_estimate=pl.CostEstimate(flops=14 * 10**9, bytes_accessed=10**7, transcendentals=0),
    )(where, *quarters, pk, pv, m1, m2, *weights)


def mix_backward(where, cots, saved, weights):
    pk = saved[1]
    heads = pk.shape[0]
    wide = heads * 128
    blocks = len(weights)
    step = weights[0].shape[0] - 16
    width = blocks * step
    return pl.pallas_call(
        partial(_bwd_kernel, heads, blocks),
        out_shape=(
            jax.ShapeDtypeStruct((512, 3 * wide + 128), BF),
            jax.ShapeDtypeStruct((heads, 16, 128), F32),
            jax.ShapeDtypeStruct((heads, 16, 128), F32),
            jax.ShapeDtypeStruct((heads, 128, 128), F32),
            jax.ShapeDtypeStruct((heads, 128, 128), F32),
            jax.ShapeDtypeStruct((256, width), F32),
            jax.ShapeDtypeStruct((256, width), BF),
        ),
        in_specs=[_SM] + [_VM] * 11 + _any(blocks),
        out_specs=(_VM,) * 7,
        scratch_shapes=[
            pltpu.VMEM((512, wide), F32),
            pltpu.VMEM((width, 3 * wide), BF),
            pltpu.VMEM((128, width), BF),
            pltpu.VMEM((width, wide), BF),
            pltpu.SemaphoreType.DMA((3, blocks)),
        ]
        + _row_scratch(heads)
        + [pltpu.VMEM((512, wide), F32)] * 6
        + [pltpu.VMEM((512, 128), F32)],
        compiler_params=pltpu.CompilerParams(vmem_limit_bytes=48 * 1024 * 1024),
        cost_estimate=pl.CostEstimate(flops=18 * 10**9, bytes_accessed=10**7, transcendentals=0),
    )(where, *cots, *saved, *weights)


def _feed_kernel(blocks, cols, batch, *rest):
    seconds = rest[:4]
    near_ref, far_ref = rest[4:6]
    weight_refs = rest[6 : 6 + blocks]
    (
        hidden_ref,
        gate_ref,
        up_ref,
        keep_ref,
        send_ref,
        feed_keep_ref,
        feed_send_ref,
        gate_s,
        up_s,
        down_s,
        sems,
    ) = rest[6 + blocks :]
    step = weight_refs[0].shape[0]
    copies = [
        _copies(weight_refs, pl.ds(0, step), pl.ds(w * cols, cols), target, sems.at[w])
        for w, target in enumerate((gate_s, up_s, down_s))
    ]
    for part in range(2):
        rows = slice(part * 256, (part + 1) * 256)
        left = jnp.concatenate([seconds[2 * part][...], seconds[2 * part + 1][...]], axis=0)
        cot = (near_ref, far_ref)[part][batch]
        if part == 0:
            for copy in copies[0]:
                copy.wait()
        gate = _nn(left, gate_s[...])
        if part == 0:
            for copy in copies[1]:
                copy.wait()
        up = _nn(left, up_s[...])
        if part == 0:
            for copy in copies[2]:
                copy.wait()
        grad = _nn(cot, down_s[...])
        sig = _sig(gate)
        act = gate * sig
        hidden = (act * up).astype(BF)
        gate_grad = (grad * up * (sig + act * (1.0 - sig))).astype(BF)
        up_grad = (grad * act).astype(BF)
        hidden_ref[rows, :] = hidden
        gate_ref[rows, :] = gate_grad
        up_ref[rows, :] = up_grad
        back = _nt(gate_grad, gate_s[...]) + _nt(up_grad, up_s[...])
        feed = _nt(hidden, down_s[...])
        if part == 0:
            keep_ref[...] = back
            feed_keep_ref[...] = feed
        else:
            send_ref[...] = back.astype(BF)
            feed_send_ref[...] = feed.astype(BF)


def feed_forward(seconds, near, far, batch, weights):
    blocks = len(weights)
    step = weights[0].shape[0]
    cols = weights[0].shape[1] // 3
    width = blocks * step
    return pl.pallas_call(
        partial(_feed_kernel, blocks, cols, batch),
        out_shape=(
            jax.ShapeDtypeStruct((512, cols), BF),
            jax.ShapeDtypeStruct((512, cols), BF),
            jax.ShapeDtypeStruct((512, cols), BF),
            jax.ShapeDtypeStruct((256, width), F32),
            jax.ShapeDtypeStruct((256, width), BF),
            jax.ShapeDtypeStruct((256, width), F32),
            jax.ShapeDtypeStruct((256, width), BF),
        ),
        in_specs=[_VM] * 6 + _any(blocks),
        out_specs=(_VM,) * 7,
        scratch_shapes=[pltpu.VMEM((width, cols), BF)] * 3
        + [pltpu.SemaphoreType.DMA((3, blocks))],
        compiler_params=pltpu.CompilerParams(vmem_limit_bytes=48 * 1024 * 1024),
        cost_estimate=pl.CostEstimate(flops=10 * 10**9, bytes_accessed=10**7, transcendentals=0),
    )(*seconds, near, far, *weights)


def _grad_kernel(counts, picks, *rest):
    total = sum(counts)
    row_refs = rest[:total]
    grad_refs = rest[total : total + len(counts)]
    keep_ref, early_ref, late_ref = rest[total + len(counts) :]
    blocks = keep_ref.shape[0]
    step = keep_ref.shape[1]
    for k in [blocks + i for i in range(blocks)] + list(range(blocks)):
        at = slice(k * step, (k + 1) * step)
        value = None
        index = 0
        for count, grad_ref in zip(counts, grad_refs):
            pieces = []
            for i in range(index, index + count):
                ref, pick = row_refs[i], picks[i]
                pieces.append(ref[:, at] if pick is None else ref[pick, :, at])
            left = pieces[0] if count == 1 else jnp.concatenate(pieces, axis=0)
            index += count
            term = _tn(left, grad_ref[...])
            value = term if value is None else value + term
        if k < blocks:
            keep_ref[k] = value
        elif k < blocks + blocks // 2:
            early_ref[k - blocks] = value.astype(BF)
        else:
            late_ref[k - blocks - blocks // 2] = value.astype(BF)


def weight_gradient(rows, grads, blocks, flops):
    width = rows[0][0][0].shape[-1]
    cols = grads[0].shape[1]
    step = width // blocks
    half = blocks // 2
    return pl.pallas_call(
        partial(_grad_kernel, tuple(len(r) for r in rows), tuple(p[1] for r in rows for p in r)),
        out_shape=(
            jax.ShapeDtypeStruct((half, step, cols), F32),
            jax.ShapeDtypeStruct((half // 2, step, cols), BF),
            jax.ShapeDtypeStruct((half // 2, step, cols), BF),
        ),
        in_specs=[_VM] * (sum(len(r) for r in rows) + len(grads)),
        out_specs=(_VM,) * 3,
        compiler_params=pltpu.CompilerParams(vmem_limit_bytes=48 * 1024 * 1024),
        cost_estimate=pl.CostEstimate(flops=flops, bytes_accessed=10**7, transcendentals=0),
    )(*[piece[0] for r in rows for piece in r], *grads)


DP = ("z", "x")


def _swap(value, axis):
    return lax.ppermute(value, axis, [(0, 1), (1, 0)])


BLOCKS = 8
STEP = 128
DOWN = (1, 2, 3, 0)
RING = [(0, 1), (1, 2), (2, 3), (3, 0)]


def _ring_sized():
    return lax.axis_size("z") == 4


def _block_ids():
    if not _ring_sized():
        return jnp.arange(BLOCKS, dtype=jnp.int32)
    z = lax.axis_index("z")
    x = lax.axis_index("x")
    zs = jnp.stack([(z + 4 - i) % 4 for i in DOWN])
    return jnp.concatenate([2 * zs + x, 2 * zs + (1 - x)]).astype(jnp.int32)


def _after(value, *others):
    return lax.optimization_barrier((value, *others))[0]


def _gather_blocks(own):
    ring = [own]
    for _ in range(3):
        ring.append(lax.ppermute(ring[-1], "z", RING))
    across = [_swap(block, "x") for block in ring]
    return [ring[i] for i in DOWN] + [across[i] for i in DOWN]


def _scatter_blocks(keep, early, late):
    early = _swap(early, "x")
    late = _swap(late, "x")
    total = keep[0] + early[0].astype(F32)
    for place in (1, 2, 3):
        passed = lax.ppermute(total.astype(BF), "z", RING)
        other = (early[1], late[0], late[1])[place - 1]
        total = keep[place] + other.astype(F32) + passed.astype(F32)
    return total


def _scatter_whole(keep, early, late):
    whole = jnp.concatenate([keep.astype(BF), early, late]).reshape(BLOCKS * STEP, -1)
    return lax.psum_scatter(whole, DP, scatter_dimension=0, tiled=True).astype(F32)


def _sum_all(value, axes):
    for axis in axes:
        size = lax.axis_size(axis)
        step = 1
        while step < size:
            value = value + lax.ppermute(value, axis, [(i, i ^ step) for i in range(size)])
            step *= 2
    return value


def _add_core(keep, send):
    half = keep.shape[0] // 2
    got = _swap(send, "c").astype(F32)
    return keep[:half] + got[:half], (keep[half:] + got[half:]).astype(BF)


def _scatter_slots(keep, send):
    own, other = _add_core(keep, send)
    return own + _swap(other, "y").astype(F32)


def _quarters(own):
    column = _swap(own, "y")
    return [own, column, _swap(own, "c"), _swap(column, "c")]


def _dot(a, b, out=F32):
    return lax.dot_general(a, b, (((1,), (0,)), ((), ())), preferred_element_type=out)


def _dot_t(a, b, out=F32):
    return lax.dot_general(a, b, (((1,), (1,)), ((), ())), preferred_element_type=out)


def per_device(
    tokens,
    grad_output,
    query_weight,
    key_weight,
    value_weight,
    rates_weight,
    out_weight,
    gate_weight,
    up_weight,
    down_weight,
    norm1_gain,
    norm2_gain,
    persist_key,
    persist_value,
    memory_first,
    memory_second,
    seq_lengths,
    deal,
):
    devices = lax.axis_size("z") * lax.axis_size("x")
    dp_index = lax.axis_index("z") * lax.axis_size("x") + lax.axis_index("x")
    place = lax.axis_index("y") * 2 + lax.axis_index("c")
    seq_count = seq_lengths.shape[0]
    batches = seq_count // devices
    local_rows = tokens.shape[2]
    width = tokens.shape[3]
    quarter = local_rows * devices
    rows_of = query_weight.shape[0]
    head_cols = query_weight.shape[1]
    rate_cols = rates_weight.shape[1]
    hidden_cols = gate_weight.shape[1]

    batch_of = deal // devices
    batch_ids = jnp.arange(batches, dtype=jnp.int32)
    batch_tokens = jnp.sum(
        jnp.where(batch_of[None, :] == batch_ids[:, None], seq_lengths[None, :], 0), axis=1
    ).astype(F32)
    batch_scale = jnp.sum(seq_lengths).astype(F32) / (batches * batch_tokens)
    span = range(batches)
    my_seqs = [batches * dp_index + b for b in span]
    lengths = [seq_lengths[s] for s in my_seqs]
    scales = [batch_scale[batch_of[s]] for s in my_seqs]
    positions = place * quarter + jnp.arange(quarter, dtype=jnp.int32)
    lives = [(positions < n).astype(F32)[:, None] for n in lengths]

    ring_sized = _ring_sized()
    ids = _block_ids()
    order = (ids[:, None] * STEP + jnp.arange(STEP, dtype=jnp.int32)[None, :]).reshape(width)
    shuffle = (jnp.arange(width, dtype=jnp.int32)[:, None] == order[None, :]).astype(BF)

    def deal_in(array):
        part = array.reshape(devices, batches, local_rows, width)
        part = lax.all_to_all(part, DP, split_axis=0, concat_axis=0, tiled=True)
        if local_rows * BLOCKS == quarter:
            return part
        part = part.transpose(1, 0, 2, 3).reshape(batches, BLOCKS, quarter // BLOCKS, width)
        return part.transpose(1, 0, 2, 3)

    def deal_out(rows):
        plain = _dot_t(jnp.concatenate(rows).astype(BF), shuffle, BF)
        part = plain.reshape(batches, devices, local_rows, width).transpose(1, 0, 2, 3)
        part = lax.all_to_all(part, DP, split_axis=0, concat_axis=0, tiled=True)
        return part.reshape(seq_count, 1, local_rows, width)

    def scatter(keep, early, late):
        return (_scatter_blocks if ring_sized else _scatter_whole)(keep, early, late)

    mix_shard = jnp.concatenate([query_weight, key_weight, value_weight, out_weight], axis=1)
    extra = jnp.concatenate(
        [
            rates_weight.T,
            norm1_gain[None],
            norm2_gain[None],
            jnp.zeros((16 - rate_cols - 2, rows_of), BF),
        ]
    )
    pad = -hidden_cols % 128
    feed_shard = jnp.concatenate(
        [jnp.pad(w, ((0, 0), (0, pad))) for w in (gate_weight, up_weight, down_weight)], axis=1
    )
    got_tokens = deal_in(tokens)
    if ring_sized:
        extra = jnp.pad(extra, ((0, 0), (0, mix_shard.shape[1] - rows_of)))
        mix_weights = _gather_blocks(jnp.concatenate([mix_shard, extra], axis=0))
        feed_weights = _gather_blocks(_after(feed_shard, mix_weights[0]))
    else:
        mix_full = lax.all_gather(mix_shard, DP, axis=0, tiled=True)
        extra = lax.all_gather(extra, DP, axis=1, tiled=True)
        extra = jnp.pad(
            extra.reshape(16, BLOCKS, STEP), ((0, 0), (0, 0), (0, mix_shard.shape[1] - STEP))
        )
        mix_weights = [
            jnp.concatenate([mix_full[k * STEP : (k + 1) * STEP], extra[:, k]])
            for k in range(BLOCKS)
        ]
        feed_full = lax.all_gather(feed_shard, DP, axis=0, tiled=True)
        feed_weights = [feed_full[k * STEP : (k + 1) * STEP] for k in range(BLOCKS)]

    quarters = _quarters(got_tokens)
    where = [
        jnp.concatenate([jnp.stack([place, lengths[b]]).astype(jnp.int32), ids]) for b in span
    ]
    got_cots = deal_in(_after(grad_output, mix_weights[2]))

    mixes = [
        mix_forward(
            where[b],
            quarters,
            b,
            mix_weights,
            persist_key,
            persist_value,
            memory_first,
            memory_second,
        )
        for b in span
    ]
    gain_one = mixes[0][1][rate_cols]
    gain_two = mixes[0][1][rate_cols + 1]
    token_rows = [m[2] for m in mixes]
    attended = [_scatter_slots(m[8], m[9]) for m in mixes]
    residual = [token_rows[b] + attended[b] for b in span]
    inverse_two = [lax.rsqrt(jnp.mean(r * r, axis=-1, keepdims=True) + EPS) for r in residual]
    normed_two = [r * i for r, i in zip(residual, inverse_two)]
    second = [_quarters((n * gain_two).astype(BF)) for n in normed_two]

    cot_rows = _dot(got_cots.reshape(batches * quarter, width), shuffle)
    cot_rows = cot_rows.reshape(BLOCKS, batches, quarter // BLOCKS, width).transpose(1, 0, 2, 3)
    cot_rows = [cot_rows[b].reshape(quarter, width) * scales[b] * lives[b] for b in span]
    cot_own = jnp.stack([c.astype(BF) for c in cot_rows])
    near = jnp.concatenate([cot_own, _swap(cot_own, "y")], axis=1)
    far = _swap(near, "c")

    feeds = [feed_forward(second[b], near, far, b, feed_weights) for b in span]
    two_grad = [_scatter_slots(f[3], f[4]) for f in feeds]
    scaled_two = [g * gain_two for g in two_grad]
    residual_grad = [
        cot_rows[b]
        + inverse_two[b]
        * (
            scaled_two[b]
            - normed_two[b] * jnp.mean(scaled_two[b] * normed_two[b], axis=-1, keepdims=True)
        )
        for b in span
    ]
    mixer_cot = [_quarters(r.astype(BF)) for r in residual_grad]
    def plain(pieces):
        return [[(piece, None) for piece in some] for some in pieces]

    down_parts = weight_gradient(
        [[(near, b), (far, b)] for b in span], [f[0] for f in feeds], BLOCKS, 3 * 10**9
    )
    gate_parts = weight_gradient(plain(second), [f[1] for f in feeds], BLOCKS, 3 * 10**9)
    up_parts = weight_gradient(plain(second), [f[2] for f in feeds], BLOCKS, 3 * 10**9)
    down_total = scatter(*down_parts)[:, :hidden_cols]
    gate_total = scatter(*gate_parts)[:, :hidden_cols]
    up_total = scatter(*up_parts)[:, :hidden_cols]

    saved = [(m[3], persist_key, persist_value, *m[4:8]) for m in mixes]
    backs = [mix_backward(where[b], mixer_cot[b], saved[b], mix_weights) for b in span]

    feed = [_scatter_slots(f[5], f[6]) for f in feeds]
    layer_out = deal_out([lives[b] * (residual[b] + feed[b]) for b in span])
    out_total = scatter(
        *weight_gradient(plain(mixer_cot), [m[4] for m in mixes], BLOCKS, 10**9)
    )

    one_grad = [_scatter_slots(k[5], k[6]) for k in backs]
    inverse_one = [lax.rsqrt(jnp.mean(t * t, axis=-1, keepdims=True) + EPS) for t in token_rows]
    normed_one = [t * i for t, i in zip(token_rows, inverse_one)]
    scaled_one = [g * gain_one for g in one_grad]
    grad_tokens = deal_out(
        [
            residual_grad[b]
            + inverse_one[b]
            * (
                scaled_one[b]
                - normed_one[b] * jnp.mean(scaled_one[b] * normed_one[b], axis=-1, keepdims=True)
            )
            for b in span
        ]
    )

    first = plain([[m[0]] for m in mixes])
    project_total = scatter(*weight_gradient(first, [k[0] for k in backs], BLOCKS, 3 * 10**9))

    memory = [sum(k[i] for k in backs) for i in (1, 2, 3, 4)]
    flat = jnp.concatenate([m.reshape(-1, 128) for m in memory])
    flat = _sum_all(flat, ("x", "z"))
    memory_out = []
    start = 0
    for m in memory:
        size = m.size // 128
        memory_out.append(flat[start : start + size].reshape(m.shape))
        start += size

    gains = jnp.stack(
        [
            sum(jnp.sum(one_grad[b] * normed_one[b], axis=0) for b in span),
            sum(jnp.sum(two_grad[b] * normed_two[b], axis=0) for b in span),
        ]
    ).reshape(2, BLOCKS, STEP)
    place_of = (ids[:, None] == jnp.arange(BLOCKS, dtype=jnp.int32)[None, :]).astype(F32)
    gains = jnp.sum(gains[:, :, None, :] * place_of[None, :, :, None], axis=1)
    gains = _sum_all(gains.reshape(2 * BLOCKS, STEP), ("c", "y", "x", "z")).reshape(2, width)

    return (
        layer_out,
        grad_tokens,
        project_total[:, :head_cols],
        project_total[:, head_cols : 2 * head_cols],
        project_total[:, 2 * head_cols : 3 * head_cols],
        project_total[:, 3 * head_cols : 3 * head_cols + rate_cols],
        out_total,
        gate_total,
        up_total,
        down_total,
        gains[0],
        gains[1],
        memory_out[0],
        memory_out[1],
        memory_out[2],
        memory_out[3],
    )


def solution(mesh):
    sizes = mesh.devices.shape
    fine = Mesh(mesh.devices.reshape(sizes[0] // 2, 2, 2, sizes[1] // 2), ("z", "x", "y", "c"))
    tensor = ("y", "c")
    return jax.shard_map(
        per_device,
        mesh=fine,
        in_specs=(
            P(None, tensor, DP, None),
            P(None, tensor, DP, None),
            P(DP, tensor),
            P(DP, tensor),
            P(DP, tensor),
            P(DP, tensor),
            P(DP, tensor),
            P(DP, tensor),
            P(DP, tensor),
            P(DP, tensor),
            P(DP),
            P(DP),
            P(tensor, None, None),
            P(tensor, None, None),
            P(tensor, None, None),
            P(tensor, None, None),
            P(),
            P(),
        ),
        out_specs=(
            P(None, tensor, DP, None),
            P(None, tensor, DP, None),
            P(DP, tensor),
            P(DP, tensor),
            P(DP, tensor),
            P(DP, tensor),
            P(DP, tensor),
            P(DP, tensor),
            P(DP, tensor),
            P(DP, tensor),
            P(),
            P(),
            P(tensor, None, None),
            P(tensor, None, None),
            P(tensor, None, None),
            P(tensor, None, None),
        ),
        check_vma=False,
    )
```

```python
from functools import partial

import jax
import jax.numpy as jnp
from jax import lax
from jax.experimental import pallas as pl
from jax.experimental.pallas import tpu as pltpu
from jax.sharding import Mesh
from jax.sharding import PartitionSpec as P

CH = 64
WINDOW = 256
EPS = 1e-06
NEG = -1e30
BF = jnp.bfloat16
F32 = jnp.float32


def _nn(a, b):
    return lax.dot_general(a, b, (((1,), (0,)), ((), ())), preferred_element_type=F32)


def _nt(a, b):
    return lax.dot_general(a, b, (((1,), (1,)), ((), ())), preferred_element_type=F32)


def _tn(a, b):
    return lax.dot_general(a, b, (((0,), (0,)), ((), ())), preferred_element_type=F32)


def _sig(v):
    return 1.0 / (1.0 + jnp.exp(-v))


def _scale_of(v):
    return lax.rsqrt(jnp.mean(v * v, axis=-1, keepdims=True) + EPS)


def _lane(shape, dim):
    return lax.broadcasted_iota(jnp.int32, shape, dim)


def _masks():
    rows = _lane((128, 128), 0)
    cols = _lane((128, 128), 1)
    return cols > rows, cols <= rows, (rows // CH) == (cols // CH)


def _scores(qs, near_keys, read_b, pkey, block, length, masks):
    older, newer, same_span = masks
    read_ok = same_span & (block * 128 + _lane((128, 128), 1) < length)
    parts = [_nt(qs, pkey), jnp.where(read_ok, _nt(qs, read_b), NEG)]
    for back, keys in near_keys:
        part = _nt(qs, keys)
        if back == 2:
            part = jnp.where(older, part, NEG)
        elif back == 0:
            part = jnp.where(newer, part, NEG)
        parts.append(part)
    return parts


def _spot(place, quarter):
    there = place ^ quarter
    return pl.multiple_of((((there & 1) << 1) | (there >> 1)) * 128, 128)


def _load_rows(place, length, qkv_ref, heads, qn_s, kn_s, qs_s, kb_s, v_s, vb_s, w_s, r_s):
    width = heads * 128
    for quarter in range(4):
        source = pl.ds(_spot(place, quarter), 128)
        here = pl.ds(quarter * 128, 128)
        live = (quarter * 128 + _lane((128, 1), 0) < length).astype(F32)
        rates = _sig(qkv_ref[source, 3 * width : 3 * width + 128])
        r_s[here, :] = rates
        for head in range(heads):
            at = slice(head * 128, (head + 1) * 128)
            q = qkv_ref[source, head * 128 : (head + 1) * 128]
            k = qkv_ref[source, width + head * 128 : width + (head + 1) * 128]
            v = qkv_ref[source, 2 * width + head * 128 : 2 * width + (head + 1) * 128]
            qn_s[here, at] = (q * _scale_of(q)).astype(BF)
            kn_s[here, at] = (k * _scale_of(k)).astype(BF)
            qs_s[here, at] = (q * (128 ** (-0.5))).astype(BF)
            kb_s[here, at] = k.astype(BF)
            v_s[here, at] = v
            vb_s[here, at] = v.astype(BF)
            weighting = rates[:, 3 * head : 3 * head + 1] * live * (2.0 / (CH * 128))
            w_s[here, at] = jnp.broadcast_to(weighting, (128, 128))


def _copies(blocks, rows, cols, target, sems):
    made = []
    for k, block in enumerate(blocks):
        copy = pltpu.make_async_copy(
            block.at[rows, cols],
            target.at[pl.ds(k * rows.size, rows.size), :],
            sems.at[k],
        )
        copy.start()
        made.append(copy)
    return made


def _fwd_kernel(
    heads,
    blocks,
    batch,
    where_ref,
    own_ref,
    ypart_ref,
    cpart_ref,
    far_ref,
    pk_ref,
    pv_ref,
    m1_ref,
    m2_ref,
    *rest,
):
    weight_refs = rest[:blocks]
    (
        first_ref,
        extra_ref,
        token_ref,
        qkv_ref,
        mixed_ref,
        reads_ref,
        lse_ref,
        states_ref,
        keep_ref,
        send_ref,
        project_s,
        rates_s,
        out_s,
        sems,
    ) = rest[blocks : blocks + 14]
    scratch = rest[blocks + 14 :]
    step = weight_refs[0].shape[0] - 16
    wide = heads * 128
    every = pl.ds(0, step)
    rates_s[16:128, :] = jnp.zeros((112, rates_s.shape[1]), BF)
    extra = []
    for k, block in enumerate(weight_refs):
        copy = pltpu.make_async_copy(
            block.at[pl.ds(step, 16), pl.ds(0, step)],
            rates_s.at[pl.ds(0, 16), pl.ds(k * step, step)],
            sems.at[2, k],
        )
        copy.start()
        extra.append(copy)
    project_copies = _copies(weight_refs, every, pl.ds(0, 3 * wide), project_s, sems.at[0])
    out_copies = _copies(weight_refs, every, pl.ds(3 * wide, wide), out_s, sems.at[1])
    for copy in extra:
        copy.wait()
    extra_rows = rates_s[0:16, :].astype(F32)
    extra_ref[...] = extra_rows
    gain = extra_rows[3 * heads : 3 * heads + 1, :]
    width = blocks * step
    for quarter, ref in enumerate((own_ref, ypart_ref, cpart_ref, far_ref)):
        raw = ref[:, batch].reshape(128, width).astype(F32)
        inverse = _scale_of(raw)
        for k in range(blocks):
            source = pl.ds(pl.multiple_of(where_ref[2 + k] * step, step), step)
            piece = ref[:, batch, :, source].reshape(128, step).astype(F32)
            at = slice(k * step, (k + 1) * step)
            if quarter == 0:
                token_ref[:, at] = piece
            first_ref[quarter * 128 : (quarter + 1) * 128, at] = (
                piece * inverse * gain[:, at]
            ).astype(BF)
    for copy in project_copies:
        copy.wait()
    for quarter in range(4):
        rows = slice(quarter * 128, (quarter + 1) * 128)
        left = first_ref[rows, :]
        qkv_ref[rows, : 3 * wide] = _nn(left, project_s[...])
        qkv_ref[rows, 3 * wide :] = _nt(left, rates_s[...])
    _mix_forward(
        heads,
        where_ref,
        qkv_ref,
        pk_ref,
        pv_ref,
        m1_ref,
        m2_ref,
        mixed_ref,
        reads_ref,
        lse_ref,
        states_ref,
        *scratch,
    )
    for copy in out_copies:
        copy.wait()
    for part in range(2):
        rows = slice(part * 128, (part + 1) * 128)
        send_ref[rows, :] = _nt(mixed_ref[256 + part * 128 : 384 + part * 128, :], out_s[...]).astype(BF)
        keep_ref[rows, :] = _nt(mixed_ref[rows, :], out_s[...])


def _mix_forward(
    heads,
    where_ref,
    qkv_ref,
    pk_ref,
    pv_ref,
    m1_ref,
    m2_ref,
    mixed_ref,
    reads_ref,
    lse_ref,
    states_ref,
    qn_s,
    kn_s,
    qs_s,
    kb_s,
    v_s,
    vb_s,
    w_s,
    r_s,
):
    place = where_ref[0]
    length = where_ref[1]
    _load_rows(place, length, qkv_ref, heads, qn_s, kn_s, qs_s, kb_s, v_s, vb_s, w_s, r_s)
    carry = [
        [m1_ref[h], m2_ref[h], jnp.zeros((128, 128), F32), jnp.zeros((128, 128), F32)]
        for h in range(heads)
    ]
    for span in range(8):
        rows = slice(span * CH, (span + 1) * CH)
        means = jnp.mean(r_s[rows, :], axis=0, keepdims=True)
        for head in range(heads):
            at = slice(head * 128, (head + 1) * 128)
            first, second, s1, s2 = carry[head]
            first_b, second_b = first.astype(BF), second.astype(BF)
            states_ref[span, 0, head] = first_b
            states_ref[span, 1, head] = second_b
            states_ref[span, 2, head] = s1.astype(BF)
            states_ref[span, 3, head] = s2.astype(BF)
            kn = kn_s[rows, at]
            qn = qn_s[rows, at]
            both = _nn(jnp.concatenate([kn, qn], axis=0), first_b)
            both = both * _sig(both) if span == 7 else both
            if span < 7:
                pre = both[:CH]
                sig = _sig(both)
                act_both = both * sig
                sig_k = sig[:CH]
            else:
                act_both = both
            out_both = _nn(act_both.astype(BF), second_b)
            reads_ref[rows, at] = out_both[CH:].astype(BF)
            if span < 7:
                act = act_both[:CH]
                miss = (out_both[:CH] - v_s[rows, at]) * w_s[rows, at]
                miss_b = miss.astype(BF)
                grad_second = _tn(act.astype(BF), miss_b)
                grad_pre = _nt(miss_b, second_b) * sig_k * (1.0 + pre * (1.0 - sig_k))
                grad_first = _tn(kn, grad_pre.astype(BF))
                eta = means[:, 3 * head + 1 : 3 * head + 2]
                keep = 1.0 - 0.5 * means[:, 3 * head + 2 : 3 * head + 3]
                s1 = eta * s1 - grad_first
                s2 = eta * s2 - grad_second
                carry[head] = [keep * first + s1, keep * second + s2, s1, s2]
    masks = _masks()
    for block in range(4):
        rows = slice(block * 128, (block + 1) * 128)
        target = pl.ds(_spot(place, block), 128)
        lse_all = jnp.zeros((128, 128), F32)
        for head in range(heads):
            at = slice(head * 128, (head + 1) * 128)
            qs = qs_s[rows, at]
            near = [
                (back, slice((block - back) * 128, (block - back + 1) * 128))
                for back in (2, 1, 0)
                if block - back >= 0
            ]
            read_b = reads_ref[rows, at]
            parts = _scores(
                qs, [(b, kb_s[r, at]) for b, r in near], read_b, pk_ref[head], block, length, masks
            )
            top = jnp.max(parts[0], axis=1, keepdims=True)
            wide = parts[1]
            for part in parts[2:]:
                wide = jnp.maximum(wide, part)
            top = jnp.maximum(top, jnp.max(wide, axis=1, keepdims=True))
            exps = [jnp.exp(part - top) for part in parts]
            wide = exps[1]
            for part in exps[2:]:
                wide = wide + part
            total = jnp.sum(exps[0], axis=1, keepdims=True) + jnp.sum(wide, axis=1, keepdims=True)
            acc = _nn(exps[0].astype(BF), pv_ref[head]) + _nn(exps[1].astype(BF), read_b)
            for (_, r), part in zip(near, exps[2:]):
                acc = acc + _nn(part.astype(BF), vb_s[r, at])
            mixed_ref[target, at] = (acc / total).astype(BF)
            lse_all = jnp.where(
                _lane((128, 128), 1) == head, jnp.broadcast_to(top + jnp.log(total), (128, 128)), lse_all
            )
        lse_ref[rows, :] = lse_all


def _bwd_kernel(heads, blocks, where_ref, *rest):
    cots = rest[:4]
    saved = rest[4:11]
    weight_refs = rest[11 : 11 + blocks]
    rest = rest[11 + blocks :]
    dqkv_ref, dpk_ref, dpv_ref, dm1_ref, dm2_ref, keep_ref, send_ref = rest[:7]
    dmix_s, project_s, rates_s, out_s, sems = rest[7:12]
    scratch = rest[12:]
    step = weight_refs[0].shape[0] - 16
    wide = heads * 128
    every = pl.ds(0, step)
    out_copies = _copies(weight_refs, every, pl.ds(3 * wide, wide), out_s, sems.at[1])
    project_copies = _copies(weight_refs, every, pl.ds(0, 3 * wide), project_s, sems.at[0])
    rates_s[16:128, :] = jnp.zeros((112, rates_s.shape[1]), BF)
    for k, block in enumerate(weight_refs):
        copy = pltpu.make_async_copy(
            block.at[pl.ds(step, 16), pl.ds(0, step)],
            rates_s.at[pl.ds(0, 16), pl.ds(k * step, step)],
            sems.at[2, k],
        )
        copy.start()
        project_copies.append(copy)
    for copy in out_copies:
        copy.wait()
    for quarter, ref in enumerate(cots):
        dmix_s[quarter * 128 : (quarter + 1) * 128, :] = _nn(ref[...], out_s[...])
    _mix_backward(
        heads,
        where_ref,
        *saved,
        dmix_s,
        dqkv_ref,
        dpk_ref,
        dpv_ref,
        dm1_ref,
        dm2_ref,
        *scratch,
    )
    for copy in project_copies:
        copy.wait()
    for quarter in (2, 3, 0, 1):
        rows = slice(quarter * 128, (quarter + 1) * 128)
        grad = _nt(dqkv_ref[rows, : 3 * wide], project_s[...])
        grad = grad + _nn(dqkv_ref[rows, 3 * wide :], rates_s[...])
        if quarter >= 2:
            send_ref[(quarter - 2) * 128 : (quarter - 1) * 128, :] = grad.astype(BF)
        else:
            keep_ref[rows, :] = grad


def _mix_backward(
    heads,
    where_ref,
    qkv_ref,
    pk_ref,
    pv_ref,
    mixed_ref,
    reads_ref,
    lse_ref,
    states_ref,
    dmix_ref,
    dqkv_ref,
    dpk_ref,
    dpv_ref,
    dm1_ref,
    dm2_ref,
    qn_s,
    kn_s,
    qs_s,
    kb_s,
    v_s,
    vb_s,
    w_s,
    r_s,
    dq_s,
    dk_s,
    dv_s,
    dr_s,
    dqn_s,
    dkn_s,
    dz_s,
):
    place = where_ref[0]
    length = where_ref[1]
    width = heads * 128
    _load_rows(place, length, qkv_ref, heads, qn_s, kn_s, qs_s, kb_s, v_s, vb_s, w_s, r_s)
    masks = _masks()
    scale = 128 ** (-0.5)
    for head in range(heads):
        at = slice(head * 128, (head + 1) * 128)
        dpk = jnp.zeros((16, 128), F32)
        dpv = jnp.zeros((16, 128), F32)
        dk = [jnp.zeros((128, 128), F32)] * 4
        dv = [jnp.zeros((128, 128), F32)] * 4
        for block in range(4):
            rows = slice(block * 128, (block + 1) * 128)
            source = pl.ds(_spot(place, block), 128)
            qs = qs_s[rows, at]
            near = [
                (back, slice((block - back) * 128, (block - back + 1) * 128))
                for back in (2, 1, 0)
                if block - back >= 0
            ]
            read_b = reads_ref[rows, at]
            parts = _scores(
                qs, [(b, kb_s[r, at]) for b, r in near], read_b, pk_ref[head], block, length, masks
            )
            lse = lse_ref[rows, head : head + 1]
            probs = [jnp.exp(part - lse) for part in parts]
            dout = dmix_ref[source, at]
            dout_b = dout.astype(BF)
            dot = jnp.sum(dout * mixed_ref[source, at].astype(F32), axis=1, keepdims=True)
            values = [pv_ref[head], read_b] + [vb_s[r, at] for _, r in near]
            keys = [pk_ref[head], read_b] + [kb_s[r, at] for _, r in near]
            ds_b = [
                (p * (_nt(dout_b, val) - dot)).astype(BF) for p, val in zip(probs, values)
            ]
            probs_b = [p.astype(BF) for p in probs]
            dq = _nn(ds_b[0], keys[0])
            for d, key in zip(ds_b[1:], keys[1:]):
                dq = dq + _nn(d, key)
            dq_s[rows, at] = dq * scale
            dpk = dpk + _tn(ds_b[0], qs)
            dpv = dpv + _tn(probs_b[0], dout_b)
            dr_s[rows, at] = _tn(ds_b[1], qs) + _tn(probs_b[1], dout_b)
            for (back, _), d, p in zip(near, ds_b[2:], probs_b[2:]):
                dk[block - back] = dk[block - back] + _tn(d, qs)
                dv[block - back] = dv[block - back] + _tn(p, dout_b)
            if block >= 2:
                dk_s[(block - 2) * 128 : (block - 1) * 128, at] = dk[block - 2]
                dv_s[(block - 2) * 128 : (block - 1) * 128, at] = dv[block - 2]
        for block in (2, 3):
            rows = slice(block * 128, (block + 1) * 128)
            dk_s[rows, at] = dk[block]
            dv_s[rows, at] = dv[block]
        dpk_ref[head] = dpk
        dpv_ref[head] = dpv
    zero = jnp.zeros((128, 128), F32)
    carry = [[zero, zero, zero, zero] for _ in range(heads)]
    lanes = _lane((CH, 128), 1)
    for span in range(7, -1, -1):
        rows = slice(span * CH, (span + 1) * CH)
        means = jnp.mean(r_s[rows, :], axis=0, keepdims=True)
        dr_row = jnp.zeros((CH, 128), F32)
        live = (span * CH + _lane((CH, 1), 0) < length).astype(F32)
        for head in range(heads):
            at = slice(head * 128, (head + 1) * 128)
            a1, a2, b1, b2 = carry[head]
            first_b = states_ref[span, 0, head]
            second_b = states_ref[span, 1, head]
            kn = kn_s[rows, at]
            qn = qn_s[rows, at]
            dread_b = dr_s[rows, at].astype(BF)
            both = _nn(jnp.concatenate([kn, qn], axis=0), first_b)
            sig_both = _sig(both)
            act_both = both * sig_both
            slope_both = sig_both * (1.0 + both * (1.0 - sig_both))
            act_b = act_both.astype(BF)
            db_b = (_nt(dread_b, second_b) * slope_both[CH:]).astype(BF)
            if span == 7:
                dqn_s[rows, at] = _nt(db_b, first_b)
                dkn_s[rows, at] = jnp.zeros((CH, 128), F32)
                carry[head] = [_tn(qn, db_b), _tn(act_b[CH:], dread_b), zero, zero]
                continue
            eta = means[:, 3 * head + 1 : 3 * head + 2]
            keep = 1.0 - 0.5 * means[:, 3 * head + 2 : 3 * head + 3]
            pre, sig, slope = both[:CH], sig_both[:CH], slope_both[:CH]
            bend = sig * (1.0 - sig) * (2.0 + pre * (1.0 - 2.0 * sig))
            u_b = act_b[:CH]
            w = w_s[rows, at]
            e = _nn(u_b, second_b) - v_s[rows, at]
            m_b = (e * w).astype(BF)
            p = _nt(m_b, second_b)
            g_b = (p * slope).astype(BF)
            ds1 = b1 + a1
            ds2 = b2 + a2
            dg1_b = (-ds1).astype(BF)
            dg2_b = (-ds2).astype(BF)
            x1 = _nn(kn, dg1_b)
            dp_b = (x1 * slope).astype(BF)
            dm = _nn(dp_b, second_b) + _nn(u_b, dg2_b)
            de = dm * w
            de_b = de.astype(BF)
            du = _nt(m_b, dg2_b) + _nt(de_b, second_b)
            da = x1 * p * bend + du * slope
            da_b = da.astype(BF)
            back = _nt(jnp.concatenate([da_b, db_b], axis=0), first_b)
            dkn_s[rows, at] = _nt(g_b, dg1_b) + back[:CH]
            dqn_s[rows, at] = back[CH:]
            dv_s[rows, at] = dv_s[rows, at] - de
            new1 = keep * a1 + _tn(
                jnp.concatenate([kn, qn], axis=0), jnp.concatenate([da_b, db_b], axis=0)
            )
            new2 = (
                keep * a2
                + _tn(act_b, jnp.concatenate([de_b, dread_b], axis=0))
                + _tn(dp_b, m_b)
            )
            prev1 = states_ref[span, 2, head].astype(F32)
            prev2 = states_ref[span, 3, head].astype(F32)
            deta = jnp.sum(
                jnp.sum(ds1 * prev1 + ds2 * prev2, axis=0, keepdims=True), axis=1, keepdims=True
            )
            dkeep = jnp.sum(
                jnp.sum(a1 * first_b.astype(F32) + a2 * second_b.astype(F32), axis=0, keepdims=True),
                axis=1,
                keepdims=True,
            )
            dw = jnp.sum(dm * e, axis=1, keepdims=True) * live * (2.0 / (CH * 128))
            dr_row = jnp.where(lanes == 3 * head, jnp.broadcast_to(dw, (CH, 128)), dr_row)
            dr_row = jnp.where(
                lanes == 3 * head + 1, jnp.broadcast_to(deta * (1.0 / CH), (CH, 128)), dr_row
            )
            dr_row = jnp.where(
                lanes == 3 * head + 2, jnp.broadcast_to(dkeep * (-0.5 / CH), (CH, 128)), dr_row
            )
            carry[head] = [new1, new2, eta * ds1, eta * ds2]
        rates = r_s[rows, :]
        dz_s[rows, :] = dr_row * rates * (1.0 - rates)
    for head in range(heads):
        dm1_ref[head] = carry[head][0]
        dm2_ref[head] = carry[head][1]
    for quarter in range(4):
        source = pl.ds(_spot(place, quarter), 128)
        here = slice(quarter * 128, (quarter + 1) * 128)
        dqkv_ref[source, 3 * width :] = dz_s[here, :].astype(BF)
        for head in range(heads):
            at = slice(head * 128, (head + 1) * 128)
            for part, grad_s, norm_s in ((0, dq_s, dqn_s), (1, dk_s, dkn_s)):
                col = slice(part * width + head * 128, part * width + (head + 1) * 128)
                raw = qkv_ref[source, col]
                inverse = _scale_of(raw)
                normed = raw * inverse
                dn = norm_s[here, at]
                inner = jnp.mean(dn * normed, axis=-1, keepdims=True)
                dqkv_ref[source, col] = (
                    grad_s[here, at] + inverse * (dn - normed * inner)
                ).astype(BF)
            col = slice(2 * width + head * 128, 2 * width + (head + 1) * 128)
            dqkv_ref[source, col] = dv_s[here, at].astype(BF)


def _row_scratch(heads):
    wide = heads * 128
    return [
        pltpu.VMEM((512, wide), BF),
        pltpu.VMEM((512, wide), BF),
        pltpu.VMEM((512, wide), BF),
        pltpu.VMEM((512, wide), BF),
        pltpu.VMEM((512, wide), F32),
        pltpu.VMEM((512, wide), BF),
        pltpu.VMEM((512, wide), F32),
        pltpu.VMEM((512, 128), F32),
    ]


_VM = pl.BlockSpec(memory_space=pltpu.VMEM)
_SM = pl.BlockSpec(memory_space=pltpu.SMEM)


def _any(count):
    return [pl.BlockSpec(memory_space=pl.ANY)] * count


def _call(kernel, operands, in_specs, after, **settings):
    count = len(operands)
    more = len(after)

    def body(*refs):
        kernel(*refs[:count], *refs[count + more :])

    return pl.pallas_call(body, in_specs=[*in_specs, *_any(more)], **settings)(*operands, *after)


def mix_forward(where, quarters, batch, weights, pk, pv, m1, m2, after=()):
    heads = pk.shape[0]
    wide = heads * 128
    blocks = len(weights)
    step = weights[0].shape[0] - 16
    width = blocks * step
    return _call(
        partial(_fwd_kernel, heads, blocks, batch),
        (where, *quarters, pk, pv, m1, m2, *weights),
        [_SM] + [_VM] * 8 + _any(blocks),
        after,
        name="mix_forward",
        out_shape=(
            jax.ShapeDtypeStruct((512, width), BF),
            jax.ShapeDtypeStruct((16, width), F32),
            jax.ShapeDtypeStruct((128, width), F32),
            jax.ShapeDtypeStruct((512, 3 * wide + 128), F32),
            jax.ShapeDtypeStruct((512, wide), BF),
            jax.ShapeDtypeStruct((512, wide), BF),
            jax.ShapeDtypeStruct((512, 128), F32),
            jax.ShapeDtypeStruct((8, 4, heads, 128, 128), BF),
            jax.ShapeDtypeStruct((256, width), F32),
            jax.ShapeDtypeStruct((256, width), BF),
        ),
        out_specs=(_VM,) * 10,
        scratch_shapes=[
            pltpu.VMEM((width, 3 * wide), BF),
            pltpu.VMEM((128, width), BF),
            pltpu.VMEM((width, wide), BF),
            pltpu.SemaphoreType.DMA((3, blocks)),
        ]
        + _row_scratch(heads),
        compiler_params=pltpu.CompilerParams(vmem_limit_bytes=60 * 1024 * 1024),
        cost_estimate=pl.CostEstimate(flops=6 * 10**9, bytes_accessed=10**4, transcendentals=0),
    )


def mix_backward(where, cots, saved, weights, after=()):
    pk = saved[1]
    heads = pk.shape[0]
    wide = heads * 128
    blocks = len(weights)
    step = weights[0].shape[0] - 16
    width = blocks * step
    return _call(
        partial(_bwd_kernel, heads, blocks),
        (where, *cots, *saved, *weights),
        [_SM] + [_VM] * 11 + _any(blocks),
        after,
        name="mix_backward",
        out_shape=(
            jax.ShapeDtypeStruct((512, 3 * wide + 128), BF),
            jax.ShapeDtypeStruct((heads, 16, 128), F32),
            jax.ShapeDtypeStruct((heads, 16, 128), F32),
            jax.ShapeDtypeStruct((heads, 128, 128), F32),
            jax.ShapeDtypeStruct((heads, 128, 128), F32),
            jax.ShapeDtypeStruct((256, width), F32),
            jax.ShapeDtypeStruct((256, width), BF),
        ),
        out_specs=(_VM,) * 7,
        scratch_shapes=[
            pltpu.VMEM((512, wide), F32),
            pltpu.VMEM((width, 3 * wide), BF),
            pltpu.VMEM((128, width), BF),
            pltpu.VMEM((width, wide), BF),
            pltpu.SemaphoreType.DMA((3, blocks)),
        ]
        + _row_scratch(heads)
        + [pltpu.VMEM((512, wide), F32)] * 6
        + [pltpu.VMEM((512, 128), F32)],
        compiler_params=pltpu.CompilerParams(vmem_limit_bytes=60 * 1024 * 1024),
        cost_estimate=pl.CostEstimate(flops=7 * 10**9, bytes_accessed=10**4, transcendentals=0),
    )


def _feed_kernel(blocks, cols, batch, *rest):
    seconds = rest[:4]
    near_ref, far_ref = rest[4:6]
    weight_refs = rest[6 : 6 + blocks]
    (
        hidden_ref,
        gate_ref,
        up_ref,
        keep_ref,
        send_ref,
        feed_keep_ref,
        feed_send_ref,
        gate_s,
        up_s,
        down_s,
        sems,
    ) = rest[6 + blocks :]
    step = weight_refs[0].shape[0]
    copies = [
        _copies(weight_refs, pl.ds(0, step), pl.ds(w * cols, cols), target, sems.at[w])
        for w, target in enumerate((gate_s, up_s, down_s))
    ]
    for part in range(2):
        rows = slice(part * 256, (part + 1) * 256)
        left = jnp.concatenate([seconds[2 * part][...], seconds[2 * part + 1][...]], axis=0)
        cot = (near_ref, far_ref)[part][batch]
        if part == 0:
            for copy in copies[0]:
                copy.wait()
        gate = _nn(left, gate_s[...])
        if part == 0:
            for copy in copies[1]:
                copy.wait()
        up = _nn(left, up_s[...])
        if part == 0:
            for copy in copies[2]:
                copy.wait()
        grad = _nn(cot, down_s[...])
        sig = _sig(gate)
        act = gate * sig
        hidden = (act * up).astype(BF)
        gate_grad = (grad * up * (sig + act * (1.0 - sig))).astype(BF)
        up_grad = (grad * act).astype(BF)
        hidden_ref[rows, :] = hidden
        gate_ref[rows, :] = gate_grad
        up_ref[rows, :] = up_grad
        back = _nt(gate_grad, gate_s[...]) + _nt(up_grad, up_s[...])
        feed = _nt(hidden, down_s[...])
        if part == 0:
            keep_ref[...] = back
            feed_keep_ref[...] = feed
        else:
            send_ref[...] = back.astype(BF)
            feed_send_ref[...] = feed.astype(BF)


def feed_forward(seconds, near, far, batch, weights, after=()):
    blocks = len(weights)
    step = weights[0].shape[0]
    cols = weights[0].shape[1] // 3
    width = blocks * step
    return _call(
        partial(_feed_kernel, blocks, cols, batch),
        (*seconds, near, far, *weights),
        [_VM] * 6 + _any(blocks),
        after,
        name="feed_forward",
        out_shape=(
            jax.ShapeDtypeStruct((512, cols), BF),
            jax.ShapeDtypeStruct((512, cols), BF),
            jax.ShapeDtypeStruct((512, cols), BF),
            jax.ShapeDtypeStruct((256, width), F32),
            jax.ShapeDtypeStruct((256, width), BF),
            jax.ShapeDtypeStruct((256, width), F32),
            jax.ShapeDtypeStruct((256, width), BF),
        ),
        out_specs=(_VM,) * 7,
        scratch_shapes=[pltpu.VMEM((width, cols), BF)] * 3
        + [pltpu.SemaphoreType.DMA((3, blocks))],
        compiler_params=pltpu.CompilerParams(vmem_limit_bytes=48 * 1024 * 1024),
        cost_estimate=pl.CostEstimate(flops=35 * 10**8, bytes_accessed=10**4, transcendentals=0),
    )


def _grad_kernel(groups, counts, picks, keep, sends, *rest):
    total = sum(counts)
    row_refs = rest[:total]
    grad_refs = rest[total : total + len(counts)]
    outs = rest[total + len(counts) :]
    keep_refs, send_refs = outs[: len(keep)], outs[len(keep) :]
    targets = [
        (k, ref, place) for ref, some in zip(send_refs, sends) for place, k in enumerate(some)
    ]
    targets += [(k, ref, None) for ref, k in zip(keep_refs, keep)]
    step = outs[0].shape[-2]
    for k, out_ref, place in targets:
        at = slice(k * step, (k + 1) * step)
        start = 0
        index = 0
        term_at = 0
        for terms in groups:
            value = None
            for count, grad_ref in zip(
                counts[term_at : term_at + terms], grad_refs[term_at : term_at + terms]
            ):
                pieces = []
                for i in range(index, index + count):
                    ref, pick = row_refs[i], picks[i]
                    pieces.append(ref[:, at] if pick is None else ref[pick, :, at])
                index += count
                left = pieces[0] if count == 1 else jnp.concatenate(pieces, axis=0)
                term = _tn(left, grad_ref[...])
                value = term if value is None else value + term
            cols = slice(start, start + grad_refs[term_at].shape[1])
            start = cols.stop
            term_at += terms
            if place is None:
                out_ref[:, cols] = value
            else:
                out_ref[place, :, cols] = value.astype(BF)


def weight_gradient(groups, blocks, keep, sends, after=()):
    terms = [term for group in groups for term in group]
    width = terms[0][0][0][0].shape[-1]
    cols = sum(group[0][1].shape[1] for group in groups)
    step = width // blocks
    pieces = [piece for rows, _ in terms for piece in rows]
    grads = [grad for _, grad in terms]
    return _call(
        partial(
            _grad_kernel,
            tuple(len(group) for group in groups),
            tuple(len(rows) for rows, _ in terms),
            tuple(pick for _, pick in pieces),
            tuple(keep),
            tuple(sends),
        ),
        (*[array for array, _ in pieces], *grads),
        [_VM] * (len(pieces) + len(grads)),
        after,
        name="weight_gradient",
        out_shape=(
            *[_f32(step, cols)] * len(keep),
            *[_bf16(len(some), step, cols) for some in sends],
        ),
        out_specs=(_VM,) * (len(keep) + len(sends)),
        compiler_params=pltpu.CompilerParams(vmem_limit_bytes=48 * 1024 * 1024),
        cost_estimate=pl.CostEstimate(
            flops=4 * 10**8 * (len(keep) + sum(len(some) for some in sends)),
            bytes_accessed=10**4,
            transcendentals=0,
        ),
    )


def _small(name, function, shapes, scalars, values, after, flops=10**5):
    return _call(
        function,
        (*scalars, *values),
        [_SM] * len(scalars) + [_VM] * len(values),
        after,
        name=name,
        out_shape=shapes,
        out_specs=(_VM,) * len(shapes),
        cost_estimate=pl.CostEstimate(flops=flops, bytes_accessed=10**4, transcendentals=0),
        compiler_params=pltpu.CompilerParams(vmem_limit_bytes=32 * 1024 * 1024),
    )


def _f32(*shape):
    return jax.ShapeDtypeStruct(shape, F32)


def _bf16(*shape):
    return jax.ShapeDtypeStruct(shape, BF)


def _add_kernel(keep_ref, got_ref, own_ref, other_ref):
    own_ref[...] = keep_ref[0:128, :] + got_ref[0:128, :].astype(F32)
    other_ref[...] = (keep_ref[128:256, :] + got_ref[128:256, :].astype(F32)).astype(BF)


def add_core(keep, got, after=()):
    width = keep.shape[1]
    return _small("add_core", _add_kernel, (_f32(128, width), _bf16(128, width)), (), (keep, got), after)


def _norm_kernel(rows_ref, own_ref, column_ref, gain_ref, second_ref, residual_ref, inverse_ref):
    residual = rows_ref[...] + own_ref[...] + column_ref[...].astype(F32)
    inverse = _scale_of(residual)
    second_ref[...] = (residual * inverse * gain_ref[...]).astype(BF)
    residual_ref[...] = residual
    inverse_ref[...] = jnp.broadcast_to(inverse, (128, 128))


def second_norm(rows, own, column, gain, after=()):
    width = rows.shape[1]
    return _small(
        "second_norm",
        _norm_kernel,
        (_bf16(128, width), _f32(128, width), _f32(128, 128)),
        (),
        (rows, own, column, gain),
        after,
    )


def _norm_grad(grad, normed, inverse, gain):
    scaled = grad * gain
    return inverse * (scaled - normed * jnp.mean(scaled * normed, axis=-1, keepdims=True))


def _second_back_kernel(batch, own_ref, column_ref, cot_ref, residual_ref, inverse_ref, gain_ref, low_ref, out_ref, sum_ref):
    grad = own_ref[...] + column_ref[...].astype(F32)
    inverse = inverse_ref[:, 0:1]
    normed = residual_ref[...] * inverse
    out = cot_ref[batch] + _norm_grad(grad, normed, inverse, gain_ref[...])
    low_ref[...] = out.astype(BF)
    out_ref[...] = out
    sum_ref[...] = jnp.sum(grad * normed, axis=0, keepdims=True)


def second_back(batch, own, column, cots, residual, inverse, gain, after=()):
    width = own.shape[1]
    return _small(
        "second_back",
        partial(_second_back_kernel, batch),
        (_bf16(128, width), _f32(128, width), _f32(1, width)),
        (),
        (own, column, cots, residual, inverse, gain),
        after,
        3 * 10**9,
    )


def _place(where_ref, k, step):
    return pl.ds(pl.multiple_of(where_ref[2 + k] * step, step), step)


def _live(where_ref):
    return (where_ref[0] * 128 + _lane((128, 1), 0) < where_ref[1]).astype(F32)


def _cots_kernel(blocks, where_a, where_b, scale_ref, got_ref, rows_ref, low_ref):
    width = got_ref.shape[3]
    step = width // blocks
    for b, where_ref in enumerate((where_a, where_b)):
        factor = _live(where_ref) * scale_ref[b]
        for k in range(blocks):
            piece = got_ref[:, b, :, _place(where_ref, k, step)].reshape(128, step).astype(F32)
            piece = piece * factor
            rows_ref[b, :, k * step : (k + 1) * step] = piece
            low_ref[b, :, k * step : (k + 1) * step] = piece.astype(BF)


def take_cots(wheres, scales, got, after=()):
    blocks, batches, _, width = got.shape
    return _small(
        "take_cots",
        partial(_cots_kernel, blocks),
        (_f32(batches, 128, width), _bf16(batches, 128, width)),
        (*wheres, scales),
        (got,),
        after,
    )


def _finish_kernel(blocks, where_a, where_b, own_a, own_b, column_ref, res_a, res_b, out_ref):
    width = column_ref.shape[2]
    step = width // blocks
    for b, (where_ref, own, res) in enumerate(((where_a, own_a, res_a), (where_b, own_b, res_b))):
        rows = _live(where_ref) * (res[...] + own[...] + column_ref[b].astype(F32))
        rows = rows.astype(BF)
        for k in range(blocks):
            piece = rows[:, k * step : (k + 1) * step].reshape(blocks, 128 // blocks, step)
            out_ref[:, b, :, _place(where_ref, k, step)] = piece


def finish_rows(blocks, wheres, owns, column, residuals, after=()):
    width = column.shape[2]
    return _small(
        "finish_rows",
        partial(_finish_kernel, blocks),
        (_bf16(blocks, 2, 128 // blocks, width),),
        wheres,
        (*owns, column, *residuals),
        after,
    )[0]


def _token_grad(own_ref, column_ref, rows_ref, back_ref, gain_ref):
    grad = own_ref[...] + column_ref[...].astype(F32)
    rows = rows_ref[...]
    inverse = _scale_of(rows)
    normed = rows * inverse
    out = back_ref[...] + _norm_grad(grad, normed, inverse, gain_ref[...])
    return out.astype(BF), jnp.sum(grad * normed, axis=0, keepdims=True)


def _first_back_kernel(own_ref, column_ref, rows_ref, back_ref, gain_ref, low_ref, sum_ref):
    low_ref[...], sum_ref[...] = _token_grad(own_ref, column_ref, rows_ref, back_ref, gain_ref)


def first_back(own, column, rows, back, gain, after=()):
    width = own.shape[1]
    return _small(
        "first_back",
        _first_back_kernel,
        (_bf16(128, width), _f32(1, width)),
        (),
        (own, column, rows, back, gain),
        after,
    )


def _last_kernel(blocks, where_ref, own_ref, column_ref, rows_ref, back_ref, gain_ref, low_ref, sum_a, two_a, two_b, out_ref, gains_ref):
    width = own_ref.shape[1]
    step = width // blocks
    low, total = _token_grad(own_ref, column_ref, rows_ref, back_ref, gain_ref)
    total = total + sum_a[...]
    two = two_a[...] + two_b[...]
    first = low_ref[...]
    gains_ref[...] = jnp.zeros((8, width), F32)
    for k in range(blocks):
        at = slice(k * step, (k + 1) * step)
        place = _place(where_ref, k, step)
        out_ref[:, 0, :, place] = first[:, at].reshape(blocks, 128 // blocks, step)
        out_ref[:, 1, :, place] = low[:, at].reshape(blocks, 128 // blocks, step)
        gains_ref[0:1, place] = total[:, at]
        gains_ref[1:2, place] = two[:, at]


def last_rows(blocks, where, own, column, rows, back, gain, low, sum_a, two_a, two_b, after=()):
    width = own.shape[1]
    return _small(
        "last_rows",
        partial(_last_kernel, blocks),
        (_bf16(blocks, 2, 128 // blocks, width), _f32(8, width)),
        (where,),
        (own, column, rows, back, gain, low, sum_a, two_a, two_b),
        after,
    )


def _ring_kernel(indices, passing, splits, *rest):
    count = len(indices)
    keeps, gots = rest[:count], rest[count : 2 * count]
    passed_ref = rest[2 * count] if passing else None
    outs = rest[2 * count + passing :]
    start = 0
    done = 0
    for keep, got, index, sizes in zip(keeps, gots, indices, splits):
        cols = keep.shape[1]
        total = keep[...] + got[index].astype(F32)
        if passing:
            total = total + passed_ref[:, start : start + cols].astype(F32)
        if sizes is None:
            outs[0][:, start : start + cols] = total.astype(BF)
        else:
            for offset, size, turned in sizes:
                piece = total[:, offset : offset + -(-size // 128) * 128]
                if turned:
                    outs[done][...] = piece.T[:size]
                else:
                    outs[done][...] = piece[:, :size]
                done += 1
        start += cols


def ring_step(keeps, gots, indices, passed, splits=None, after=()):
    step = keeps[0].shape[0]
    cols = sum(k.shape[1] for k in keeps)
    if splits is None:
        shapes = (_bf16(step, cols),)
        splits = (None,) * len(keeps)
    else:
        shapes = tuple(
            _f32(size, step) if turned else _f32(step, size)
            for sizes in splits
            for _, size, turned in sizes
        )
    return _small(
        "ring_step",
        partial(_ring_kernel, tuple(indices), len(passed), tuple(splits)),
        shapes,
        (),
        (*keeps, *gots, *passed),
        after,
    )


def _hop_kernel(value_ref, got_ref, out_ref):
    out_ref[...] = value_ref[...] + got_ref[...].astype(F32)


def add_hop(value, got, after=()):
    return _small("add_hop", _hop_kernel, (_f32(*value.shape),), (), (value, got), after)[0]


def _join_kernel(*refs):
    *grads, out_ref = refs
    count = len(grads) // 2
    start = 0
    for one, two in zip(grads[:count], grads[count:]):
        for head in range(one.shape[0]):
            rows = one.shape[1]
            out_ref[start : start + rows, :] = one[head] + two[head]
            start += rows


def join_sums(one, two, after=()):
    rows = sum(g.shape[0] * g.shape[1] for g in one)
    return _small("join_sums", _join_kernel, (_f32(rows, 128),), (), (*one, *two), after)[0]


def _tick_kernel(out_ref):
    out_ref[...] = jnp.zeros((8, 128), F32)


def tick(after=()):
    return _small("tick", _tick_kernel, (_f32(8, 128),), (), (), after, 4 * 10**9)[0]


DP = ("z", "x")


def _swap(value, axis):
    return lax.ppermute(value, axis, [(0, 1), (1, 0)])


BLOCKS = 8
STEP = 128
DOWN = (1, 2, 3, 0)
RING = [(0, 1), (1, 2), (2, 3), (3, 0)]


def _ring_sized():
    return lax.axis_size("z") == 4


def _block_ids():
    if not _ring_sized():
        return jnp.arange(BLOCKS, dtype=jnp.int32)
    z = lax.axis_index("z")
    x = lax.axis_index("x")
    zs = jnp.stack([(z + 4 - i) % 4 for i in DOWN])
    return jnp.concatenate([2 * zs + x, 2 * zs + (1 - x)]).astype(jnp.int32)


class _Order:
    def __init__(self):
        self.last = []

    def __call__(self, function, *values, need=()):
        result = function(*values, after=(*self.last, *need))
        self.last = [min(jax.tree.leaves(result), key=lambda leaf: leaf.size)]
        return result


def _ring(block):
    return lax.ppermute(block, "z", RING)


def _in_order(ring, across):
    return [ring[i] for i in DOWN] + [across[i] for i in DOWN]


def _scatter_whole(keep, *sends):
    whole = jnp.concatenate([keep.astype(BF), *sends]).reshape(BLOCKS * STEP, -1)
    return lax.psum_scatter(whole, DP, scatter_dimension=0, tiled=True).astype(F32)


def _quarters(own):
    column = _swap(own, "y")
    return [own, column, _swap(own, "c"), _swap(column, "c")]


def per_device(
    tokens,
    grad_output,
    query_weight,
    key_weight,
    value_weight,
    rates_weight,
    out_weight,
    gate_weight,
    up_weight,
    down_weight,
    norm1_gain,
    norm2_gain,
    persist_key,
    persist_value,
    memory_first,
    memory_second,
    seq_lengths,
    deal,
):
    devices = lax.axis_size("z") * lax.axis_size("x")
    dp_index = lax.axis_index("z") * lax.axis_size("x") + lax.axis_index("x")
    place = lax.axis_index("y") * 2 + lax.axis_index("c")
    seq_count = seq_lengths.shape[0]
    batches = seq_count // devices
    local_rows = tokens.shape[2]
    width = tokens.shape[3]
    quarter = local_rows * devices
    rows_of = query_weight.shape[0]
    head_cols = query_weight.shape[1]
    rate_cols = rates_weight.shape[1]
    hidden_cols = gate_weight.shape[1]

    batch_of = deal // devices
    batch_ids = jnp.arange(batches, dtype=jnp.int32)
    batch_tokens = jnp.sum(
        jnp.where(batch_of[None, :] == batch_ids[:, None], seq_lengths[None, :], 0), axis=1
    ).astype(F32)
    batch_scale = jnp.sum(seq_lengths).astype(F32) / (batches * batch_tokens)
    span = range(batches)
    my_seqs = [batches * dp_index + b for b in span]
    lengths = [seq_lengths[s] for s in my_seqs]
    scales = [batch_scale[batch_of[s]] for s in my_seqs]
    ring_sized = _ring_sized()
    ids = _block_ids()
    where = [
        jnp.concatenate([jnp.stack([place, lengths[b]]).astype(jnp.int32), ids]) for b in span
    ]
    scale = jnp.stack(scales)

    def deal_in(array):
        part = array.reshape(devices, batches, local_rows, width)
        part = lax.all_to_all(part, DP, split_axis=0, concat_axis=0, tiled=True)
        if local_rows * BLOCKS == quarter:
            return part
        part = part.transpose(1, 0, 2, 3).reshape(batches, BLOCKS, quarter // BLOCKS, width)
        return part.transpose(1, 0, 2, 3)

    def deal_out(part):
        if local_rows * BLOCKS != quarter:
            part = part.transpose(1, 0, 2, 3).reshape(batches, devices, local_rows, width)
            part = part.transpose(1, 0, 2, 3)
        part = lax.all_to_all(part, DP, split_axis=0, concat_axis=0, tiled=True)
        return part.reshape(seq_count, 1, local_rows, width)

    mix_shard = jnp.concatenate([query_weight, key_weight, value_weight, out_weight], axis=1)
    extra = jnp.concatenate(
        [
            rates_weight.T,
            norm1_gain[None],
            norm2_gain[None],
            jnp.zeros((16 - rate_cols - 2, rows_of), BF),
        ]
    )
    pad = -hidden_cols % 128
    feed_shard = jnp.concatenate(
        [jnp.pad(w, ((0, 0), (0, pad))) for w in (gate_weight, up_weight, down_weight)], axis=1
    )
    got_tokens = deal_in(tokens)

    run = _Order()

    def mix_of(b, wheres, need=()):
        return run(
            mix_forward,
            wheres[b],
            quarters,
            b,
            mix_weights,
            persist_key,
            persist_value,
            memory_first,
            memory_second,
            need=need,
        )

    if ring_sized:
        extra = jnp.pad(extra, ((0, 0), (0, mix_shard.shape[1] - rows_of)))
        mix0 = jnp.concatenate([mix_shard, extra], axis=0)
        mix1 = _ring(mix0)
        mix_across0 = _swap(mix0, "x")
        mix1, mix_across0, feed0 = lax.optimization_barrier((mix1, mix_across0, feed_shard))
        mix2 = _ring(mix1)
        mix_across1 = _swap(mix1, "x")
        mix2, mix_across1 = lax.optimization_barrier((mix2, mix_across1))
        got_tokens, scale, *where = lax.optimization_barrier((got_tokens, scale, *where))
        mix3 = _ring(mix2)
        mix_across2 = _swap(mix2, "x")
        quarters = _quarters(got_tokens)
        mix3, mix_across2, feed0, cots_in = lax.optimization_barrier(
            (mix3, mix_across2, feed0, grad_output)
        )
        got_cots = deal_in(cots_in)
        mix_across3 = _swap(mix3, "x")
        feed1 = _ring(feed0)
        feed0, feed1, mix_across3 = lax.optimization_barrier((feed0, feed1, mix_across3))
        feed2 = _ring(feed1)
        feed_across0 = _swap(feed0, "x")
        mix_weights = _in_order(
            [mix0, mix1, mix2, mix3], [mix_across0, mix_across1, mix_across2, mix_across3]
        )
    else:
        mix_full = lax.all_gather(mix_shard, DP, axis=0, tiled=True)
        extra = lax.all_gather(extra, DP, axis=1, tiled=True)
        extra = jnp.pad(
            extra.reshape(16, BLOCKS, STEP), ((0, 0), (0, 0), (0, mix_shard.shape[1] - STEP))
        )
        mix_weights = [
            jnp.concatenate([mix_full[k * STEP : (k + 1) * STEP], extra[:, k]])
            for k in range(BLOCKS)
        ]
        feed_full = lax.all_gather(feed_shard, DP, axis=0, tiled=True)
        feed_weights = [feed_full[k * STEP : (k + 1) * STEP] for k in range(BLOCKS)]
        quarters = _quarters(got_tokens)
        got_cots = deal_in(grad_output)

    mix_a = mix_of(0, where, [feed1] if ring_sized else [])
    gain_one = mix_a[1][rate_cols : rate_cols + 1]
    gain_two = mix_a[1][rate_cols + 1 : rate_cols + 2]
    core_a = _swap(mix_a[9], "c")
    early = []
    run(tick, need=[feed2] if ring_sized else [])
    cot_rows, cot_own = run(take_cots, where, scale, got_cots)
    if ring_sized:
        feed3 = _ring(feed2)
        feed_across1 = _swap(feed1, "x")
        feed_across2 = _swap(feed2, "x")
        early = [feed3, feed_across1, feed_across2]
    own_a, other_a = run(
        add_core, mix_a[8], core_a, need=[feed_across0] if ring_sized else []
    )
    column_a = _swap(other_a, "y")
    cot_column = _swap(cot_own, "y")
    mix_b = mix_of(1, where)
    cot_column, *mix_b = lax.optimization_barrier((cot_column, *mix_b))
    mixes = [mix_a, mix_b]
    core_b = _swap(mix_b[9], "c")
    token_rows = [m[2] for m in mixes]
    run(tick, need=[*early, column_a, cot_column])
    second_a, residual_a, inverse_a = run(second_norm, token_rows[0], own_a, column_a, gain_two)
    early = []
    if ring_sized:
        feed_across3 = _swap(feed3, "x")
        feed_weights = _in_order(
            [feed0, feed1, feed2, feed3],
            [feed_across0, feed_across1, feed_across2, feed_across3],
        )
    second_a = _quarters(second_a)
    own_b, other_b = run(add_core, mix_b[8], core_b, need=[second_a[2]])
    column_b = _swap(other_b, "y")
    near = jnp.concatenate([cot_own, cot_column], axis=1)
    far = _swap(near, "c")
    second_b, residual_b, inverse_b = run(
        second_norm, token_rows[1], own_b, column_b, gain_two, need=[*early, far]
    )
    second_b = _quarters(second_b)
    second = [second_a, second_b]
    residual = [residual_a, residual_b]

    def feed_of(b, need=()):
        return run(feed_forward, second[b], near, far, b, feed_weights, need=need)

    feed_a = feed_of(0)
    core_a = _swap(feed_a[4], "c")
    run(tick, need=second_b[1:2])
    own_a, other_a = run(add_core, feed_a[3], core_a)
    column_a = _swap(other_a, "y")
    feed_b = feed_of(1)
    feeds = [feed_a, feed_b]
    core_b = _swap(feed_b[4], "c")
    def plain(pieces):
        return [(piece, None) for piece in pieces]

    def across(part):
        return _swap(part, "x") if ring_sized else part

    feed_groups = [
        [(plain(second[b]), feeds[b][1]) for b in span],
        [(plain(second[b]), feeds[b][2]) for b in span],
        [([(near, b), (far, b)], feeds[b][0]) for b in span],
    ]
    class Sum:
        def __init__(self, keeps, gots, splits):
            self.keeps = keeps
            self.gots = gots
            self.splits = splits
            self.pieces = [
                [(part, i) for part in got for i in range(part.shape[0])] for got in gots
            ]
            self.place = 0
            self.passed = []
            self.results = None

        def step(self, need=()):
            place = self.place
            self.place += 1
            final = place == 3
            if not ring_sized:
                if final:
                    self.results = [
                        whole[:, at : at + size].T if turned else whole[:, at : at + size]
                        for keep, got, sizes in zip(self.keeps, self.gots, self.splits)
                        for whole in [_scatter_whole(jnp.stack(keep), *got)]
                        for at, size, turned in sizes
                    ]
                return
            keeps = [keep[place] for keep in self.keeps]
            gots = [pieces[place][0] for pieces in self.pieces]
            indices = [pieces[place][1] for pieces in self.pieces]
            results = run(
                ring_step, keeps, gots, indices, self.passed, self.splits if final else None, need=need
            )
            if final:
                self.results = results
            else:
                self.passed = [_ring(results[0])]

    class AllSum:
        def __init__(self, value, axes, sent):
            self.value = value
            self.sent = sent
            self.hops = []
            for axis in axes:
                size = lax.axis_size(axis)
                step = 1
                while step < size:
                    self.hops.append((axis, [(i, i ^ step) for i in range(size)]))
                    step *= 2
            self.start()

        def start(self):
            if self.hops:
                axis, pairs = self.hops.pop(0)
                self.got = lax.ppermute(self.value.astype(self.sent), axis, pairs)

        def step(self, need=()):
            self.value = run(add_hop, self.value, self.got, need=need)
            self.got = None
            self.start()

        def rest(self):
            while self.got is not None:
                self.step()
            return self.value

    run(tick, need=[column_a])
    mixer_a, back_a, two_a = run(
        second_back, 0, own_a, column_a, cot_rows, residual_a, inverse_a, gain_two
    )
    mixer_column = _swap(mixer_a, "y")
    mixer_core = _swap(mixer_a, "c")
    own_b, other_b = run(add_core, feed_b[3], core_b)
    column_b = _swap(other_b, "y")
    first_sends = run(weight_gradient, feed_groups, BLOCKS, (), ((4,),))
    feed_got = [across(first_sends[0])]
    feed_core = [_swap(f[6], "c") for f in feeds]
    feed_own, feed_other = zip(
        *[run(add_core, feeds[b][5], feed_core[b], need=[mixer_core]) for b in span],
        strict=True,
    )
    feed_parts = run(weight_gradient, feed_groups, BLOCKS, range(4), ((5,), (6, 7)))
    feed_got += [across(part) for part in feed_parts[4:]]
    feed_keep = feed_parts[:4]
    mixer_column, *feed_keep = lax.optimization_barrier((mixer_column, *feed_keep))
    mixer_a = [mixer_a, mixer_column, mixer_core, _swap(mixer_column, "c")]
    mixer_b, back_b, two_b = run(
        second_back, 1, own_b, column_b, cot_rows, residual_b, inverse_b, gain_two
    )
    mixer_b = _quarters(mixer_b)
    feed_column = _swap(jnp.stack(feed_other), "y")
    stride = feed_keep[0].shape[1] // 3
    feed_sum = Sum(
        [feed_keep],
        [feed_got],
        [[(i * stride, hidden_cols, True) for i in range(3)]],
    )
    feed_sum.step()

    def mix_back_of(b, cots, need=()):
        saved = (mixes[b][3], persist_key, persist_value, *mixes[b][4:8])
        return run(mix_backward, where[b], cots, saved, mix_weights, need=need)

    mix_back_a = mix_back_of(0, mixer_a, need=[mixer_b[2]])
    core_a = _swap(mix_back_a[6], "c")
    run(tick, need=[*feed_sum.passed, mixer_b[1], feed_column])
    feed_sum.step()
    layer_out = deal_out(run(finish_rows, BLOCKS, where, feed_own, feed_column, residual))
    own_a, other_a = run(add_core, mix_back_a[5], core_a)
    column_a = _swap(other_a, "y")
    mix_back_b = mix_back_of(1, mixer_b)
    backs = [mix_back_a, mix_back_b]
    core_b = _swap(mix_back_b[6], "c")
    run(tick, need=[column_a, *feed_sum.passed, feed_got[-1], layer_out])
    project_groups = [
        [(plain([m[0]]), k[0]) for m, k in zip(mixes, backs)],
        [(plain(mixer), m[4]) for mixer, m in ((mixer_a, mix_a), (mixer_b, mix_b))],
    ]
    first_sends = run(weight_gradient, project_groups, BLOCKS, (), ((4,),))
    project_got = [across(first_sends[0])]
    feed_sum.step()
    own_b, other_b = run(add_core, mix_back_b[5], core_b)
    column_b = _swap(other_b, "y")
    memory_sum = AllSum(
        run(join_sums, mix_back_a[1:5], mix_back_b[1:5]), DP[::-1], BF
    )
    project_parts = run(weight_gradient, project_groups, BLOCKS, range(4), ((5,), (6, 7)))
    project_keep = project_parts[:4]
    if ring_sized:
        project_got[0], *late = lax.optimization_barrier((project_got[0], *project_parts[4:]))
    else:
        late = project_parts[4:]
    project_got += [across(part) for part in late]
    rates_at = 3 * head_cols
    project_sum = Sum(
        [project_keep],
        [project_got],
        [
            [(i * head_cols, head_cols, False) for i in range(3)]
            + [(rates_at, rate_cols, False), (rates_at + 128, head_cols, False)]
        ],
    )
    project_sum.step()
    memory_sum.step()
    token_a, one_a = run(first_back, own_a, column_a, token_rows[0], back_a, gain_one)
    token_send, gains = run(
        last_rows,
        BLOCKS,
        where[1],
        own_b,
        column_b,
        token_rows[1],
        back_b,
        gain_one,
        token_a,
        one_a,
        two_a,
        two_b,
    )
    grad_tokens = deal_out(token_send)
    gain_sum = AllSum(gains, ("c", "y", "x", "z"), F32)
    gain_sum.step()
    project_sum.step()
    feed_sum.step()
    gain_sum.step()
    memory_sum.step()
    gain_sum.step()
    project_sum.step()
    gain_sum.step()
    flat = memory_sum.rest()
    gains = gain_sum.rest()
    project_sum.step()
    gate_total, up_total, down_total = feed_sum.results
    *project_totals, out_total = project_sum.results

    memory_out = []
    start = 0
    for m in mix_back_a[1:5]:
        size = m.size // 128
        memory_out.append(flat[start : start + size].reshape(m.shape))
        start += size

    return (
        layer_out,
        grad_tokens,
        *project_totals,
        out_total,
        gate_total.T,
        up_total.T,
        down_total.T,
        gains[0],
        gains[1],
        memory_out[0],
        memory_out[1],
        memory_out[2],
        memory_out[3],
    )


def solution(mesh):
    sizes = mesh.devices.shape
    fine = Mesh(mesh.devices.reshape(sizes[0] // 2, 2, 2, sizes[1] // 2), ("z", "x", "y", "c"))
    tensor = ("y", "c")
    return jax.shard_map(
        per_device,
        mesh=fine,
        in_specs=(
            P(None, tensor, DP, None),
            P(None, tensor, DP, None),
            P(DP, tensor),
            P(DP, tensor),
            P(DP, tensor),
            P(DP, tensor),
            P(DP, tensor),
            P(DP, tensor),
            P(DP, tensor),
            P(DP, tensor),
            P(DP),
            P(DP),
            P(tensor, None, None),
            P(tensor, None, None),
            P(tensor, None, None),
            P(tensor, None, None),
            P(),
            P(),
        ),
        out_specs=(
            P(None, tensor, DP, None),
            P(None, tensor, DP, None),
            P(DP, tensor),
            P(DP, tensor),
            P(DP, tensor),
            P(DP, tensor),
            P(DP, tensor),
            P(DP, tensor),
            P(DP, tensor),
            P(DP, tensor),
            P(),
            P(),
            P(tensor, None, None),
            P(tensor, None, None),
            P(tensor, None, None),
            P(tensor, None, None),
        ),
        check_vma=False,
    )
```

```python
from functools import partial

import jax
import jax.numpy as jnp
from jax import lax
from jax.experimental import pallas as pl
from jax.experimental.pallas import tpu as pltpu
from jax.sharding import Mesh
from jax.sharding import PartitionSpec as P

CH = 64
WINDOW = 256
EPS = 1e-06
NEG = -1e30
BF = jnp.bfloat16
F32 = jnp.float32


def _nn(a, b):
    return lax.dot_general(a, b, (((1,), (0,)), ((), ())), preferred_element_type=F32)


def _nt(a, b):
    return lax.dot_general(a, b, (((1,), (1,)), ((), ())), preferred_element_type=F32)


def _tn(a, b):
    return lax.dot_general(a, b, (((0,), (0,)), ((), ())), preferred_element_type=F32)


def _sig(v):
    return 1.0 / (1.0 + jnp.exp(-v))


def _scale_of(v):
    return lax.rsqrt(jnp.mean(v * v, axis=-1, keepdims=True) + EPS)


def _lane(shape, dim):
    return lax.broadcasted_iota(jnp.int32, shape, dim)


def _masks():
    rows = _lane((128, 128), 0)
    cols = _lane((128, 128), 1)
    return cols > rows, cols <= rows, (rows // CH) == (cols // CH)


def _scores(qs, near_keys, read_b, pkey, block, length, masks):
    older, newer, same_span = masks
    read_ok = same_span & (block * 128 + _lane((128, 128), 1) < length)
    parts = [_nt(qs, pkey), jnp.where(read_ok, _nt(qs, read_b), NEG)]
    for back, keys in near_keys:
        part = _nt(qs, keys)
        if back == 2:
            part = jnp.where(older, part, NEG)
        elif back == 0:
            part = jnp.where(newer, part, NEG)
        parts.append(part)
    return parts


def _spot(place, quarter):
    there = place ^ quarter
    return pl.multiple_of((((there & 1) << 1) | (there >> 1)) * 128, 128)


def _load_rows(place, length, qkv_ref, heads, qn_s, kn_s, qs_s, kb_s, v_s, vb_s, w_s, r_s):
    width = heads * 128
    for quarter in range(4):
        source = pl.ds(_spot(place, quarter), 128)
        here = pl.ds(quarter * 128, 128)
        live = (quarter * 128 + _lane((128, 1), 0) < length).astype(F32)
        rates = _sig(qkv_ref[source, 3 * width : 3 * width + 128])
        r_s[here, :] = rates
        for head in range(heads):
            at = slice(head * 128, (head + 1) * 128)
            q = qkv_ref[source, head * 128 : (head + 1) * 128]
            k = qkv_ref[source, width + head * 128 : width + (head + 1) * 128]
            v = qkv_ref[source, 2 * width + head * 128 : 2 * width + (head + 1) * 128]
            qn_s[here, at] = (q * _scale_of(q)).astype(BF)
            kn_s[here, at] = (k * _scale_of(k)).astype(BF)
            qs_s[here, at] = (q * (128 ** (-0.5))).astype(BF)
            kb_s[here, at] = k.astype(BF)
            v_s[here, at] = v
            vb_s[here, at] = v.astype(BF)
            weighting = rates[:, 3 * head : 3 * head + 1] * live * (2.0 / (CH * 128))
            w_s[here, at] = jnp.broadcast_to(weighting, (128, 128))


def _block(block, pick, rows, cols):
    return block.at[rows, cols] if pick is None else block.at[pick, rows, cols]


def _copies(blocks, rows, cols, target, sems, picks=None):
    made = []
    for k, block in enumerate(blocks):
        copy = pltpu.make_async_copy(
            _block(block, picks[k] if picks else None, rows, cols),
            target.at[pl.ds(k * rows.size, rows.size), :],
            sems.at[k],
        )
        copy.start()
        made.append(copy)
    return made


def _fwd_kernel(
    heads,
    blocks,
    batch,
    where_ref,
    own_ref,
    ypart_ref,
    cpart_ref,
    far_ref,
    pk_ref,
    pv_ref,
    m1_ref,
    m2_ref,
    *rest,
):
    weight_refs = rest[:blocks]
    extra_ref, token_ref, mixed_ref, lse_ref, keep_ref, send_ref = rest[blocks : blocks + 6]
    first_hbm, qkv_hbm, reads_hbm, states_hbm = rest[blocks + 6 : blocks + 10]
    (
        pieces_s,
        first_s,
        qkv_s,
        reads_s,
        states_s,
        project_s,
        rates_s,
        out_s,
        sems,
        piece_sems,
        out_sems,
        state_sems,
    ) = rest[blocks + 10 : blocks + 22]
    scratch = rest[blocks + 22 :]
    step = weight_refs[0].shape[0] - 16
    wide = heads * 128
    every = pl.ds(0, step)
    piece_copies = []
    for quarter, ref in enumerate((own_ref, ypart_ref, cpart_ref, far_ref)):
        copy = pltpu.make_async_copy(
            ref.at[:, batch], pieces_s.at[quarter], piece_sems.at[quarter]
        )
        copy.start()
        piece_copies.append(copy)
    rates_s[16:128, :] = jnp.zeros((112, rates_s.shape[1]), BF)
    extra = []
    for k, block in enumerate(weight_refs):
        copy = pltpu.make_async_copy(
            block.at[pl.ds(step, 16), pl.ds(0, step)],
            rates_s.at[pl.ds(0, 16), pl.ds(k * step, step)],
            sems.at[2, k],
        )
        copy.start()
        extra.append(copy)
    project_copies = _copies(weight_refs, every, pl.ds(0, 3 * wide), project_s, sems.at[0])
    out_copies = _copies(weight_refs, every, pl.ds(3 * wide, wide), out_s, sems.at[1])
    for copy in extra:
        copy.wait()
    extra_rows = rates_s[0:16, :].astype(F32)
    extra_ref[...] = extra_rows
    gain = extra_rows[3 * heads : 3 * heads + 1, :]
    width = blocks * step
    for quarter in range(4):
        piece_copies[quarter].wait()
        raw = pieces_s[quarter].reshape(128, width).astype(F32)
        inverse = _scale_of(raw)
        for k in range(blocks):
            source = pl.ds(pl.multiple_of(where_ref[2 + k] * step, step), step)
            piece = pieces_s[quarter, :, :, source].reshape(128, step).astype(F32)
            at = slice(k * step, (k + 1) * step)
            if quarter == 0:
                token_ref[:, at] = piece
            first_s[quarter * 128 : (quarter + 1) * 128, at] = (
                piece * inverse * gain[:, at]
            ).astype(BF)
    outgoing = [pltpu.make_async_copy(first_s, first_hbm, out_sems.at[0])]
    outgoing[0].start()
    for copy in project_copies:
        copy.wait()
    for quarter in range(4):
        rows = slice(quarter * 128, (quarter + 1) * 128)
        left = first_s[rows, :]
        qkv_s[rows, : 3 * wide] = _nn(left, project_s[...])
        qkv_s[rows, 3 * wide :] = _nt(left, rates_s[...])
    outgoing.append(pltpu.make_async_copy(qkv_s, qkv_hbm, out_sems.at[1]))
    outgoing[1].start()

    def send_state(span):
        copy = pltpu.make_async_copy(
            states_s.at[span], states_hbm.at[span], state_sems.at[span]
        )
        copy.start()
        outgoing.append(copy)

    def send_reads():
        copy = pltpu.make_async_copy(reads_s, reads_hbm, out_sems.at[2])
        copy.start()
        outgoing.append(copy)

    _mix_forward(
        heads,
        send_state,
        send_reads,
        where_ref,
        qkv_s,
        pk_ref,
        pv_ref,
        m1_ref,
        m2_ref,
        mixed_ref,
        reads_s,
        lse_ref,
        states_s,
        *scratch,
    )
    for copy in out_copies:
        copy.wait()
    send_ref[...] = _nt(mixed_ref[256:512, :], out_s[...]).astype(BF)
    keep_ref[...] = _nt(mixed_ref[0:256, :], out_s[...]).astype(BF)
    for copy in outgoing:
        copy.wait()


def _mix_forward(
    heads,
    send_state,
    send_reads,
    where_ref,
    qkv_ref,
    pk_ref,
    pv_ref,
    m1_ref,
    m2_ref,
    mixed_ref,
    reads_ref,
    lse_ref,
    states_ref,
    qn_s,
    kn_s,
    qs_s,
    kb_s,
    v_s,
    vb_s,
    w_s,
    r_s,
):
    place = where_ref[0]
    length = where_ref[1]
    _load_rows(place, length, qkv_ref, heads, qn_s, kn_s, qs_s, kb_s, v_s, vb_s, w_s, r_s)
    carry = [
        [m1_ref[h], m2_ref[h], jnp.zeros((128, 128), F32), jnp.zeros((128, 128), F32)]
        for h in range(heads)
    ]
    for span in range(8):
        rows = slice(span * CH, (span + 1) * CH)
        means = jnp.mean(r_s[rows, :], axis=0, keepdims=True)
        for head in range(heads):
            at = slice(head * 128, (head + 1) * 128)
            first, second, s1, s2 = carry[head]
            first_b, second_b = first.astype(BF), second.astype(BF)
            states_ref[span, 0, head] = first_b
            states_ref[span, 1, head] = second_b
            states_ref[span, 2, head] = s1.astype(BF)
            states_ref[span, 3, head] = s2.astype(BF)
            kn = kn_s[rows, at]
            qn = qn_s[rows, at]
            both = _nn(jnp.concatenate([kn, qn], axis=0), first_b)
            both = both * _sig(both) if span == 7 else both
            if span < 7:
                pre = both[:CH]
                sig = _sig(both)
                act_both = both * sig
                sig_k = sig[:CH]
            else:
                act_both = both
            out_both = _nn(act_both.astype(BF), second_b)
            reads_ref[rows, at] = out_both[CH:].astype(BF)
            if span < 7:
                act = act_both[:CH]
                miss = (out_both[:CH] - v_s[rows, at]) * w_s[rows, at]
                miss_b = miss.astype(BF)
                grad_second = _tn(act.astype(BF), miss_b)
                grad_pre = _nt(miss_b, second_b) * sig_k * (1.0 + pre * (1.0 - sig_k))
                grad_first = _tn(kn, grad_pre.astype(BF))
                eta = means[:, 3 * head + 1 : 3 * head + 2]
                keep = 1.0 - 0.5 * means[:, 3 * head + 2 : 3 * head + 3]
                s1 = eta * s1 - grad_first
                s2 = eta * s2 - grad_second
                carry[head] = [keep * first + s1, keep * second + s2, s1, s2]
        send_state(span)
    send_reads()
    masks = _masks()
    for block in range(4):
        rows = slice(block * 128, (block + 1) * 128)
        target = pl.ds(_spot(place, block), 128)
        lse_all = jnp.zeros((128, 128), F32)
        for head in range(heads):
            at = slice(head * 128, (head + 1) * 128)
            qs = qs_s[rows, at]
            near = [
                (back, slice((block - back) * 128, (block - back + 1) * 128))
                for back in (2, 1, 0)
                if block - back >= 0
            ]
            read_b = reads_ref[rows, at]
            parts = _scores(
                qs, [(b, kb_s[r, at]) for b, r in near], read_b, pk_ref[head], block, length, masks
            )
            top = jnp.max(parts[0], axis=1, keepdims=True)
            wide = parts[1]
            for part in parts[2:]:
                wide = jnp.maximum(wide, part)
            top = jnp.maximum(top, jnp.max(wide, axis=1, keepdims=True))
            exps = [jnp.exp(part - top) for part in parts]
            wide = exps[1]
            for part in exps[2:]:
                wide = wide + part
            total = jnp.sum(exps[0], axis=1, keepdims=True) + jnp.sum(wide, axis=1, keepdims=True)
            acc = _nn(exps[0].astype(BF), pv_ref[head]) + _nn(exps[1].astype(BF), read_b)
            for (_, r), part in zip(near, exps[2:]):
                acc = acc + _nn(part.astype(BF), vb_s[r, at])
            mixed_ref[target, at] = (acc * (1.0 / total)).astype(BF)
            lse_all = jnp.where(
                _lane((128, 128), 1) == head, jnp.broadcast_to(top + jnp.log(total), (128, 128)), lse_all
            )
        lse_ref[rows, :] = lse_all


def _bwd_kernel(heads, blocks, where_ref, *rest):
    cots = rest[:4]
    qkv_hbm, pk_ref, pv_ref, mixed_ref, reads_ref, lse_ref, states_hbm = rest[4:11]
    weight_refs = rest[11 : 11 + blocks]
    rest = rest[11 + blocks :]
    dqkv_hbm, dpk_ref, dpv_ref, dm1_ref, dm2_ref, keep_ref, send_ref = rest[:7]
    cots_s, qkv_s, states_s, dqkv_s, dmix_s, project_s, rates_s, out_s, sems, more_sems = rest[7:17]
    scratch = rest[17:]
    step = weight_refs[0].shape[0] - 16
    wide = heads * 128
    every = pl.ds(0, step)
    out_copies = _copies(weight_refs, every, pl.ds(3 * wide, wide), out_s, sems.at[1])
    cot_copies = []
    for quarter, ref in enumerate(cots):
        copy = pltpu.make_async_copy(ref, cots_s.at[quarter], more_sems.at[quarter])
        copy.start()
        cot_copies.append(copy)
    qkv_copy = pltpu.make_async_copy(qkv_hbm, qkv_s, more_sems.at[4])
    qkv_copy.start()
    states_copy = pltpu.make_async_copy(states_hbm, states_s, more_sems.at[5])
    states_copy.start()
    project_copies = _copies(weight_refs, every, pl.ds(0, 3 * wide), project_s, sems.at[0])
    rates_s[16:128, :] = jnp.zeros((112, rates_s.shape[1]), BF)
    for k, block in enumerate(weight_refs):
        copy = pltpu.make_async_copy(
            block.at[pl.ds(step, 16), pl.ds(0, step)],
            rates_s.at[pl.ds(0, 16), pl.ds(k * step, step)],
            sems.at[2, k],
        )
        copy.start()
        project_copies.append(copy)
    for copy in out_copies:
        copy.wait()
    for quarter in range(4):
        cot_copies[quarter].wait()
        dmix_s[quarter * 128 : (quarter + 1) * 128, :] = _nn(cots_s[quarter], out_s[...])
    qkv_copy.wait()
    _mix_backward(
        heads,
        states_copy.wait,
        where_ref,
        qkv_s,
        pk_ref,
        pv_ref,
        mixed_ref,
        reads_ref,
        lse_ref,
        states_s,
        dmix_s,
        dqkv_s,
        dpk_ref,
        dpv_ref,
        dm1_ref,
        dm2_ref,
        *scratch,
    )
    dqkv_copy = pltpu.make_async_copy(dqkv_s, dqkv_hbm, more_sems.at[6])
    dqkv_copy.start()
    for copy in project_copies:
        copy.wait()
    for rows in (slice(256, 512), slice(0, 256)):
        grad = _nt(dqkv_s[rows, : 3 * wide], project_s[...])
        grad = grad + _nn(dqkv_s[rows, 3 * wide :], rates_s[...])
        if rows.start:
            send_ref[...] = grad.astype(BF)
        else:
            keep_ref[...] = grad.astype(BF)
    dqkv_copy.wait()


def _mix_backward(
    heads,
    wait_states,
    where_ref,
    qkv_ref,
    pk_ref,
    pv_ref,
    mixed_ref,
    reads_ref,
    lse_ref,
    states_ref,
    dmix_ref,
    dqkv_ref,
    dpk_ref,
    dpv_ref,
    dm1_ref,
    dm2_ref,
    qn_s,
    kn_s,
    qs_s,
    kb_s,
    v_s,
    vb_s,
    w_s,
    r_s,
    dq_s,
    dk_s,
    dv_s,
    dr_s,
    dqn_s,
    dkn_s,
    dz_s,
):
    place = where_ref[0]
    length = where_ref[1]
    width = heads * 128
    _load_rows(place, length, qkv_ref, heads, qn_s, kn_s, qs_s, kb_s, v_s, vb_s, w_s, r_s)
    masks = _masks()
    scale = 128 ** (-0.5)
    for head in range(heads):
        at = slice(head * 128, (head + 1) * 128)
        dpk = jnp.zeros((16, 128), F32)
        dpv = jnp.zeros((16, 128), F32)
        dk = [jnp.zeros((128, 128), F32)] * 4
        dv = [jnp.zeros((128, 128), F32)] * 4
        for block in range(4):
            rows = slice(block * 128, (block + 1) * 128)
            source = pl.ds(_spot(place, block), 128)
            qs = qs_s[rows, at]
            near = [
                (back, slice((block - back) * 128, (block - back + 1) * 128))
                for back in (2, 1, 0)
                if block - back >= 0
            ]
            read_b = reads_ref[rows, at]
            parts = _scores(
                qs, [(b, kb_s[r, at]) for b, r in near], read_b, pk_ref[head], block, length, masks
            )
            lse = lse_ref[rows, head : head + 1]
            probs = [jnp.exp(part - lse) for part in parts]
            dout = dmix_ref[source, at]
            dout_b = dout.astype(BF)
            dot = jnp.sum(dout * mixed_ref[source, at].astype(F32), axis=1, keepdims=True)
            values = [pv_ref[head], read_b] + [vb_s[r, at] for _, r in near]
            keys = [pk_ref[head], read_b] + [kb_s[r, at] for _, r in near]
            ds_b = [
                (p * (_nt(dout_b, val) - dot)).astype(BF) for p, val in zip(probs, values)
            ]
            probs_b = [p.astype(BF) for p in probs]
            dq = _nn(ds_b[0], keys[0])
            for d, key in zip(ds_b[1:], keys[1:]):
                dq = dq + _nn(d, key)
            dq_s[rows, at] = dq * scale
            dpk = dpk + _tn(ds_b[0], qs)
            dpv = dpv + _tn(probs_b[0], dout_b)
            dr_s[rows, at] = _tn(ds_b[1], qs) + _tn(probs_b[1], dout_b)
            for (back, _), d, p in zip(near, ds_b[2:], probs_b[2:]):
                dk[block - back] = dk[block - back] + _tn(d, qs)
                dv[block - back] = dv[block - back] + _tn(p, dout_b)
            if block >= 2:
                dk_s[(block - 2) * 128 : (block - 1) * 128, at] = dk[block - 2]
                dv_s[(block - 2) * 128 : (block - 1) * 128, at] = dv[block - 2]
        for block in (2, 3):
            rows = slice(block * 128, (block + 1) * 128)
            dk_s[rows, at] = dk[block]
            dv_s[rows, at] = dv[block]
        dpk_ref[head] = dpk
        dpv_ref[head] = dpv
    wait_states()
    zero = jnp.zeros((128, 128), F32)
    carry = [[zero, zero, zero, zero] for _ in range(heads)]
    lanes = _lane((CH, 128), 1)
    for span in range(7, -1, -1):
        rows = slice(span * CH, (span + 1) * CH)
        means = jnp.mean(r_s[rows, :], axis=0, keepdims=True)
        dr_row = jnp.zeros((CH, 128), F32)
        live = (span * CH + _lane((CH, 1), 0) < length).astype(F32)
        for head in range(heads):
            at = slice(head * 128, (head + 1) * 128)
            a1, a2, b1, b2 = carry[head]
            first_b = states_ref[span, 0, head]
            second_b = states_ref[span, 1, head]
            kn = kn_s[rows, at]
            qn = qn_s[rows, at]
            dread_b = dr_s[rows, at].astype(BF)
            both = _nn(jnp.concatenate([kn, qn], axis=0), first_b)
            sig_both = _sig(both)
            act_both = both * sig_both
            slope_both = sig_both * (1.0 + both * (1.0 - sig_both))
            act_b = act_both.astype(BF)
            db_b = (_nt(dread_b, second_b) * slope_both[CH:]).astype(BF)
            if span == 7:
                dqn_s[rows, at] = _nt(db_b, first_b)
                dkn_s[rows, at] = jnp.zeros((CH, 128), F32)
                carry[head] = [_tn(qn, db_b), _tn(act_b[CH:], dread_b), zero, zero]
                continue
            eta = means[:, 3 * head + 1 : 3 * head + 2]
            keep = 1.0 - 0.5 * means[:, 3 * head + 2 : 3 * head + 3]
            pre, sig, slope = both[:CH], sig_both[:CH], slope_both[:CH]
            bend = sig * (1.0 - sig) * (2.0 + pre * (1.0 - 2.0 * sig))
            u_b = act_b[:CH]
            w = w_s[rows, at]
            e = _nn(u_b, second_b) - v_s[rows, at]
            m_b = (e * w).astype(BF)
            p = _nt(m_b, second_b)
            g_b = (p * slope).astype(BF)
            ds1 = b1 + a1
            ds2 = b2 + a2
            dg1_b = (-ds1).astype(BF)
            dg2_b = (-ds2).astype(BF)
            x1 = _nn(kn, dg1_b)
            dp_b = (x1 * slope).astype(BF)
            dm = _nn(dp_b, second_b) + _nn(u_b, dg2_b)
            de = dm * w
            de_b = de.astype(BF)
            du = _nt(m_b, dg2_b) + _nt(de_b, second_b)
            da = x1 * p * bend + du * slope
            da_b = da.astype(BF)
            back = _nt(jnp.concatenate([da_b, db_b], axis=0), first_b)
            dkn_s[rows, at] = _nt(g_b, dg1_b) + back[:CH]
            dqn_s[rows, at] = back[CH:]
            dv_s[rows, at] = dv_s[rows, at] - de
            new1 = keep * a1 + _tn(
                jnp.concatenate([kn, qn], axis=0), jnp.concatenate([da_b, db_b], axis=0)
            )
            new2 = (
                keep * a2
                + _tn(act_b, jnp.concatenate([de_b, dread_b], axis=0))
                + _tn(dp_b, m_b)
            )
            prev1 = states_ref[span, 2, head].astype(F32)
            prev2 = states_ref[span, 3, head].astype(F32)
            deta = jnp.sum(
                jnp.sum(ds1 * prev1 + ds2 * prev2, axis=0, keepdims=True), axis=1, keepdims=True
            )
            dkeep = jnp.sum(
                jnp.sum(a1 * first_b.astype(F32) + a2 * second_b.astype(F32), axis=0, keepdims=True),
                axis=1,
                keepdims=True,
            )
            dw = jnp.sum(dm * e, axis=1, keepdims=True) * live * (2.0 / (CH * 128))
            dr_row = jnp.where(lanes == 3 * head, jnp.broadcast_to(dw, (CH, 128)), dr_row)
            dr_row = jnp.where(
                lanes == 3 * head + 1, jnp.broadcast_to(deta * (1.0 / CH), (CH, 128)), dr_row
            )
            dr_row = jnp.where(
                lanes == 3 * head + 2, jnp.broadcast_to(dkeep * (-0.5 / CH), (CH, 128)), dr_row
            )
            carry[head] = [new1, new2, eta * ds1, eta * ds2]
        rates = r_s[rows, :]
        dz_s[rows, :] = dr_row * rates * (1.0 - rates)
    for head in range(heads):
        dm1_ref[head] = carry[head][0]
        dm2_ref[head] = carry[head][1]
    for quarter in range(4):
        source = pl.ds(_spot(place, quarter), 128)
        here = slice(quarter * 128, (quarter + 1) * 128)
        dqkv_ref[source, 3 * width :] = dz_s[here, :].astype(BF)
        for head in range(heads):
            at = slice(head * 128, (head + 1) * 128)
            for part, grad_s, norm_s in ((0, dq_s, dqn_s), (1, dk_s, dkn_s)):
                col = slice(part * width + head * 128, part * width + (head + 1) * 128)
                raw = qkv_ref[source, col]
                inverse = _scale_of(raw)
                normed = raw * inverse
                dn = norm_s[here, at]
                inner = jnp.mean(dn * normed, axis=-1, keepdims=True)
                dqkv_ref[source, col] = (
                    grad_s[here, at] + inverse * (dn - normed * inner)
                ).astype(BF)
            col = slice(2 * width + head * 128, 2 * width + (head + 1) * 128)
            dqkv_ref[source, col] = dv_s[here, at].astype(BF)


def _row_scratch(heads):
    wide = heads * 128
    return [
        pltpu.VMEM((512, wide), BF),
        pltpu.VMEM((512, wide), BF),
        pltpu.VMEM((512, wide), BF),
        pltpu.VMEM((512, wide), BF),
        pltpu.VMEM((512, wide), F32),
        pltpu.VMEM((512, wide), BF),
        pltpu.VMEM((512, wide), F32),
        pltpu.VMEM((512, 128), F32),
    ]


_VM = pl.BlockSpec(memory_space=pltpu.VMEM)
_SM = pl.BlockSpec(memory_space=pltpu.SMEM)


def _any(count):
    return [pl.BlockSpec(memory_space=pl.ANY)] * count


def _call(kernel, operands, in_specs, after, **settings):
    count = len(operands)
    more = len(after)

    def body(*refs):
        kernel(*refs[:count], *refs[count + more :])

    held = [pl.BlockSpec(memory_space=pltpu.HBM)] * more
    return pl.pallas_call(body, in_specs=[*in_specs, *held], **settings)(*operands, *after)


def mix_forward(where, quarters, batch, weights, pk, pv, m1, m2, after=()):
    heads = pk.shape[0]
    wide = heads * 128
    blocks = len(weights)
    step = weights[0].shape[0] - 16
    width = blocks * step
    local = quarters[0].shape[2]
    extra, token, mixed, lse, keep, send, first, qkv, reads, states = _call(
        partial(_fwd_kernel, heads, blocks, batch),
        (where, *quarters, pk, pv, m1, m2, *weights),
        [_SM] + _any(4) + [_VM] * 4 + _any(blocks),
        after,
        name="mix_forward",
        out_shape=(
            _f32(16, width),
            _f32(128, width),
            _bf16(512, wide),
            _f32(512, 128),
            _bf16(256, width),
            _bf16(256, width),
            _bf16(512, width),
            _f32(512, 3 * wide + 128),
            _bf16(512, wide),
            _bf16(8, 4, heads, 128, 128),
        ),
        out_specs=(*[_VM] * 6, *_any(4)),
        scratch_shapes=[
            pltpu.VMEM((4, blocks, local, width), BF),
            pltpu.VMEM((512, width), BF),
            pltpu.VMEM((512, 3 * wide + 128), F32),
            pltpu.VMEM((512, wide), BF),
            pltpu.VMEM((8, 4, heads, 128, 128), BF),
            pltpu.VMEM((width, 3 * wide), BF),
            pltpu.VMEM((128, width), BF),
            pltpu.VMEM((width, wide), BF),
            pltpu.SemaphoreType.DMA((3, blocks)),
            pltpu.SemaphoreType.DMA((4,)),
            pltpu.SemaphoreType.DMA((3,)),
            pltpu.SemaphoreType.DMA((8,)),
        ]
        + _row_scratch(heads),
        compiler_params=pltpu.CompilerParams(vmem_limit_bytes=60 * 1024 * 1024),
        cost_estimate=pl.CostEstimate(flops=10**5, bytes_accessed=10**4, transcendentals=0),
    )
    return first, extra, token, qkv, mixed, reads, lse, states, keep, send


def mix_backward(where, cots, saved, weights, after=()):
    pk = saved[1]
    heads = pk.shape[0]
    wide = heads * 128
    blocks = len(weights)
    step = weights[0].shape[0] - 16
    width = blocks * step
    return _call(
        partial(_bwd_kernel, heads, blocks),
        (where, *cots, *saved, *weights),
        [_SM] + _any(5) + [_VM] * 5 + _any(1 + blocks),
        after,
        name="mix_backward",
        out_shape=(
            _bf16(512, 3 * wide + 128),
            _f32(heads, 16, 128),
            _f32(heads, 16, 128),
            _f32(heads, 128, 128),
            _f32(heads, 128, 128),
            _bf16(256, width),
            _bf16(256, width),
        ),
        out_specs=(*_any(1), *[_VM] * 6),
        scratch_shapes=[
            pltpu.VMEM((4, 128, width), BF),
            pltpu.VMEM((512, 3 * wide + 128), F32),
            pltpu.VMEM((8, 4, heads, 128, 128), BF),
            pltpu.VMEM((512, 3 * wide + 128), BF),
            pltpu.VMEM((512, wide), F32),
            pltpu.VMEM((width, 3 * wide), BF),
            pltpu.VMEM((128, width), BF),
            pltpu.VMEM((width, wide), BF),
            pltpu.SemaphoreType.DMA((3, blocks)),
            pltpu.SemaphoreType.DMA((7,)),
        ]
        + _row_scratch(heads)
        + [pltpu.VMEM((512, wide), F32)] * 6
        + [pltpu.VMEM((512, 128), F32)],
        compiler_params=pltpu.CompilerParams(vmem_limit_bytes=60 * 1024 * 1024),
        cost_estimate=pl.CostEstimate(flops=7 * 10**9, bytes_accessed=10**4, transcendentals=0),
    )


def _feed_kernel(blocks, picks, cols, batch, *rest):
    seconds = rest[:4]
    cots = rest[4:8]
    weight_refs = rest[8 : 8 + blocks]
    (
        hidden_ref,
        gate_ref,
        up_ref,
        keep_ref,
        send_ref,
        feed_keep_ref,
        feed_send_ref,
        gate_s,
        up_s,
        down_s,
        sems,
    ) = rest[8 + blocks :]
    step = weight_refs[0].shape[-2]
    copies = [
        _copies(weight_refs, pl.ds(0, step), pl.ds(w * cols, cols), target, sems.at[w], picks)
        for w, target in enumerate((gate_s, up_s, down_s))
    ]
    for part in range(2):
        rows = slice(part * 256, (part + 1) * 256)
        left = jnp.concatenate([seconds[2 * part][...], seconds[2 * part + 1][...]], axis=0)
        cot = jnp.concatenate([cots[2 * part][batch], cots[2 * part + 1][batch]], axis=0)
        if part == 0:
            for copy in copies[0]:
                copy.wait()
        gate = _nn(left, gate_s[...])
        if part == 0:
            for copy in copies[1]:
                copy.wait()
        up = _nn(left, up_s[...])
        if part == 0:
            for copy in copies[2]:
                copy.wait()
        grad = _nn(cot, down_s[...])
        sig = _sig(gate)
        act = gate * sig
        hidden = (act * up).astype(BF)
        gate_grad = (grad * up * (sig + act * (1.0 - sig))).astype(BF)
        up_grad = (grad * act).astype(BF)
        hidden_ref[rows, :] = hidden
        gate_ref[rows, :] = gate_grad
        up_ref[rows, :] = up_grad
        back = _nt(gate_grad, gate_s[...]) + _nt(up_grad, up_s[...])
        feed = _nt(hidden, down_s[...])
        if part == 0:
            keep_ref[...] = back.astype(BF)
            feed_keep_ref[...] = feed.astype(BF)
        else:
            send_ref[...] = back.astype(BF)
            feed_send_ref[...] = feed.astype(BF)


def feed_forward(seconds, cots, batch, weights, after=()):
    blocks = len(weights)
    picks = tuple(pick for _, pick in weights)
    weights = [array for array, _ in weights]
    step = weights[0].shape[-2]
    cols = weights[0].shape[-1] // 3
    width = blocks * step
    return _call(
        partial(_feed_kernel, blocks, picks, cols, batch),
        (*seconds, *cots, *weights),
        [_VM] * 8 + _any(blocks),
        after,
        name="feed_forward",
        out_shape=(
            jax.ShapeDtypeStruct((512, cols), BF),
            jax.ShapeDtypeStruct((512, cols), BF),
            jax.ShapeDtypeStruct((512, cols), BF),
            jax.ShapeDtypeStruct((256, width), BF),
            jax.ShapeDtypeStruct((256, width), BF),
            jax.ShapeDtypeStruct((256, width), BF),
            jax.ShapeDtypeStruct((256, width), BF),
        ),
        out_specs=(_VM,) * 7,
        scratch_shapes=[pltpu.VMEM((width, cols), BF)] * 3
        + [pltpu.SemaphoreType.DMA((3, blocks))],
        compiler_params=pltpu.CompilerParams(vmem_limit_bytes=48 * 1024 * 1024),
        cost_estimate=pl.CostEstimate(flops=35 * 10**8, bytes_accessed=10**4, transcendentals=0),
    )


def _grad_kernel(groups, counts, picks, keep, sends, *rest):
    total = sum(counts)
    row_refs = rest[:total]
    grad_refs = rest[total : total + len(counts)]
    outs = rest[total + len(counts) :]
    keep_refs, send_refs = outs[: len(keep)], outs[len(keep) :]
    targets = [
        (k, ref, place) for ref, some in zip(send_refs, sends) for place, k in enumerate(some)
    ]
    targets += [(k, ref, None) for ref, k in zip(keep_refs, keep)]
    step = outs[0].shape[-2]
    for k, out_ref, place in targets:
        at = slice(k * step, (k + 1) * step)
        start = 0
        index = 0
        term_at = 0
        for terms in groups:
            value = None
            for count, grad_ref in zip(
                counts[term_at : term_at + terms], grad_refs[term_at : term_at + terms]
            ):
                pieces = []
                for i in range(index, index + count):
                    ref, pick = row_refs[i], picks[i]
                    pieces.append(ref[:, at] if pick is None else ref[pick, :, at])
                index += count
                left = pieces[0] if count == 1 else jnp.concatenate(pieces, axis=0)
                term = _tn(left, grad_ref[...])
                value = term if value is None else value + term
            cols = slice(start, start + grad_refs[term_at].shape[1])
            start = cols.stop
            term_at += terms
            if place is None:
                out_ref[:, cols] = value.astype(BF)
            else:
                out_ref[place, :, cols] = value.astype(BF)


def weight_gradient(groups, blocks, keep, sends, flops=None, after=()):
    terms = [term for group in groups for term in group]
    width = terms[0][0][0][0].shape[-1]
    cols = sum(group[0][1].shape[1] for group in groups)
    step = width // blocks
    pieces = [piece for rows, _ in terms for piece in rows]
    grads = [grad for _, grad in terms]
    return _call(
        partial(
            _grad_kernel,
            tuple(len(group) for group in groups),
            tuple(len(rows) for rows, _ in terms),
            tuple(pick for _, pick in pieces),
            tuple(keep),
            tuple(sends),
        ),
        (*[array for array, _ in pieces], *grads),
        [_VM] * (len(pieces) + len(grads)),
        after,
        name="weight_gradient",
        out_shape=(
            *[_bf16(step, cols)] * len(keep),
            *[_bf16(len(some), step, cols) for some in sends],
        ),
        out_specs=(_VM,) * (len(keep) + len(sends)),
        compiler_params=pltpu.CompilerParams(vmem_limit_bytes=48 * 1024 * 1024),
        cost_estimate=pl.CostEstimate(
            flops=flops or 4 * 10**8 * (len(keep) + sum(len(some) for some in sends)),
            bytes_accessed=10**4,
            transcendentals=0,
        ),
    )


def _small(name, function, shapes, scalars, values, after, flops=10**5):
    return _call(
        function,
        (*scalars, *values),
        [_SM] * len(scalars) + [_VM] * len(values),
        after,
        name=name,
        out_shape=shapes,
        out_specs=(_VM,) * len(shapes),
        cost_estimate=pl.CostEstimate(flops=flops, bytes_accessed=10**4, transcendentals=0),
        compiler_params=pltpu.CompilerParams(vmem_limit_bytes=32 * 1024 * 1024),
    )


def _f32(*shape):
    return jax.ShapeDtypeStruct(shape, F32)


def _bf16(*shape):
    return jax.ShapeDtypeStruct(shape, BF)


def _add_kernel(keep_ref, got_ref, own_ref, other_ref):
    total = keep_ref[...].astype(F32) + got_ref[...].astype(F32)
    own_ref[...] = total[0:128, :]
    other_ref[...] = total[128:256, :].astype(BF)


def add_core(keep, got, after=()):
    width = keep.shape[1]
    return _small("add_core", _add_kernel, (_f32(128, width), _bf16(128, width)), (), (keep, got), after)


def _norm_kernel(rows_ref, own_ref, column_ref, gain_ref, second_ref, residual_ref, inverse_ref):
    residual = rows_ref[...] + own_ref[...] + column_ref[...].astype(F32)
    inverse = _scale_of(residual)
    second_ref[...] = (residual * inverse * gain_ref[...]).astype(BF)
    residual_ref[...] = residual
    inverse_ref[...] = jnp.broadcast_to(inverse, (128, 128))


def second_norm(rows, own, column, gain, after=()):
    width = rows.shape[1]
    return _small(
        "second_norm",
        _norm_kernel,
        (_bf16(128, width), _f32(128, width), _f32(128, 128)),
        (),
        (rows, own, column, gain),
        after,
    )


def _norm_grad(grad, normed, inverse, gain):
    scaled = grad * gain
    return inverse * (scaled - normed * jnp.mean(scaled * normed, axis=-1, keepdims=True))


def _second_back_kernel(batch, own_ref, column_ref, cot_ref, residual_ref, inverse_ref, gain_ref, low_ref, out_ref, sum_ref):
    grad = own_ref[...] + column_ref[...].astype(F32)
    inverse = inverse_ref[:, 0:1]
    normed = residual_ref[...] * inverse
    out = cot_ref[batch] + _norm_grad(grad, normed, inverse, gain_ref[...])
    low_ref[...] = out.astype(BF)
    out_ref[...] = out
    sum_ref[...] = jnp.sum(grad * normed, axis=0, keepdims=True)


def second_back(batch, own, column, cots, residual, inverse, gain, after=()):
    width = own.shape[1]
    return _small(
        "second_back",
        partial(_second_back_kernel, batch),
        (_bf16(128, width), _f32(128, width), _f32(1, width)),
        (),
        (own, column, cots, residual, inverse, gain),
        after,
        3 * 10**9,
    )


def _place(where_ref, k, step):
    return pl.ds(pl.multiple_of(where_ref[2 + k] * step, step), step)


def _live(where_ref):
    return (where_ref[0] * 128 + _lane((128, 1), 0) < where_ref[1]).astype(F32)


def _cots_kernel(blocks, where_a, where_b, scale_ref, got_ref, rows_ref, low_ref):
    width = got_ref.shape[3]
    step = width // blocks
    for b, where_ref in enumerate((where_a, where_b)):
        factor = _live(where_ref) * scale_ref[b]
        for k in range(blocks):
            piece = got_ref[:, b, :, _place(where_ref, k, step)].reshape(128, step).astype(F32)
            piece = piece * factor
            rows_ref[b, :, k * step : (k + 1) * step] = piece
            low_ref[b, :, k * step : (k + 1) * step] = piece.astype(BF)


def take_cots(wheres, scales, got, after=()):
    blocks, batches, _, width = got.shape
    return _small(
        "take_cots",
        partial(_cots_kernel, blocks),
        (_f32(batches, 128, width), _bf16(batches, 128, width)),
        (*wheres, scales),
        (got,),
        after,
    )


def _finish_kernel(blocks, where_a, where_b, own_a, own_b, column_ref, res_a, res_b, out_ref):
    width = column_ref.shape[2]
    step = width // blocks
    for b, (where_ref, own, res) in enumerate(((where_a, own_a, res_a), (where_b, own_b, res_b))):
        rows = _live(where_ref) * (res[...] + own[...] + column_ref[b].astype(F32))
        rows = rows.astype(BF)
        for k in range(blocks):
            piece = rows[:, k * step : (k + 1) * step].reshape(blocks, 128 // blocks, step)
            out_ref[:, b, :, _place(where_ref, k, step)] = piece


def finish_rows(blocks, wheres, owns, column, residuals, after=()):
    width = column.shape[2]
    return _small(
        "finish_rows",
        partial(_finish_kernel, blocks),
        (_bf16(blocks, 2, 128 // blocks, width),),
        wheres,
        (*owns, column, *residuals),
        after,
    )[0]


def _token_grad(own_ref, column_ref, rows_ref, back_ref, gain_ref):
    grad = own_ref[...] + column_ref[...].astype(F32)
    rows = rows_ref[...]
    inverse = _scale_of(rows)
    normed = rows * inverse
    out = back_ref[...] + _norm_grad(grad, normed, inverse, gain_ref[...])
    return out.astype(BF), jnp.sum(grad * normed, axis=0, keepdims=True)


def _first_back_kernel(own_ref, column_ref, rows_ref, back_ref, gain_ref, low_ref, sum_ref):
    low_ref[...], sum_ref[...] = _token_grad(own_ref, column_ref, rows_ref, back_ref, gain_ref)


def first_back(own, column, rows, back, gain, after=()):
    width = own.shape[1]
    return _small(
        "first_back",
        _first_back_kernel,
        (_bf16(128, width), _f32(1, width)),
        (),
        (own, column, rows, back, gain),
        after,
    )


def _last_kernel(blocks, where_ref, own_ref, column_ref, rows_ref, back_ref, gain_ref, low_ref, sum_a, two_a, two_b, out_ref, gains_ref):
    width = own_ref.shape[1]
    step = width // blocks
    low, total = _token_grad(own_ref, column_ref, rows_ref, back_ref, gain_ref)
    total = total + sum_a[...]
    two = two_a[...] + two_b[...]
    first = low_ref[...]
    gains_ref[...] = jnp.zeros((8, width), F32)
    for k in range(blocks):
        at = slice(k * step, (k + 1) * step)
        place = _place(where_ref, k, step)
        out_ref[:, 0, :, place] = first[:, at].reshape(blocks, 128 // blocks, step)
        out_ref[:, 1, :, place] = low[:, at].reshape(blocks, 128 // blocks, step)
        gains_ref[0:1, place] = total[:, at]
        gains_ref[1:2, place] = two[:, at]


def last_rows(blocks, where, own, column, rows, back, gain, low, sum_a, two_a, two_b, after=()):
    width = own.shape[1]
    return _small(
        "last_rows",
        partial(_last_kernel, blocks),
        (_bf16(blocks, 2, 128 // blocks, width), _f32(8, width)),
        (where,),
        (own, column, rows, back, gain, low, sum_a, two_a, two_b),
        after,
    )


def _ring_kernel(indices, passing, splits, *rest):
    count = len(indices)
    keeps, gots = rest[:count], rest[count : 2 * count]
    passed_ref = rest[2 * count] if passing else None
    outs = rest[2 * count + passing :]
    start = 0
    done = 0
    for keep, got, index, sizes in zip(keeps, gots, indices, splits):
        cols = keep.shape[1]
        total = keep[...].astype(F32) + got[index].astype(F32)
        if passing:
            total = total + passed_ref[:, start : start + cols].astype(F32)
        if sizes is None:
            outs[0][:, start : start + cols] = total.astype(BF)
        else:
            for offset, size, turned in sizes:
                piece = total[:, offset : offset + -(-size // 128) * 128]
                if turned:
                    outs[done][...] = piece.T[:size]
                else:
                    outs[done][...] = piece[:, :size]
                done += 1
        start += cols


def ring_step(keeps, gots, indices, passed, splits=None, after=()):
    step = keeps[0].shape[0]
    cols = sum(k.shape[1] for k in keeps)
    if splits is None:
        shapes = (_bf16(step, cols),)
        splits = (None,) * len(keeps)
    else:
        shapes = tuple(
            _f32(size, step) if turned else _f32(step, size)
            for sizes in splits
            for _, size, turned in sizes
        )
    return _small(
        "ring_step",
        partial(_ring_kernel, tuple(indices), len(passed), tuple(splits)),
        shapes,
        (),
        (*keeps, *gots, *passed),
        after,
    )


def _hop_kernel(value_ref, got_ref, out_ref):
    out_ref[...] = value_ref[...] + got_ref[...].astype(F32)


def add_hop(value, got, after=()):
    return _small("add_hop", _hop_kernel, (_f32(*value.shape),), (), (value, got), after)[0]


def _join_kernel(*refs):
    *grads, out_ref = refs
    count = len(grads) // 2
    start = 0
    for one, two in zip(grads[:count], grads[count:]):
        for head in range(one.shape[0]):
            rows = one.shape[1]
            out_ref[start : start + rows, :] = one[head] + two[head]
            start += rows


def join_sums(one, two, after=()):
    rows = sum(g.shape[0] * g.shape[1] for g in one)
    return _small("join_sums", _join_kernel, (_f32(rows, 128),), (), (*one, *two), after)[0]


def _tick_kernel(out_ref):
    out_ref[...] = jnp.zeros((8, 128), F32)


def tick(after=()):
    return _small("tick", _tick_kernel, (_f32(8, 128),), (), (), after, 4 * 10**9)[0]


DP = ("z", "x")


def _swap(value, axis):
    return lax.ppermute(value, axis, [(0, 1), (1, 0)])


BLOCKS = 8
STEP = 128
DOWN = (1, 2, 3, 0)
RING = [(0, 1), (1, 2), (2, 3), (3, 0)]


def _ring_sized():
    return lax.axis_size("z") == 4


def _block_ids():
    if not _ring_sized():
        return jnp.arange(BLOCKS, dtype=jnp.int32)
    z = lax.axis_index("z")
    x = lax.axis_index("x")
    zs = jnp.stack([(z + 4 - i) % 4 for i in DOWN])
    return jnp.concatenate([2 * zs + x, 2 * zs + (1 - x)]).astype(jnp.int32)


class _Order:
    def __init__(self):
        self.last = []

    def __call__(self, function, *values, need=()):
        result = function(*values, after=(*self.last, *need))
        self.last = [min(jax.tree.leaves(result), key=lambda leaf: leaf.size)]
        return result


def _ring(block):
    return lax.ppermute(block, "z", RING)


def _in_order(ring, across):
    return [ring[i] for i in DOWN] + [across[i] for i in DOWN]


def _scatter_whole(keep, *sends):
    whole = jnp.concatenate([keep, *sends]).reshape(BLOCKS * STEP, -1)
    return lax.psum_scatter(whole, DP, scatter_dimension=0, tiled=True).astype(F32)


def _quarters(own):
    column = _swap(own, "y")
    return [own, column, _swap(own, "c"), _swap(column, "c")]


def per_device(
    tokens,
    grad_output,
    query_weight,
    key_weight,
    value_weight,
    rates_weight,
    out_weight,
    gate_weight,
    up_weight,
    down_weight,
    norm1_gain,
    norm2_gain,
    persist_key,
    persist_value,
    memory_first,
    memory_second,
    seq_lengths,
    deal,
):
    devices = lax.axis_size("z") * lax.axis_size("x")
    dp_index = lax.axis_index("z") * lax.axis_size("x") + lax.axis_index("x")
    place = lax.axis_index("y") * 2 + lax.axis_index("c")
    seq_count = seq_lengths.shape[0]
    batches = seq_count // devices
    local_rows = tokens.shape[2]
    width = tokens.shape[3]
    quarter = local_rows * devices
    rows_of = query_weight.shape[0]
    head_cols = query_weight.shape[1]
    rate_cols = rates_weight.shape[1]
    hidden_cols = gate_weight.shape[1]

    batch_of = deal // devices
    batch_ids = jnp.arange(batches, dtype=jnp.int32)
    batch_tokens = jnp.sum(
        jnp.where(batch_of[None, :] == batch_ids[:, None], seq_lengths[None, :], 0), axis=1
    ).astype(F32)
    batch_scale = jnp.sum(seq_lengths).astype(F32) / (batches * batch_tokens)
    span = range(batches)
    my_seqs = [batches * dp_index + b for b in span]
    lengths = [seq_lengths[s] for s in my_seqs]
    scales = [batch_scale[batch_of[s]] for s in my_seqs]
    ring_sized = _ring_sized()
    ids = _block_ids()
    where = [
        jnp.concatenate([jnp.stack([place, lengths[b]]).astype(jnp.int32), ids]) for b in span
    ]
    scale = jnp.stack(scales)

    def deal_in(array):
        part = array.reshape(devices, batches, local_rows, width)
        part = lax.all_to_all(part, DP, split_axis=0, concat_axis=0, tiled=True)
        if local_rows * BLOCKS == quarter:
            return part
        part = part.transpose(1, 0, 2, 3).reshape(batches, BLOCKS, quarter // BLOCKS, width)
        return part.transpose(1, 0, 2, 3)

    def deal_out(part):
        if local_rows * BLOCKS != quarter:
            part = part.transpose(1, 0, 2, 3).reshape(batches, devices, local_rows, width)
            part = part.transpose(1, 0, 2, 3)
        part = lax.all_to_all(part, DP, split_axis=0, concat_axis=0, tiled=True)
        return part.reshape(seq_count, 1, local_rows, width)

    mix_shard = jnp.concatenate([query_weight, key_weight, value_weight, out_weight], axis=1)
    extra = jnp.concatenate(
        [
            rates_weight.T,
            norm1_gain[None],
            norm2_gain[None],
            jnp.zeros((16 - rate_cols - 2, rows_of), BF),
        ]
    )
    pad = -hidden_cols % 128
    feed_shard = jnp.concatenate(
        [jnp.pad(w, ((0, 0), (0, pad))) for w in (gate_weight, up_weight, down_weight)], axis=1
    )
    got_tokens = deal_in(tokens)

    run = _Order()

    def mix_of(b, wheres, need=()):
        return run(
            mix_forward,
            wheres[b],
            quarters,
            b,
            mix_weights,
            persist_key,
            persist_value,
            memory_first,
            memory_second,
            need=need,
        )

    if ring_sized:
        extra = jnp.pad(extra, ((0, 0), (0, mix_shard.shape[1] - rows_of)))
        mix0 = jnp.concatenate([mix_shard, extra], axis=0)
        mix1 = _ring(mix0)
        mix_across0 = _swap(mix0, "x")
        mix1, mix_across0, feed0, scale, *where = lax.optimization_barrier(
            (mix1, mix_across0, feed_shard, scale, *where)
        )
        mix2 = _ring(mix1)
        mix_across1 = _swap(mix1, "x")
        mix2, mix_across1 = lax.optimization_barrier((mix2, mix_across1))
        mix3 = _ring(mix2)
        mix_across2 = _swap(mix2, "x")
        quarters = _quarters(got_tokens)
        mix3, mix_across2, feed0, cots_in = lax.optimization_barrier(
            (mix3, mix_across2, feed0, grad_output)
        )
        got_cots = deal_in(cots_in)
        mix_across3 = _swap(mix3, "x")
        feed1 = _ring(feed0)
        feed0, feed1, mix_across3 = lax.optimization_barrier((feed0, feed1, mix_across3))
        feed2 = _ring(feed1)
        feed_across01 = _swap(jnp.stack([feed0, feed1]), "x")
        mix_weights = _in_order(
            [mix0, mix1, mix2, mix3], [mix_across0, mix_across1, mix_across2, mix_across3]
        )
    else:
        mix_full = lax.all_gather(mix_shard, DP, axis=0, tiled=True)
        extra = lax.all_gather(extra, DP, axis=1, tiled=True)
        extra = jnp.pad(
            extra.reshape(16, BLOCKS, STEP), ((0, 0), (0, 0), (0, mix_shard.shape[1] - STEP))
        )
        mix_weights = [
            jnp.concatenate([mix_full[k * STEP : (k + 1) * STEP], extra[:, k]])
            for k in range(BLOCKS)
        ]
        feed_full = lax.all_gather(feed_shard, DP, axis=0, tiled=True)
        feed_weights = [(feed_full[k * STEP : (k + 1) * STEP], None) for k in range(BLOCKS)]
        quarters = _quarters(got_tokens)
        got_cots = deal_in(grad_output)

    mix_a = mix_of(0, where, [feed1] if ring_sized else [])
    gain_one = mix_a[1][rate_cols : rate_cols + 1]
    gain_two = mix_a[1][rate_cols + 1 : rate_cols + 2]
    core_a = _swap(mix_a[9], "c")
    early = []
    run(tick, need=[feed2] if ring_sized else [])
    cot_rows, cot_own = run(take_cots, where, scale, got_cots)
    if ring_sized:
        feed3 = _ring(feed2)
        feed_across2 = _swap(feed2, "x")
        early = [feed3, feed_across01, feed_across2]
    own_a, other_a = run(add_core, mix_a[8], core_a)
    column_a = _swap(other_a, "y")
    cot_column = _swap(cot_own, "y")
    cot_core = _swap(cot_own, "c")
    mix_b = mix_of(1, where)
    mixes = [mix_a, mix_b]
    core_b = _swap(mix_b[9], "c")
    token_rows = [m[2] for m in mixes]
    run(tick, need=[*early, column_a, cot_column])
    second_a, residual_a, inverse_a = run(second_norm, token_rows[0], own_a, column_a, gain_two)
    early = []
    if ring_sized:
        feed_across3 = _swap(feed3, "x")
        feed_weights = _in_order(
            [(feed0, None), (feed1, None), (feed2, None), (feed3, None)],
            [(feed_across01, 0), (feed_across01, 1), (feed_across2, None), (feed_across3, None)],
        )
    second_a = _quarters(second_a)
    own_b, other_b = run(add_core, mix_b[8], core_b, need=[second_a[2]])
    column_b = _swap(other_b, "y")
    cots = [cot_own, cot_column, cot_core, _swap(cot_column, "c")]
    second_b, residual_b, inverse_b = run(
        second_norm, token_rows[1], own_b, column_b, gain_two, need=[*early, cots[3]]
    )
    second_b = _quarters(second_b)
    second = [second_a, second_b]
    residual = [residual_a, residual_b]

    def feed_of(b, need=()):
        return run(feed_forward, second[b], cots, b, feed_weights, need=need)

    feed_a = feed_of(0)
    core_a = _swap(feed_a[4], "c")
    run(tick, need=second_b[1:2])
    own_a, other_a = run(add_core, feed_a[3], core_a)
    column_a = _swap(other_a, "y")
    feed_b = feed_of(1)
    feeds = [feed_a, feed_b]
    core_b = _swap(feed_b[4], "c")
    def plain(pieces):
        return [(piece, None) for piece in pieces]

    def across(part):
        return _swap(part, "x") if ring_sized else part

    feed_groups = [
        [(plain(second[b]), feeds[b][1]) for b in span],
        [(plain(second[b]), feeds[b][2]) for b in span],
        [([(piece, b) for piece in cots], feeds[b][0]) for b in span],
    ]
    class Sum:
        def __init__(self, keeps, gots, splits):
            self.keeps = keeps
            self.gots = gots
            self.splits = splits
            self.place = 0
            self.passed = []
            self.results = None

        def step(self, need=()):
            place = self.place
            self.place += 1
            final = place == 3
            if not ring_sized:
                if final:
                    self.results = [
                        whole[:, at : at + size].T if turned else whole[:, at : at + size]
                        for keep, got, sizes in zip(self.keeps, self.gots, self.splits)
                        for whole in [_scatter_whole(jnp.stack(keep), *got)]
                        for at, size, turned in sizes
                    ]
                return
            keeps = [keep[place] for keep in self.keeps]
            pieces = [
                [(part, i) for part in got for i in range(part.shape[0])][place]
                for got in self.gots
            ]
            gots = [part for part, _ in pieces]
            indices = [i for _, i in pieces]
            results = run(
                ring_step, keeps, gots, indices, self.passed, self.splits if final else None, need=need
            )
            if final:
                self.results = results
            else:
                self.passed = [_ring(results[0])]

    class AllSum:
        def __init__(self, value, axes, sent):
            self.value = value
            self.sent = sent
            self.hops = []
            for axis in axes:
                size = lax.axis_size(axis)
                step = 1
                while step < size:
                    self.hops.append((axis, [(i, i ^ step) for i in range(size)]))
                    step *= 2
            self.start()

        def start(self):
            if self.hops:
                axis, pairs = self.hops.pop(0)
                self.got = lax.ppermute(self.value.astype(self.sent), axis, pairs)

        def step(self, need=()):
            self.value = run(add_hop, self.value, self.got, need=need)
            self.got = None
            self.start()

        def rest(self):
            while self.got is not None:
                self.step()
            return self.value

    first_sends = run(
        weight_gradient, feed_groups, BLOCKS, (), ((4,),), 4 * 10**9, need=[column_a]
    )
    feed_got = [across(first_sends[0])]
    mixer_a, back_a, two_a = run(
        second_back, 0, own_a, column_a, cot_rows, residual_a, inverse_a, gain_two
    )
    mixer_column = _swap(mixer_a, "y")
    mixer_core = _swap(mixer_a, "c")
    own_b, other_b = run(add_core, feed_b[3], core_b)
    column_b = _swap(other_b, "y")
    feed_core = [_swap(f[6], "c") for f in feeds]
    feed_own, feed_other = zip(
        *[run(add_core, feeds[b][5], feed_core[b], need=[mixer_core]) for b in span],
        strict=True,
    )
    feed_parts = run(weight_gradient, feed_groups, BLOCKS, range(4), ((5,), (6, 7)))
    feed_got.append(across(feed_parts[4]))
    feed_keep = feed_parts[:4]
    mixer_column, *feed_keep = lax.optimization_barrier((mixer_column, *feed_keep))
    mixer_a = [mixer_a, mixer_column, mixer_core, _swap(mixer_column, "c")]
    mixer_b, back_b, two_b = run(
        second_back, 1, own_b, column_b, cot_rows, residual_b, inverse_b, gain_two
    )
    mixer_b_column = _swap(mixer_b, "y")
    mixer_b_core = _swap(mixer_b, "c")
    feed_column = _swap(jnp.stack(feed_other), "y")
    stride = feed_keep[0].shape[1] // 3
    feed_sum = Sum(
        [feed_keep],
        [feed_got],
        [[(i * stride, hidden_cols, True) for i in range(3)]],
    )
    feed_sum.step()

    def mix_back_of(b, cots, need=()):
        saved = (mixes[b][3], persist_key, persist_value, *mixes[b][4:8])
        return run(mix_backward, where[b], cots, saved, mix_weights, need=need)

    mix_back_a = mix_back_of(0, mixer_a, need=[mixer_b_core])
    core_a = _swap(mix_back_a[6], "c")
    run(tick, need=[*feed_sum.passed, mixer_b_column, feed_column])
    mixer_b_column, last_part, *mix_back_a = lax.optimization_barrier(
        (mixer_b_column, feed_parts[5], *mix_back_a)
    )
    feed_got.append(across(last_part))
    mixer_b = [mixer_b, mixer_b_column, mixer_b_core, _swap(mixer_b_column, "c")]
    feed_sum.step()
    layer_out = deal_out(run(finish_rows, BLOCKS, where, feed_own, feed_column, residual))
    own_a, other_a = run(add_core, mix_back_a[5], core_a)
    column_a = _swap(other_a, "y")
    mix_back_b = mix_back_of(1, mixer_b)
    backs = [mix_back_a, mix_back_b]
    core_b = _swap(mix_back_b[6], "c")
    run(tick, need=[column_a, *feed_sum.passed, feed_got[-1], layer_out])
    project_groups = [
        [(plain([m[0]]), k[0]) for m, k in zip(mixes, backs)],
        [(plain(mixer), m[4]) for mixer, m in ((mixer_a, mix_a), (mixer_b, mix_b))],
    ]
    first_sends = run(weight_gradient, project_groups, BLOCKS, (), ((4,),))
    project_got = [across(first_sends[0])]
    feed_sum.step()
    own_b, other_b = run(add_core, mix_back_b[5], core_b)
    column_b = _swap(other_b, "y")
    memory_sum = AllSum(
        run(join_sums, mix_back_a[1:5], mix_back_b[1:5]), DP[::-1], BF
    )
    project_parts = run(weight_gradient, project_groups, BLOCKS, range(4), ((5,), (6, 7)))
    project_keep = project_parts[:4]
    if ring_sized:
        project_got[0], *late = lax.optimization_barrier((project_got[0], *project_parts[4:]))
    else:
        late = project_parts[4:]
    project_got += [across(part) for part in late]
    rates_at = 3 * head_cols
    project_sum = Sum(
        [project_keep],
        [project_got],
        [
            [(i * head_cols, head_cols, False) for i in range(3)]
            + [(rates_at, rate_cols, False), (rates_at + 128, head_cols, False)]
        ],
    )
    project_sum.step()
    memory_sum.step()
    token_a, one_a = run(first_back, own_a, column_a, token_rows[0], back_a, gain_one)
    token_send, gains = run(
        last_rows,
        BLOCKS,
        where[1],
        own_b,
        column_b,
        token_rows[1],
        back_b,
        gain_one,
        token_a,
        one_a,
        two_a,
        two_b,
    )
    grad_tokens = deal_out(token_send)
    gain_sum = AllSum(gains, ("c", "y", "x", "z"), F32)
    gain_sum.step()
    project_sum.step()
    feed_sum.step()
    gain_sum.step()
    memory_sum.step()
    gain_sum.step()
    project_sum.step()
    gain_sum.step()
    flat = memory_sum.rest()
    gains = gain_sum.rest()
    project_sum.step()
    gate_total, up_total, down_total = feed_sum.results
    *project_totals, out_total = project_sum.results

    memory_out = []
    start = 0
    for m in mix_back_a[1:5]:
        size = m.size // 128
        memory_out.append(flat[start : start + size].reshape(m.shape))
        start += size

    return (
        layer_out,
        grad_tokens,
        *project_totals,
        out_total,
        gate_total.T,
        up_total.T,
        down_total.T,
        gains[0],
        gains[1],
        memory_out[0],
        memory_out[1],
        memory_out[2],
        memory_out[3],
    )


def solution(mesh):
    sizes = mesh.devices.shape
    fine = Mesh(mesh.devices.reshape(sizes[0] // 2, 2, 2, sizes[1] // 2), ("z", "x", "y", "c"))
    tensor = ("y", "c")
    return jax.shard_map(
        per_device,
        mesh=fine,
        in_specs=(
            P(None, tensor, DP, None),
            P(None, tensor, DP, None),
            P(DP, tensor),
            P(DP, tensor),
            P(DP, tensor),
            P(DP, tensor),
            P(DP, tensor),
            P(DP, tensor),
            P(DP, tensor),
            P(DP, tensor),
            P(DP),
            P(DP),
            P(tensor, None, None),
            P(tensor, None, None),
            P(tensor, None, None),
            P(tensor, None, None),
            P(),
            P(),
        ),
        out_specs=(
            P(None, tensor, DP, None),
            P(None, tensor, DP, None),
            P(DP, tensor),
            P(DP, tensor),
            P(DP, tensor),
            P(DP, tensor),
            P(DP, tensor),
            P(DP, tensor),
            P(DP, tensor),
            P(DP, tensor),
            P(),
            P(),
            P(tensor, None, None),
            P(tensor, None, None),
            P(tensor, None, None),
            P(tensor, None, None),
        ),
        check_vma=False,
    )
```

```python
from functools import partial

import jax
import jax.numpy as jnp
from jax import lax
from jax.experimental import pallas as pl
from jax.experimental.pallas import tpu as pltpu
from jax.sharding import Mesh
from jax.sharding import PartitionSpec as P

CH = 64
WINDOW = 256
EPS = 1e-06
NEG = -1e30
BF = jnp.bfloat16
F32 = jnp.float32


def _nn(a, b):
    return lax.dot_general(a, b, (((1,), (0,)), ((), ())), preferred_element_type=F32)


def _nt(a, b):
    return lax.dot_general(a, b, (((1,), (1,)), ((), ())), preferred_element_type=F32)


def _tn(a, b):
    return lax.dot_general(a, b, (((0,), (0,)), ((), ())), preferred_element_type=F32)


def _sig(v):
    return 1.0 / (1.0 + jnp.exp(-v))


def _scale_of(v):
    return lax.rsqrt(jnp.mean(v * v, axis=-1, keepdims=True) + EPS)


def _lane(shape, dim):
    return lax.broadcasted_iota(jnp.int32, shape, dim)


def _masks():
    rows = _lane((128, 128), 0)
    cols = _lane((128, 128), 1)
    return cols > rows, cols <= rows, (rows // CH) == (cols // CH)


def _scores(qs, near_keys, read_b, pkey, block, length, masks):
    older, newer, same_span = masks
    read_ok = same_span & (block * 128 + _lane((128, 128), 1) < length)
    parts = [_nt(qs, pkey), jnp.where(read_ok, _nt(qs, read_b), NEG)]
    for back, keys in near_keys:
        part = _nt(qs, keys)
        if back == 2:
            part = jnp.where(older, part, NEG)
        elif back == 0:
            part = jnp.where(newer, part, NEG)
        parts.append(part)
    return parts


def _spot(place, quarter):
    there = place ^ quarter
    return pl.multiple_of((((there & 1) << 1) | (there >> 1)) * 128, 128)


def _load_rows(place, length, qkv_ref, heads, qn_s, kn_s, qs_s, kb_s, v_s, vb_s, w_s, r_s):
    width = heads * 128
    for quarter in range(4):
        source = pl.ds(_spot(place, quarter), 128)
        here = pl.ds(quarter * 128, 128)
        live = (quarter * 128 + _lane((128, 1), 0) < length).astype(F32)
        rates = _sig(qkv_ref[source, 3 * width : 3 * width + 128])
        r_s[here, :] = rates
        for head in range(heads):
            at = slice(head * 128, (head + 1) * 128)
            q = qkv_ref[source, head * 128 : (head + 1) * 128]
            k = qkv_ref[source, width + head * 128 : width + (head + 1) * 128]
            v = qkv_ref[source, 2 * width + head * 128 : 2 * width + (head + 1) * 128]
            qn_s[here, at] = (q * _scale_of(q)).astype(BF)
            kn_s[here, at] = (k * _scale_of(k)).astype(BF)
            qs_s[here, at] = (q * (128 ** (-0.5))).astype(BF)
            kb_s[here, at] = k.astype(BF)
            v_s[here, at] = v
            vb_s[here, at] = v.astype(BF)
            weighting = rates[:, 3 * head : 3 * head + 1] * live * (2.0 / (CH * 128))
            w_s[here, at] = jnp.broadcast_to(weighting, (128, 128))


def _block(block, pick, rows, cols):
    return block.at[rows, cols] if pick is None else block.at[pick, rows, cols]


def _copies(blocks, rows, cols, target, sems, picks=None):
    made = []
    for k, block in enumerate(blocks):
        copy = pltpu.make_async_copy(
            _block(block, picks[k] if picks else None, rows, cols),
            target.at[pl.ds(k * rows.size, rows.size), :],
            sems.at[k],
        )
        copy.start()
        made.append(copy)
    return made


def _fwd_kernel(
    heads,
    blocks,
    batch,
    where_ref,
    own_ref,
    ypart_ref,
    cpart_ref,
    far_ref,
    pk_ref,
    pv_ref,
    m1_ref,
    m2_ref,
    *rest,
):
    weight_refs = rest[:blocks]
    extra_ref, token_ref, mixed_ref, lse_ref, keep_ref, send_ref = rest[blocks : blocks + 6]
    first_hbm, qkv_hbm, reads_hbm, states_hbm = rest[blocks + 6 : blocks + 10]
    (
        pieces_s,
        first_s,
        qkv_s,
        reads_s,
        states_s,
        project_s,
        rates_s,
        out_s,
        sems,
        piece_sems,
        out_sems,
        state_sems,
    ) = rest[blocks + 10 : blocks + 22]
    scratch = rest[blocks + 22 :]
    step = weight_refs[0].shape[0] - 16
    wide = heads * 128
    every = pl.ds(0, step)
    piece_copies = []
    for quarter, ref in enumerate((own_ref, ypart_ref, cpart_ref, far_ref)):
        copy = pltpu.make_async_copy(
            ref.at[:, batch], pieces_s.at[quarter], piece_sems.at[quarter]
        )
        copy.start()
        piece_copies.append(copy)
    rates_s[16:128, :] = jnp.zeros((112, rates_s.shape[1]), BF)
    extra = []
    for k, block in enumerate(weight_refs):
        copy = pltpu.make_async_copy(
            block.at[pl.ds(step, 16), pl.ds(0, step)],
            rates_s.at[pl.ds(0, 16), pl.ds(k * step, step)],
            sems.at[2, k],
        )
        copy.start()
        extra.append(copy)
    project_copies = _copies(weight_refs, every, pl.ds(0, 3 * wide), project_s, sems.at[0])
    out_copies = _copies(weight_refs, every, pl.ds(3 * wide, wide), out_s, sems.at[1])
    for copy in extra:
        copy.wait()
    extra_rows = rates_s[0:16, :].astype(F32)
    extra_ref[...] = extra_rows
    gain = extra_rows[3 * heads : 3 * heads + 1, :]
    width = blocks * step
    for quarter in range(4):
        piece_copies[quarter].wait()
        raw = pieces_s[quarter].reshape(128, width).astype(F32)
        inverse = _scale_of(raw)
        for k in range(blocks):
            source = pl.ds(pl.multiple_of(where_ref[2 + k] * step, step), step)
            piece = pieces_s[quarter, :, :, source].reshape(128, step).astype(F32)
            at = slice(k * step, (k + 1) * step)
            if quarter == 0:
                token_ref[:, at] = piece
            first_s[quarter * 128 : (quarter + 1) * 128, at] = (
                piece * inverse * gain[:, at]
            ).astype(BF)
    outgoing = [pltpu.make_async_copy(first_s, first_hbm, out_sems.at[0])]
    outgoing[0].start()
    for copy in project_copies:
        copy.wait()
    for quarter in range(4):
        rows = slice(quarter * 128, (quarter + 1) * 128)
        left = first_s[rows, :]
        qkv_s[rows, : 3 * wide] = _nn(left, project_s[...])
        qkv_s[rows, 3 * wide :] = _nt(left, rates_s[...])
    outgoing.append(pltpu.make_async_copy(qkv_s, qkv_hbm, out_sems.at[1]))
    outgoing[1].start()

    def send_state(span):
        copy = pltpu.make_async_copy(
            states_s.at[span], states_hbm.at[span], state_sems.at[span]
        )
        copy.start()
        outgoing.append(copy)

    def send_reads():
        copy = pltpu.make_async_copy(reads_s, reads_hbm, out_sems.at[2])
        copy.start()
        outgoing.append(copy)

    _mix_forward(
        heads,
        send_state,
        send_reads,
        where_ref,
        qkv_s,
        pk_ref,
        pv_ref,
        m1_ref,
        m2_ref,
        mixed_ref,
        reads_s,
        lse_ref,
        states_s,
        *scratch,
    )
    for copy in out_copies:
        copy.wait()
    send_ref[...] = _nt(mixed_ref[256:512, :], out_s[...]).astype(BF)
    keep_ref[...] = _nt(mixed_ref[0:256, :], out_s[...]).astype(BF)
    for copy in outgoing:
        copy.wait()


def _mix_forward(
    heads,
    send_state,
    send_reads,
    where_ref,
    qkv_ref,
    pk_ref,
    pv_ref,
    m1_ref,
    m2_ref,
    mixed_ref,
    reads_ref,
    lse_ref,
    states_ref,
    qn_s,
    kn_s,
    qs_s,
    kb_s,
    v_s,
    vb_s,
    w_s,
    r_s,
):
    place = where_ref[0]
    length = where_ref[1]
    _load_rows(place, length, qkv_ref, heads, qn_s, kn_s, qs_s, kb_s, v_s, vb_s, w_s, r_s)
    carry = [
        [m1_ref[h], m2_ref[h], jnp.zeros((128, 128), F32), jnp.zeros((128, 128), F32)]
        for h in range(heads)
    ]
    for span in range(8):
        rows = slice(span * CH, (span + 1) * CH)
        means = jnp.mean(r_s[rows, :], axis=0, keepdims=True)
        for head in range(heads):
            at = slice(head * 128, (head + 1) * 128)
            first, second, s1, s2 = carry[head]
            first_b, second_b = first.astype(BF), second.astype(BF)
            states_ref[span, 0, head] = first_b
            states_ref[span, 1, head] = second_b
            states_ref[span, 2, head] = s1.astype(BF)
            states_ref[span, 3, head] = s2.astype(BF)
            kn = kn_s[rows, at]
            qn = qn_s[rows, at]
            both = _nn(jnp.concatenate([kn, qn], axis=0), first_b)
            both = both * _sig(both) if span == 7 else both
            if span < 7:
                pre = both[:CH]
                sig = _sig(both)
                act_both = both * sig
                sig_k = sig[:CH]
            else:
                act_both = both
            out_both = _nn(act_both.astype(BF), second_b)
            reads_ref[rows, at] = out_both[CH:].astype(BF)
            if span < 7:
                act = act_both[:CH]
                miss = (out_both[:CH] - v_s[rows, at]) * w_s[rows, at]
                miss_b = miss.astype(BF)
                grad_second = _tn(act.astype(BF), miss_b)
                grad_pre = _nt(miss_b, second_b) * sig_k * (1.0 + pre * (1.0 - sig_k))
                grad_first = _tn(kn, grad_pre.astype(BF))
                eta = means[:, 3 * head + 1 : 3 * head + 2]
                keep = 1.0 - 0.5 * means[:, 3 * head + 2 : 3 * head + 3]
                s1 = eta * s1 - grad_first
                s2 = eta * s2 - grad_second
                carry[head] = [keep * first + s1, keep * second + s2, s1, s2]
        send_state(span)
    send_reads()
    masks = _masks()
    for block in range(4):
        rows = slice(block * 128, (block + 1) * 128)
        target = pl.ds(_spot(place, block), 128)
        lse_all = jnp.zeros((128, 128), F32)
        for head in range(heads):
            at = slice(head * 128, (head + 1) * 128)
            qs = qs_s[rows, at]
            near = [
                (back, slice((block - back) * 128, (block - back + 1) * 128))
                for back in (2, 1, 0)
                if block - back >= 0
            ]
            read_b = reads_ref[rows, at]
            parts = _scores(
                qs, [(b, kb_s[r, at]) for b, r in near], read_b, pk_ref[head], block, length, masks
            )
            top = jnp.max(parts[0], axis=1, keepdims=True)
            wide = parts[1]
            for part in parts[2:]:
                wide = jnp.maximum(wide, part)
            top = jnp.maximum(top, jnp.max(wide, axis=1, keepdims=True))
            exps = [jnp.exp(part - top) for part in parts]
            wide = exps[1]
            for part in exps[2:]:
                wide = wide + part
            total = jnp.sum(exps[0], axis=1, keepdims=True) + jnp.sum(wide, axis=1, keepdims=True)
            acc = _nn(exps[0].astype(BF), pv_ref[head]) + _nn(exps[1].astype(BF), read_b)
            for (_, r), part in zip(near, exps[2:]):
                acc = acc + _nn(part.astype(BF), vb_s[r, at])
            mixed_ref[target, at] = (acc * (1.0 / total)).astype(BF)
            lse_all = jnp.where(
                _lane((128, 128), 1) == head, jnp.broadcast_to(top + jnp.log(total), (128, 128)), lse_all
            )
        lse_ref[rows, :] = lse_all


def _bwd_kernel(heads, blocks, where_ref, *rest):
    cots = rest[:4]
    qkv_hbm, pk_ref, pv_ref, mixed_ref, reads_ref, lse_ref, states_hbm = rest[4:11]
    weight_refs = rest[11 : 11 + blocks]
    rest = rest[11 + blocks :]
    dqkv_hbm, dpk_ref, dpv_ref, dm1_ref, dm2_ref, keep_ref, send_ref = rest[:7]
    cots_s, qkv_s, states_s, dqkv_s, dmix_s, project_s, rates_s, out_s, sems, more_sems = rest[7:17]
    scratch = rest[17:]
    step = weight_refs[0].shape[0] - 16
    wide = heads * 128
    every = pl.ds(0, step)
    out_copies = _copies(weight_refs, every, pl.ds(3 * wide, wide), out_s, sems.at[1])
    cot_copies = []
    for quarter, ref in enumerate(cots):
        copy = pltpu.make_async_copy(ref, cots_s.at[quarter], more_sems.at[quarter])
        copy.start()
        cot_copies.append(copy)
    qkv_copy = pltpu.make_async_copy(qkv_hbm, qkv_s, more_sems.at[4])
    qkv_copy.start()
    states_copy = pltpu.make_async_copy(states_hbm, states_s, more_sems.at[5])
    states_copy.start()
    project_copies = _copies(weight_refs, every, pl.ds(0, 3 * wide), project_s, sems.at[0])
    rates_s[16:128, :] = jnp.zeros((112, rates_s.shape[1]), BF)
    for k, block in enumerate(weight_refs):
        copy = pltpu.make_async_copy(
            block.at[pl.ds(step, 16), pl.ds(0, step)],
            rates_s.at[pl.ds(0, 16), pl.ds(k * step, step)],
            sems.at[2, k],
        )
        copy.start()
        project_copies.append(copy)
    for copy in out_copies:
        copy.wait()
    for quarter in range(4):
        cot_copies[quarter].wait()
        dmix_s[quarter * 128 : (quarter + 1) * 128, :] = _nn(cots_s[quarter], out_s[...])
    qkv_copy.wait()
    _mix_backward(
        heads,
        states_copy.wait,
        where_ref,
        qkv_s,
        pk_ref,
        pv_ref,
        mixed_ref,
        reads_ref,
        lse_ref,
        states_s,
        dmix_s,
        dqkv_s,
        dpk_ref,
        dpv_ref,
        dm1_ref,
        dm2_ref,
        *scratch,
    )
    dqkv_copy = pltpu.make_async_copy(dqkv_s, dqkv_hbm, more_sems.at[6])
    dqkv_copy.start()
    for copy in project_copies:
        copy.wait()
    for rows in (slice(256, 512), slice(0, 256)):
        grad = _nt(dqkv_s[rows, : 3 * wide], project_s[...])
        grad = grad + _nn(dqkv_s[rows, 3 * wide :], rates_s[...])
        if rows.start:
            send_ref[...] = grad.astype(BF)
        else:
            keep_ref[...] = grad.astype(BF)
    dqkv_copy.wait()


def _mix_backward(
    heads,
    wait_states,
    where_ref,
    qkv_ref,
    pk_ref,
    pv_ref,
    mixed_ref,
    reads_ref,
    lse_ref,
    states_ref,
    dmix_ref,
    dqkv_ref,
    dpk_ref,
    dpv_ref,
    dm1_ref,
    dm2_ref,
    qn_s,
    kn_s,
    qs_s,
    kb_s,
    v_s,
    vb_s,
    w_s,
    r_s,
    dq_s,
    dk_s,
    dv_s,
    dr_s,
    dqn_s,
    dkn_s,
    dz_s,
):
    place = where_ref[0]
    length = where_ref[1]
    width = heads * 128
    _load_rows(place, length, qkv_ref, heads, qn_s, kn_s, qs_s, kb_s, v_s, vb_s, w_s, r_s)
    masks = _masks()
    scale = 128 ** (-0.5)
    for head in range(heads):
        at = slice(head * 128, (head + 1) * 128)
        dpk = jnp.zeros((16, 128), F32)
        dpv = jnp.zeros((16, 128), F32)
        dk = [jnp.zeros((128, 128), F32)] * 4
        dv = [jnp.zeros((128, 128), F32)] * 4
        for block in range(4):
            rows = slice(block * 128, (block + 1) * 128)
            source = pl.ds(_spot(place, block), 128)
            qs = qs_s[rows, at]
            near = [
                (back, slice((block - back) * 128, (block - back + 1) * 128))
                for back in (2, 1, 0)
                if block - back >= 0
            ]
            read_b = reads_ref[rows, at]
            parts = _scores(
                qs, [(b, kb_s[r, at]) for b, r in near], read_b, pk_ref[head], block, length, masks
            )
            lse = lse_ref[rows, head : head + 1]
            probs = [jnp.exp(part - lse) for part in parts]
            dout = dmix_ref[source, at]
            dout_b = dout.astype(BF)
            dot = jnp.sum(dout * mixed_ref[source, at].astype(F32), axis=1, keepdims=True)
            values = [pv_ref[head], read_b] + [vb_s[r, at] for _, r in near]
            keys = [pk_ref[head], read_b] + [kb_s[r, at] for _, r in near]
            ds_b = [
                (p * (_nt(dout_b, val) - dot)).astype(BF) for p, val in zip(probs, values)
            ]
            probs_b = [p.astype(BF) for p in probs]
            dq = _nn(ds_b[0], keys[0])
            for d, key in zip(ds_b[1:], keys[1:]):
                dq = dq + _nn(d, key)
            dq_s[rows, at] = dq * scale
            dpk = dpk + _tn(ds_b[0], qs)
            dpv = dpv + _tn(probs_b[0], dout_b)
            dr_s[rows, at] = _tn(ds_b[1], qs) + _tn(probs_b[1], dout_b)
            for (back, _), d, p in zip(near, ds_b[2:], probs_b[2:]):
                dk[block - back] = dk[block - back] + _tn(d, qs)
                dv[block - back] = dv[block - back] + _tn(p, dout_b)
            if block >= 2:
                dk_s[(block - 2) * 128 : (block - 1) * 128, at] = dk[block - 2]
                dv_s[(block - 2) * 128 : (block - 1) * 128, at] = dv[block - 2]
        for block in (2, 3):
            rows = slice(block * 128, (block + 1) * 128)
            dk_s[rows, at] = dk[block]
            dv_s[rows, at] = dv[block]
        dpk_ref[head] = dpk
        dpv_ref[head] = dpv
    wait_states()
    zero = jnp.zeros((128, 128), F32)
    carry = [[zero, zero, zero, zero] for _ in range(heads)]
    lanes = _lane((CH, 128), 1)
    for span in range(7, -1, -1):
        rows = slice(span * CH, (span + 1) * CH)
        means = jnp.mean(r_s[rows, :], axis=0, keepdims=True)
        dr_row = jnp.zeros((CH, 128), F32)
        live = (span * CH + _lane((CH, 1), 0) < length).astype(F32)
        for head in range(heads):
            at = slice(head * 128, (head + 1) * 128)
            a1, a2, b1, b2 = carry[head]
            first_b = states_ref[span, 0, head]
            second_b = states_ref[span, 1, head]
            kn = kn_s[rows, at]
            qn = qn_s[rows, at]
            dread_b = dr_s[rows, at].astype(BF)
            both = _nn(jnp.concatenate([kn, qn], axis=0), first_b)
            sig_both = _sig(both)
            act_both = both * sig_both
            slope_both = sig_both * (1.0 + both * (1.0 - sig_both))
            act_b = act_both.astype(BF)
            db_b = (_nt(dread_b, second_b) * slope_both[CH:]).astype(BF)
            if span == 7:
                dqn_s[rows, at] = _nt(db_b, first_b)
                dkn_s[rows, at] = jnp.zeros((CH, 128), F32)
                carry[head] = [_tn(qn, db_b), _tn(act_b[CH:], dread_b), zero, zero]
                continue
            eta = means[:, 3 * head + 1 : 3 * head + 2]
            keep = 1.0 - 0.5 * means[:, 3 * head + 2 : 3 * head + 3]
            pre, sig, slope = both[:CH], sig_both[:CH], slope_both[:CH]
            bend = sig * (1.0 - sig) * (2.0 + pre * (1.0 - 2.0 * sig))
            u_b = act_b[:CH]
            w = w_s[rows, at]
            e = _nn(u_b, second_b) - v_s[rows, at]
            m_b = (e * w).astype(BF)
            p = _nt(m_b, second_b)
            g_b = (p * slope).astype(BF)
            ds1 = b1 + a1
            ds2 = b2 + a2
            dg1_b = (-ds1).astype(BF)
            dg2_b = (-ds2).astype(BF)
            x1 = _nn(kn, dg1_b)
            dp_b = (x1 * slope).astype(BF)
            dm = _nn(dp_b, second_b) + _nn(u_b, dg2_b)
            de = dm * w
            de_b = de.astype(BF)
            du = _nt(m_b, dg2_b) + _nt(de_b, second_b)
            da = x1 * p * bend + du * slope
            da_b = da.astype(BF)
            back = _nt(jnp.concatenate([da_b, db_b], axis=0), first_b)
            dkn_s[rows, at] = _nt(g_b, dg1_b) + back[:CH]
            dqn_s[rows, at] = back[CH:]
            dv_s[rows, at] = dv_s[rows, at] - de
            new1 = keep * a1 + _tn(
                jnp.concatenate([kn, qn], axis=0), jnp.concatenate([da_b, db_b], axis=0)
            )
            new2 = (
                keep * a2
                + _tn(act_b, jnp.concatenate([de_b, dread_b], axis=0))
                + _tn(dp_b, m_b)
            )
            prev1 = states_ref[span, 2, head].astype(F32)
            prev2 = states_ref[span, 3, head].astype(F32)
            deta = jnp.sum(
                jnp.sum(ds1 * prev1 + ds2 * prev2, axis=0, keepdims=True), axis=1, keepdims=True
            )
            dkeep = jnp.sum(
                jnp.sum(a1 * first_b.astype(F32) + a2 * second_b.astype(F32), axis=0, keepdims=True),
                axis=1,
                keepdims=True,
            )
            dw = jnp.sum(dm * e, axis=1, keepdims=True) * live * (2.0 / (CH * 128))
            dr_row = jnp.where(lanes == 3 * head, jnp.broadcast_to(dw, (CH, 128)), dr_row)
            dr_row = jnp.where(
                lanes == 3 * head + 1, jnp.broadcast_to(deta * (1.0 / CH), (CH, 128)), dr_row
            )
            dr_row = jnp.where(
                lanes == 3 * head + 2, jnp.broadcast_to(dkeep * (-0.5 / CH), (CH, 128)), dr_row
            )
            carry[head] = [new1, new2, eta * ds1, eta * ds2]
        rates = r_s[rows, :]
        dz_s[rows, :] = dr_row * rates * (1.0 - rates)
    for head in range(heads):
        dm1_ref[head] = carry[head][0]
        dm2_ref[head] = carry[head][1]
    for quarter in range(4):
        source = pl.ds(_spot(place, quarter), 128)
        here = slice(quarter * 128, (quarter + 1) * 128)
        dqkv_ref[source, 3 * width :] = dz_s[here, :].astype(BF)
        for head in range(heads):
            at = slice(head * 128, (head + 1) * 128)
            for part, grad_s, norm_s in ((0, dq_s, dqn_s), (1, dk_s, dkn_s)):
                col = slice(part * width + head * 128, part * width + (head + 1) * 128)
                raw = qkv_ref[source, col]
                inverse = _scale_of(raw)
                normed = raw * inverse
                dn = norm_s[here, at]
                inner = jnp.mean(dn * normed, axis=-1, keepdims=True)
                dqkv_ref[source, col] = (
                    grad_s[here, at] + inverse * (dn - normed * inner)
                ).astype(BF)
            col = slice(2 * width + head * 128, 2 * width + (head + 1) * 128)
            dqkv_ref[source, col] = dv_s[here, at].astype(BF)


def _row_scratch(heads):
    wide = heads * 128
    return [
        pltpu.VMEM((512, wide), BF),
        pltpu.VMEM((512, wide), BF),
        pltpu.VMEM((512, wide), BF),
        pltpu.VMEM((512, wide), BF),
        pltpu.VMEM((512, wide), F32),
        pltpu.VMEM((512, wide), BF),
        pltpu.VMEM((512, wide), F32),
        pltpu.VMEM((512, 128), F32),
    ]


_VM = pl.BlockSpec(memory_space=pltpu.VMEM)
_SM = pl.BlockSpec(memory_space=pltpu.SMEM)


def _any(count):
    return [pl.BlockSpec(memory_space=pl.ANY)] * count


def _call(kernel, operands, in_specs, after, **settings):
    count = len(operands)
    more = len(after)

    def body(*refs):
        kernel(*refs[:count], *refs[count + more :])

    return pl.pallas_call(body, in_specs=[*in_specs, *_any(more)], **settings)(*operands, *after)


def mix_forward(where, quarters, batch, weights, pk, pv, m1, m2, after=()):
    heads = pk.shape[0]
    wide = heads * 128
    blocks = len(weights)
    step = weights[0].shape[0] - 16
    width = blocks * step
    local = quarters[0].shape[2]
    extra, token, mixed, lse, keep, send, first, qkv, reads, states = _call(
        partial(_fwd_kernel, heads, blocks, batch),
        (where, *quarters, pk, pv, m1, m2, *weights),
        [_SM] + _any(4) + [_VM] * 4 + _any(blocks),
        after,
        name="mix_forward",
        out_shape=(
            _f32(16, width),
            _f32(128, width),
            _bf16(512, wide),
            _f32(512, 128),
            _bf16(256, width),
            _bf16(256, width),
            _bf16(512, width),
            _f32(512, 3 * wide + 128),
            _bf16(512, wide),
            _bf16(8, 4, heads, 128, 128),
        ),
        out_specs=(*[_VM] * 6, *_any(4)),
        scratch_shapes=[
            pltpu.VMEM((4, blocks, local, width), BF),
            pltpu.VMEM((512, width), BF),
            pltpu.VMEM((512, 3 * wide + 128), F32),
            pltpu.VMEM((512, wide), BF),
            pltpu.VMEM((8, 4, heads, 128, 128), BF),
            pltpu.VMEM((width, 3 * wide), BF),
            pltpu.VMEM((128, width), BF),
            pltpu.VMEM((width, wide), BF),
            pltpu.SemaphoreType.DMA((3, blocks)),
            pltpu.SemaphoreType.DMA((4,)),
            pltpu.SemaphoreType.DMA((3,)),
            pltpu.SemaphoreType.DMA((8,)),
        ]
        + _row_scratch(heads),
        compiler_params=pltpu.CompilerParams(vmem_limit_bytes=60 * 1024 * 1024),
        cost_estimate=pl.CostEstimate(flops=10**5, bytes_accessed=10**4, transcendentals=0),
    )
    return first, extra, token, qkv, mixed, reads, lse, states, keep, send


def mix_backward(where, cots, saved, weights, after=()):
    pk = saved[1]
    heads = pk.shape[0]
    wide = heads * 128
    blocks = len(weights)
    step = weights[0].shape[0] - 16
    width = blocks * step
    return _call(
        partial(_bwd_kernel, heads, blocks),
        (where, *cots, *saved, *weights),
        [_SM] + _any(5) + [_VM] * 5 + _any(1 + blocks),
        after,
        name="mix_backward",
        out_shape=(
            _bf16(512, 3 * wide + 128),
            _f32(heads, 16, 128),
            _f32(heads, 16, 128),
            _f32(heads, 128, 128),
            _f32(heads, 128, 128),
            _bf16(256, width),
            _bf16(256, width),
        ),
        out_specs=(*_any(1), *[_VM] * 6),
        scratch_shapes=[
            pltpu.VMEM((4, 128, width), BF),
            pltpu.VMEM((512, 3 * wide + 128), F32),
            pltpu.VMEM((8, 4, heads, 128, 128), BF),
            pltpu.VMEM((512, 3 * wide + 128), BF),
            pltpu.VMEM((512, wide), F32),
            pltpu.VMEM((width, 3 * wide), BF),
            pltpu.VMEM((128, width), BF),
            pltpu.VMEM((width, wide), BF),
            pltpu.SemaphoreType.DMA((3, blocks)),
            pltpu.SemaphoreType.DMA((7,)),
        ]
        + _row_scratch(heads)
        + [pltpu.VMEM((512, wide), F32)] * 6
        + [pltpu.VMEM((512, 128), F32)],
        compiler_params=pltpu.CompilerParams(vmem_limit_bytes=60 * 1024 * 1024),
        cost_estimate=pl.CostEstimate(flops=7 * 10**9, bytes_accessed=10**4, transcendentals=0),
    )


def _feed_kernel(blocks, picks, cols, batch, *rest):
    seconds = rest[:4]
    cots = rest[4:8]
    weight_refs = rest[8 : 8 + blocks]
    (
        hidden_ref,
        gate_ref,
        up_ref,
        keep_ref,
        send_ref,
        feed_keep_ref,
        feed_send_ref,
        gate_s,
        up_s,
        down_s,
        sems,
    ) = rest[8 + blocks :]
    step = weight_refs[0].shape[-2]
    copies = [
        _copies(weight_refs, pl.ds(0, step), pl.ds(w * cols, cols), target, sems.at[w], picks)
        for w, target in enumerate((gate_s, up_s, down_s))
    ]
    for part in range(2):
        rows = slice(part * 256, (part + 1) * 256)
        left = jnp.concatenate([seconds[2 * part][...], seconds[2 * part + 1][...]], axis=0)
        cot = jnp.concatenate([cots[2 * part][batch], cots[2 * part + 1][batch]], axis=0)
        if part == 0:
            for copy in copies[0]:
                copy.wait()
        gate = _nn(left, gate_s[...])
        if part == 0:
            for copy in copies[1]:
                copy.wait()
        up = _nn(left, up_s[...])
        if part == 0:
            for copy in copies[2]:
                copy.wait()
        grad = _nn(cot, down_s[...])
        sig = _sig(gate)
        act = gate * sig
        hidden = (act * up).astype(BF)
        gate_grad = (grad * up * (sig + act * (1.0 - sig))).astype(BF)
        up_grad = (grad * act).astype(BF)
        hidden_ref[rows, :] = hidden
        gate_ref[rows, :] = gate_grad
        up_ref[rows, :] = up_grad
        back = _nt(gate_grad, gate_s[...]) + _nt(up_grad, up_s[...])
        feed = _nt(hidden, down_s[...])
        if part == 0:
            keep_ref[...] = back.astype(BF)
            feed_keep_ref[...] = feed.astype(BF)
        else:
            send_ref[...] = back.astype(BF)
            feed_send_ref[...] = feed.astype(BF)


def feed_forward(seconds, cots, batch, weights, after=()):
    blocks = len(weights)
    picks = tuple(pick for _, pick in weights)
    weights = [array for array, _ in weights]
    step = weights[0].shape[-2]
    cols = weights[0].shape[-1] // 3
    width = blocks * step
    return _call(
        partial(_feed_kernel, blocks, picks, cols, batch),
        (*seconds, *cots, *weights),
        [_VM] * 8 + _any(blocks),
        after,
        name="feed_forward",
        out_shape=(
            jax.ShapeDtypeStruct((512, cols), BF),
            jax.ShapeDtypeStruct((512, cols), BF),
            jax.ShapeDtypeStruct((512, cols), BF),
            jax.ShapeDtypeStruct((256, width), BF),
            jax.ShapeDtypeStruct((256, width), BF),
            jax.ShapeDtypeStruct((256, width), BF),
            jax.ShapeDtypeStruct((256, width), BF),
        ),
        out_specs=(_VM,) * 7,
        scratch_shapes=[pltpu.VMEM((width, cols), BF)] * 3
        + [pltpu.SemaphoreType.DMA((3, blocks))],
        compiler_params=pltpu.CompilerParams(vmem_limit_bytes=48 * 1024 * 1024),
        cost_estimate=pl.CostEstimate(flops=35 * 10**8, bytes_accessed=10**4, transcendentals=0),
    )


def _grad_kernel(groups, counts, picks, keep, sends, *rest):
    total = sum(counts)
    row_refs = rest[:total]
    grad_refs = rest[total : total + len(counts)]
    outs = rest[total + len(counts) :]
    keep_refs, send_refs = outs[: len(keep)], outs[len(keep) :]
    targets = [
        (k, ref, place) for ref, some in zip(send_refs, sends) for place, k in enumerate(some)
    ]
    targets += [(k, ref, None) for ref, k in zip(keep_refs, keep)]
    step = outs[0].shape[-2]
    for k, out_ref, place in targets:
        at = slice(k * step, (k + 1) * step)
        start = 0
        index = 0
        term_at = 0
        for terms in groups:
            value = None
            for count, grad_ref in zip(
                counts[term_at : term_at + terms], grad_refs[term_at : term_at + terms]
            ):
                pieces = []
                for i in range(index, index + count):
                    ref, pick = row_refs[i], picks[i]
                    pieces.append(ref[:, at] if pick is None else ref[pick, :, at])
                index += count
                left = pieces[0] if count == 1 else jnp.concatenate(pieces, axis=0)
                term = _tn(left, grad_ref[...])
                value = term if value is None else value + term
            cols = slice(start, start + grad_refs[term_at].shape[1])
            start = cols.stop
            term_at += terms
            if place is None:
                out_ref[:, cols] = value.astype(BF)
            else:
                out_ref[place, :, cols] = value.astype(BF)


def weight_gradient(groups, blocks, keep, sends, flops=None, after=()):
    terms = [term for group in groups for term in group]
    width = terms[0][0][0][0].shape[-1]
    cols = sum(group[0][1].shape[1] for group in groups)
    step = width // blocks
    pieces = [piece for rows, _ in terms for piece in rows]
    grads = [grad for _, grad in terms]
    return _call(
        partial(
            _grad_kernel,
            tuple(len(group) for group in groups),
            tuple(len(rows) for rows, _ in terms),
            tuple(pick for _, pick in pieces),
            tuple(keep),
            tuple(sends),
        ),
        (*[array for array, _ in pieces], *grads),
        [_VM] * (len(pieces) + len(grads)),
        after,
        name="weight_gradient",
        out_shape=(
            *[_bf16(step, cols)] * len(keep),
            *[_bf16(len(some), step, cols) for some in sends],
        ),
        out_specs=(_VM,) * (len(keep) + len(sends)),
        compiler_params=pltpu.CompilerParams(vmem_limit_bytes=48 * 1024 * 1024),
        cost_estimate=pl.CostEstimate(
            flops=flops or 4 * 10**8 * (len(keep) + sum(len(some) for some in sends)),
            bytes_accessed=10**4,
            transcendentals=0,
        ),
    )


def _small(name, function, shapes, scalars, values, after, flops=10**5):
    return _call(
        function,
        (*scalars, *values),
        [_SM] * len(scalars) + [_VM] * len(values),
        after,
        name=name,
        out_shape=shapes,
        out_specs=(_VM,) * len(shapes),
        cost_estimate=pl.CostEstimate(flops=flops, bytes_accessed=10**4, transcendentals=0),
        compiler_params=pltpu.CompilerParams(vmem_limit_bytes=32 * 1024 * 1024),
    )


def _f32(*shape):
    return jax.ShapeDtypeStruct(shape, F32)


def _bf16(*shape):
    return jax.ShapeDtypeStruct(shape, BF)


def _add_kernel(keep_ref, got_ref, own_ref, other_ref):
    total = keep_ref[...].astype(F32) + got_ref[...].astype(F32)
    own_ref[...] = total[0:128, :]
    other_ref[...] = total[128:256, :].astype(BF)


def add_core(keep, got, after=()):
    width = keep.shape[1]
    return _small("add_core", _add_kernel, (_f32(128, width), _bf16(128, width)), (), (keep, got), after)


def _norm_kernel(rows_ref, own_ref, column_ref, gain_ref, second_ref, residual_ref, inverse_ref):
    residual = rows_ref[...] + own_ref[...] + column_ref[...].astype(F32)
    inverse = _scale_of(residual)
    second_ref[...] = (residual * inverse * gain_ref[...]).astype(BF)
    residual_ref[...] = residual
    inverse_ref[...] = jnp.broadcast_to(inverse, (128, 128))


def second_norm(rows, own, column, gain, flops=10**5, after=()):
    width = rows.shape[1]
    return _small(
        "second_norm",
        _norm_kernel,
        (_bf16(128, width), _f32(128, width), _f32(128, 128)),
        (),
        (rows, own, column, gain),
        after,
        flops,
    )


def _norm_grad(grad, normed, inverse, gain):
    scaled = grad * gain
    return inverse * (scaled - normed * jnp.mean(scaled * normed, axis=-1, keepdims=True))


def _second_back_kernel(batch, own_ref, column_ref, cot_ref, residual_ref, inverse_ref, gain_ref, low_ref, out_ref, sum_ref):
    grad = own_ref[...] + column_ref[...].astype(F32)
    inverse = inverse_ref[:, 0:1]
    normed = residual_ref[...] * inverse
    out = cot_ref[batch] + _norm_grad(grad, normed, inverse, gain_ref[...])
    low_ref[...] = out.astype(BF)
    out_ref[...] = out
    sum_ref[...] = jnp.sum(grad * normed, axis=0, keepdims=True)


def second_back(batch, own, column, cots, residual, inverse, gain, after=()):
    width = own.shape[1]
    return _small(
        "second_back",
        partial(_second_back_kernel, batch),
        (_bf16(128, width), _f32(128, width), _f32(1, width)),
        (),
        (own, column, cots, residual, inverse, gain),
        after,
        3 * 10**9,
    )


def _place(where_ref, k, step):
    return pl.ds(pl.multiple_of(where_ref[2 + k] * step, step), step)


def _live(where_ref):
    return (where_ref[0] * 128 + _lane((128, 1), 0) < where_ref[1]).astype(F32)


def _cots_kernel(blocks, where_a, where_b, scale_ref, got_ref, rows_ref, low_ref):
    width = got_ref.shape[3]
    step = width // blocks
    for b, where_ref in enumerate((where_a, where_b)):
        factor = _live(where_ref) * scale_ref[b]
        for k in range(blocks):
            piece = got_ref[:, b, :, _place(where_ref, k, step)].reshape(128, step).astype(F32)
            piece = piece * factor
            rows_ref[b, :, k * step : (k + 1) * step] = piece
            low_ref[b, :, k * step : (k + 1) * step] = piece.astype(BF)


def take_cots(wheres, scales, got, flops=10**5, after=()):
    blocks, batches, _, width = got.shape
    return _small(
        "take_cots",
        partial(_cots_kernel, blocks),
        (_f32(batches, 128, width), _bf16(batches, 128, width)),
        (*wheres, scales),
        (got,),
        after,
        flops,
    )


def _finish_kernel(blocks, where_a, where_b, own_a, own_b, column_ref, res_a, res_b, out_ref):
    width = column_ref.shape[2]
    step = width // blocks
    for b, (where_ref, own, res) in enumerate(((where_a, own_a, res_a), (where_b, own_b, res_b))):
        rows = _live(where_ref) * (res[...] + own[...] + column_ref[b].astype(F32))
        rows = rows.astype(BF)
        for k in range(blocks):
            piece = rows[:, k * step : (k + 1) * step].reshape(blocks, 128 // blocks, step)
            out_ref[:, b, :, _place(where_ref, k, step)] = piece


def finish_rows(blocks, wheres, owns, column, residuals, flops=10**5, after=()):
    width = column.shape[2]
    return _small(
        "finish_rows",
        partial(_finish_kernel, blocks),
        (_bf16(blocks, 2, 128 // blocks, width),),
        wheres,
        (*owns, column, *residuals),
        after,
        flops,
    )[0]


def _token_grad(own_ref, column_ref, rows_ref, back_ref, gain_ref):
    grad = own_ref[...] + column_ref[...].astype(F32)
    rows = rows_ref[...]
    inverse = _scale_of(rows)
    normed = rows * inverse
    out = back_ref[...] + _norm_grad(grad, normed, inverse, gain_ref[...])
    return out.astype(BF), jnp.sum(grad * normed, axis=0, keepdims=True)


def _first_back_kernel(own_ref, column_ref, rows_ref, back_ref, gain_ref, low_ref, sum_ref):
    low_ref[...], sum_ref[...] = _token_grad(own_ref, column_ref, rows_ref, back_ref, gain_ref)


def first_back(own, column, rows, back, gain, after=()):
    width = own.shape[1]
    return _small(
        "first_back",
        _first_back_kernel,
        (_bf16(128, width), _f32(1, width)),
        (),
        (own, column, rows, back, gain),
        after,
    )


def _last_kernel(blocks, where_ref, own_ref, column_ref, rows_ref, back_ref, gain_ref, low_ref, sum_a, two_a, two_b, out_ref, gains_ref):
    width = own_ref.shape[1]
    step = width // blocks
    low, total = _token_grad(own_ref, column_ref, rows_ref, back_ref, gain_ref)
    total = total + sum_a[...]
    two = two_a[...] + two_b[...]
    first = low_ref[...]
    gains_ref[...] = jnp.zeros((8, width), F32)
    for k in range(blocks):
        at = slice(k * step, (k + 1) * step)
        place = _place(where_ref, k, step)
        out_ref[:, 0, :, place] = first[:, at].reshape(blocks, 128 // blocks, step)
        out_ref[:, 1, :, place] = low[:, at].reshape(blocks, 128 // blocks, step)
        gains_ref[0:1, place] = total[:, at]
        gains_ref[1:2, place] = two[:, at]


def last_rows(blocks, where, own, column, rows, back, gain, low, sum_a, two_a, two_b, after=()):
    width = own.shape[1]
    return _small(
        "last_rows",
        partial(_last_kernel, blocks),
        (_bf16(blocks, 2, 128 // blocks, width), _f32(8, width)),
        (where,),
        (own, column, rows, back, gain, low, sum_a, two_a, two_b),
        after,
    )


def _ring_kernel(indices, passing, splits, *rest):
    count = len(indices)
    keeps, gots = rest[:count], rest[count : 2 * count]
    passed_ref = rest[2 * count] if passing else None
    outs = rest[2 * count + passing :]
    start = 0
    done = 0
    for keep, got, index, sizes in zip(keeps, gots, indices, splits):
        cols = keep.shape[1]
        total = keep[...].astype(F32) + got[index].astype(F32)
        if passing:
            total = total + passed_ref[:, start : start + cols].astype(F32)
        if sizes is None:
            outs[0][:, start : start + cols] = total.astype(BF)
        else:
            for offset, size, turned in sizes:
                piece = total[:, offset : offset + -(-size // 128) * 128]
                if turned:
                    outs[done][...] = piece.T[:size]
                else:
                    outs[done][...] = piece[:, :size]
                done += 1
        start += cols


def ring_step(keeps, gots, indices, passed, splits=None, after=()):
    step = keeps[0].shape[0]
    cols = sum(k.shape[1] for k in keeps)
    if splits is None:
        shapes = (_bf16(step, cols),)
        splits = (None,) * len(keeps)
    else:
        shapes = tuple(
            _f32(size, step) if turned else _f32(step, size)
            for sizes in splits
            for _, size, turned in sizes
        )
    return _small(
        "ring_step",
        partial(_ring_kernel, tuple(indices), len(passed), tuple(splits)),
        shapes,
        (),
        (*keeps, *gots, *passed),
        after,
    )


def _hop_kernel(value_ref, got_ref, out_ref):
    out_ref[...] = value_ref[...] + got_ref[...].astype(F32)


def add_hop(value, got, after=()):
    return _small("add_hop", _hop_kernel, (_f32(*value.shape),), (), (value, got), after)[0]


def _join_kernel(*refs):
    *grads, out_ref = refs
    count = len(grads) // 2
    start = 0
    for one, two in zip(grads[:count], grads[count:]):
        for head in range(one.shape[0]):
            rows = one.shape[1]
            out_ref[start : start + rows, :] = one[head] + two[head]
            start += rows


def join_sums(one, two, after=()):
    rows = sum(g.shape[0] * g.shape[1] for g in one)
    return _small("join_sums", _join_kernel, (_f32(rows, 128),), (), (*one, *two), after)[0]


def _tick_kernel(out_ref):
    out_ref[...] = jnp.zeros((8, 128), F32)


def tick(after=()):
    return _small("tick", _tick_kernel, (_f32(8, 128),), (), (), after, 4 * 10**9)[0]


DP = ("z", "x")


def _swap(value, axis):
    return lax.ppermute(value, axis, [(0, 1), (1, 0)])


BLOCKS = 8
LONG = 4 * 10**9
STEP = 128
DOWN = (1, 2, 3, 0)
RING = [(0, 1), (1, 2), (2, 3), (3, 0)]
BACK = [(1, 0), (2, 1), (3, 2), (0, 3)]


def _ring_sized():
    return lax.axis_size("z") == 4


def _block_ids():
    if not _ring_sized():
        return jnp.arange(BLOCKS, dtype=jnp.int32)
    z = lax.axis_index("z")
    x = lax.axis_index("x")
    zs = jnp.stack([(z + 4 - i) % 4 for i in DOWN])
    return jnp.concatenate([2 * zs + x, 2 * zs + (1 - x)]).astype(jnp.int32)


class _Order:
    def __init__(self):
        self.last = []

    def __call__(self, function, *values, need=()):
        result = function(*values, after=(*self.last, *need))
        self.last = [min(jax.tree.leaves(result), key=lambda leaf: leaf.size)]
        return result


def _ring(block):
    return lax.ppermute(block, "z", RING)


def _in_order(ring, across):
    return [ring[i] for i in DOWN] + [across[i] for i in DOWN]


def _scatter_whole(keep, *sends):
    whole = jnp.concatenate([keep, *sends]).reshape(BLOCKS * STEP, -1)
    return lax.psum_scatter(whole, DP, scatter_dimension=0, tiled=True).astype(F32)


def _quarters(own):
    column = _swap(own, "y")
    return [own, column, _swap(own, "c"), _swap(column, "c")]


def per_device(
    tokens,
    grad_output,
    query_weight,
    key_weight,
    value_weight,
    rates_weight,
    out_weight,
    gate_weight,
    up_weight,
    down_weight,
    norm1_gain,
    norm2_gain,
    persist_key,
    persist_value,
    memory_first,
    memory_second,
    seq_lengths,
    deal,
):
    devices = lax.axis_size("z") * lax.axis_size("x")
    dp_index = lax.axis_index("z") * lax.axis_size("x") + lax.axis_index("x")
    place = lax.axis_index("y") * 2 + lax.axis_index("c")
    seq_count = seq_lengths.shape[0]
    batches = seq_count // devices
    local_rows = tokens.shape[2]
    width = tokens.shape[3]
    quarter = local_rows * devices
    rows_of = query_weight.shape[0]
    head_cols = query_weight.shape[1]
    rate_cols = rates_weight.shape[1]
    hidden_cols = gate_weight.shape[1]

    batch_of = deal // devices
    batch_ids = jnp.arange(batches, dtype=jnp.int32)
    batch_tokens = jnp.sum(
        jnp.where(batch_of[None, :] == batch_ids[:, None], seq_lengths[None, :], 0), axis=1
    ).astype(F32)
    batch_scale = jnp.sum(seq_lengths).astype(F32) / (batches * batch_tokens)
    span = range(batches)
    my_seqs = [batches * dp_index + b for b in span]
    lengths = [seq_lengths[s] for s in my_seqs]
    scales = [batch_scale[batch_of[s]] for s in my_seqs]
    ring_sized = _ring_sized()
    ids = _block_ids()
    where = [
        jnp.concatenate([jnp.stack([place, lengths[b]]).astype(jnp.int32), ids]) for b in span
    ]
    scale = jnp.stack(scales)

    def deal_in(array):
        part = array.reshape(devices, batches, local_rows, width)
        part = lax.all_to_all(part, DP, split_axis=0, concat_axis=0, tiled=True)
        if local_rows * BLOCKS == quarter:
            return part
        part = part.transpose(1, 0, 2, 3).reshape(batches, BLOCKS, quarter // BLOCKS, width)
        return part.transpose(1, 0, 2, 3)

    def deal_out(part):
        if local_rows * BLOCKS != quarter:
            part = part.transpose(1, 0, 2, 3).reshape(batches, devices, local_rows, width)
            part = part.transpose(1, 0, 2, 3)
        part = lax.all_to_all(part, DP, split_axis=0, concat_axis=0, tiled=True)
        return part.reshape(seq_count, 1, local_rows, width)

    mix_shard = jnp.concatenate([query_weight, key_weight, value_weight, out_weight], axis=1)
    extra = jnp.concatenate(
        [
            rates_weight.T,
            norm1_gain[None],
            norm2_gain[None],
            jnp.zeros((16 - rate_cols - 2, rows_of), BF),
        ]
    )
    pad = -hidden_cols % 128
    feed_shard = jnp.concatenate(
        [jnp.pad(w, ((0, 0), (0, pad))) for w in (gate_weight, up_weight, down_weight)], axis=1
    )
    got_tokens = deal_in(tokens)

    run = _Order()

    def mix_of(b, wheres, need=()):
        return run(
            mix_forward,
            wheres[b],
            quarters,
            b,
            mix_weights,
            persist_key,
            persist_value,
            memory_first,
            memory_second,
            need=need,
        )

    if ring_sized:
        extra = jnp.pad(extra, ((0, 0), (0, mix_shard.shape[1] - rows_of)))
        mix0 = jnp.concatenate([mix_shard, extra], axis=0)
        mix1 = _ring(mix0)
        mix_across0 = _swap(mix0, "x")
        mix1, mix_across0, feed0, scale, *where = lax.optimization_barrier(
            (mix1, mix_across0, feed_shard, scale, *where)
        )
        mix2 = _ring(mix1)
        mix_across1 = _swap(mix1, "x")
        mix2, mix_across1 = lax.optimization_barrier((mix2, mix_across1))
        mix3 = _ring(mix2)
        mix_across2 = _swap(mix2, "x")
        quarters = _quarters(got_tokens)
        mix3, mix_across2, feed0, cots_in = lax.optimization_barrier(
            (mix3, mix_across2, feed0, grad_output)
        )
        got_cots = deal_in(cots_in)
        mix_across3 = _swap(mix3, "x")
        feed1 = _ring(feed0)
        feed3 = lax.ppermute(feed0, "z", BACK)
        feed0, mix_across3 = lax.optimization_barrier((feed0, mix_across3))
        feed_across0 = _swap(feed0, "x")
        mix_weights = _in_order(
            [mix0, mix1, mix2, mix3], [mix_across0, mix_across1, mix_across2, mix_across3]
        )
    else:
        mix_full = lax.all_gather(mix_shard, DP, axis=0, tiled=True)
        extra = lax.all_gather(extra, DP, axis=1, tiled=True)
        extra = jnp.pad(
            extra.reshape(16, BLOCKS, STEP), ((0, 0), (0, 0), (0, mix_shard.shape[1] - STEP))
        )
        mix_weights = [
            jnp.concatenate([mix_full[k * STEP : (k + 1) * STEP], extra[:, k]])
            for k in range(BLOCKS)
        ]
        feed_full = lax.all_gather(feed_shard, DP, axis=0, tiled=True)
        feed_weights = [(feed_full[k * STEP : (k + 1) * STEP], None) for k in range(BLOCKS)]
        quarters = _quarters(got_tokens)
        got_cots = deal_in(grad_output)

    mix_a = mix_of(0, where)
    if ring_sized:
        feed1, feed3, *mix_a = lax.optimization_barrier((feed1, feed3, *mix_a))
    gain_one = mix_a[1][rate_cols : rate_cols + 1]
    gain_two = mix_a[1][rate_cols + 1 : rate_cols + 2]
    core_a = _swap(mix_a[9], "c")
    early = []
    cot_rows, cot_own = run(
        take_cots, where, scale, got_cots, LONG, need=[feed_across0] if ring_sized else []
    )
    if ring_sized:
        feed2 = _ring(feed1)
        feed_across13 = _swap(jnp.stack([feed1, feed3]), "x")
        early = [feed2, feed_across13]
    own_a, other_a = run(add_core, mix_a[8], core_a)
    column_a = _swap(other_a, "y")
    cot_column = _swap(cot_own, "y")
    cot_core = _swap(cot_own, "c")
    mix_b = mix_of(1, where)
    mixes = [mix_a, mix_b]
    core_b = _swap(mix_b[9], "c")
    token_rows = [m[2] for m in mixes]
    second_a, residual_a, inverse_a = run(
        second_norm, token_rows[0], own_a, column_a, gain_two, LONG, need=[*early, cot_column]
    )
    early = []
    if ring_sized:
        feed_across2 = _swap(feed2, "x")
        feed_weights = _in_order(
            [(feed0, None), (feed1, None), (feed2, None), (feed3, None)],
            [(feed_across0, None), (feed_across13, 0), (feed_across2, None), (feed_across13, 1)],
        )
    second_a = _quarters(second_a)
    own_b, other_b = run(add_core, mix_b[8], core_b, need=[second_a[2]])
    column_b = _swap(other_b, "y")
    cots = [cot_own, cot_column, cot_core, _swap(cot_column, "c")]
    second_b, residual_b, inverse_b = run(
        second_norm, token_rows[1], own_b, column_b, gain_two, need=[*early, cots[3]]
    )
    second_b = _quarters(second_b)
    second = [second_a, second_b]
    residual = [residual_a, residual_b]

    def feed_of(b, need=()):
        return run(feed_forward, second[b], cots, b, feed_weights, need=need)

    feed_a = feed_of(0)
    core_a = _swap(feed_a[4], "c")
    run(tick, need=second_b[1:2])
    own_a, other_a = run(add_core, feed_a[3], core_a)
    column_a = _swap(other_a, "y")
    feed_b = feed_of(1)
    feeds = [feed_a, feed_b]
    core_b = _swap(feed_b[4], "c")
    def plain(pieces):
        return [(piece, None) for piece in pieces]

    def across(part):
        return _swap(part, "x") if ring_sized else part

    feed_groups = [
        [(plain(second[b]), feeds[b][1]) for b in span],
        [(plain(second[b]), feeds[b][2]) for b in span],
        [([(piece, b) for piece in cots], feeds[b][0]) for b in span],
    ]
    class Sum:
        def __init__(self, keeps, gots, splits):
            self.keeps = keeps
            self.gots = gots
            self.splits = splits
            self.place = 0
            self.passed = []
            self.results = None

        def step(self, need=()):
            place = self.place
            self.place += 1
            final = place == 3
            if not ring_sized:
                if final:
                    self.results = [
                        whole[:, at : at + size].T if turned else whole[:, at : at + size]
                        for keep, got, sizes in zip(self.keeps, self.gots, self.splits)
                        for whole in [_scatter_whole(jnp.stack(keep), *got)]
                        for at, size, turned in sizes
                    ]
                return
            keeps = [keep[place] for keep in self.keeps]
            pieces = [
                [(part, i) for part in got for i in range(part.shape[0])][place]
                for got in self.gots
            ]
            gots = [part for part, _ in pieces]
            indices = [i for _, i in pieces]
            results = run(
                ring_step, keeps, gots, indices, self.passed, self.splits if final else None, need=need
            )
            if final:
                self.results = results
            else:
                self.passed = [_ring(results[0])]

    class AllSum:
        def __init__(self, value, axes, sent):
            self.value = value
            self.sent = sent
            self.hops = []
            for axis in axes:
                size = lax.axis_size(axis)
                step = 1
                while step < size:
                    self.hops.append((axis, [(i, i ^ step) for i in range(size)]))
                    step *= 2
            self.start()

        def start(self):
            if self.hops:
                axis, pairs = self.hops.pop(0)
                self.got = lax.ppermute(self.value.astype(self.sent), axis, pairs)

        def step(self, need=()):
            self.value = run(add_hop, self.value, self.got, need=need)
            self.got = None
            self.start()

        def rest(self):
            while self.got is not None:
                self.step()
            return self.value

    first_sends = run(
        weight_gradient, feed_groups, BLOCKS, (), ((4,),), LONG, need=[column_a]
    )
    feed_got = [across(first_sends[0])]
    mixer_a, back_a, two_a = run(
        second_back, 0, own_a, column_a, cot_rows, residual_a, inverse_a, gain_two
    )
    mixer_column = _swap(mixer_a, "y")
    mixer_core = _swap(mixer_a, "c")
    own_b, other_b = run(add_core, feed_b[3], core_b)
    column_b = _swap(other_b, "y")
    feed_core = [_swap(f[6], "c") for f in feeds]
    feed_own, feed_other = zip(
        *[run(add_core, feeds[b][5], feed_core[b], need=[mixer_core]) for b in span],
        strict=True,
    )
    feed_parts = run(weight_gradient, feed_groups, BLOCKS, range(4), ((5,), (6, 7)))
    feed_got.append(across(feed_parts[4]))
    feed_keep = feed_parts[:4]
    mixer_column, *feed_keep = lax.optimization_barrier((mixer_column, *feed_keep))
    mixer_a = [mixer_a, mixer_column, mixer_core, _swap(mixer_column, "c")]
    mixer_b, back_b, two_b = run(
        second_back, 1, own_b, column_b, cot_rows, residual_b, inverse_b, gain_two
    )
    mixer_b_column = _swap(mixer_b, "y")
    mixer_b_core = _swap(mixer_b, "c")
    feed_column = _swap(jnp.stack(feed_other), "y")
    stride = feed_keep[0].shape[1] // 3
    feed_sum = Sum(
        [feed_keep],
        [feed_got],
        [[(i * stride, hidden_cols, True) for i in range(3)]],
    )
    feed_sum.step()

    def mix_back_of(b, cots, need=()):
        saved = (mixes[b][3], persist_key, persist_value, *mixes[b][4:8])
        return run(mix_backward, where[b], cots, saved, mix_weights, need=need)

    mix_back_a = mix_back_of(0, mixer_a, need=[mixer_b_core])
    core_a = _swap(mix_back_a[6], "c")
    mixer_b_column, last_part, *mix_back_a = lax.optimization_barrier(
        (mixer_b_column, feed_parts[5], *mix_back_a)
    )
    feed_got.append(across(last_part))
    mixer_b = [mixer_b, mixer_b_column, mixer_b_core, _swap(mixer_b_column, "c")]
    feed_sum.step()
    layer_out = deal_out(run(finish_rows, BLOCKS, where, feed_own, feed_column, residual, LONG))
    own_a, other_a = run(add_core, mix_back_a[5], core_a)
    column_a = _swap(other_a, "y")
    mix_back_b = mix_back_of(1, mixer_b)
    backs = [mix_back_a, mix_back_b]
    core_b = _swap(mix_back_b[6], "c")
    feed_sum.step()
    project_groups = [
        [(plain([m[0]]), k[0]) for m, k in zip(mixes, backs)],
        [(plain(mixer), m[4]) for mixer, m in ((mixer_a, mix_a), (mixer_b, mix_b))],
    ]
    run(tick, need=[layer_out])
    first_sends = run(weight_gradient, project_groups, BLOCKS, (), ((4,),))
    project_got = [across(first_sends[0])]
    own_b, other_b = run(add_core, mix_back_b[5], core_b)
    column_b = _swap(other_b, "y")
    memory_sum = AllSum(
        run(join_sums, mix_back_a[1:5], mix_back_b[1:5]), DP[::-1], BF
    )
    project_parts = run(weight_gradient, project_groups, BLOCKS, range(4), ((5,), (6, 7)))
    project_keep = project_parts[:4]
    if ring_sized:
        project_got[0], *late = lax.optimization_barrier((project_got[0], *project_parts[4:]))
    else:
        late = project_parts[4:]
    project_got += [across(part) for part in late]
    rates_at = 3 * head_cols
    project_sum = Sum(
        [project_keep],
        [project_got],
        [
            [(i * head_cols, head_cols, False) for i in range(3)]
            + [(rates_at, rate_cols, False), (rates_at + 128, head_cols, False)]
        ],
    )
    project_sum.step()
    memory_sum.step()
    token_a, one_a = run(first_back, own_a, column_a, token_rows[0], back_a, gain_one)
    token_send, gains = run(
        last_rows,
        BLOCKS,
        where[1],
        own_b,
        column_b,
        token_rows[1],
        back_b,
        gain_one,
        token_a,
        one_a,
        two_a,
        two_b,
    )
    grad_tokens = deal_out(token_send)
    gain_sum = AllSum(gains, ("c", "y", "x", "z"), F32)
    gain_sum.step()
    project_sum.step()
    feed_sum.step()
    gain_sum.step()
    memory_sum.step()
    gain_sum.step()
    project_sum.step()
    gain_sum.step()
    flat = memory_sum.rest()
    gains = gain_sum.rest()
    project_sum.step()
    gate_total, up_total, down_total = feed_sum.results
    *project_totals, out_total = project_sum.results

    memory_out = []
    start = 0
    for m in mix_back_a[1:5]:
        size = m.size // 128
        memory_out.append(flat[start : start + size].reshape(m.shape))
        start += size

    return (
        layer_out,
        grad_tokens,
        *project_totals,
        out_total,
        gate_total.T,
        up_total.T,
        down_total.T,
        gains[0],
        gains[1],
        memory_out[0],
        memory_out[1],
        memory_out[2],
        memory_out[3],
    )


def solution(mesh):
    sizes = mesh.devices.shape
    fine = Mesh(mesh.devices.reshape(sizes[0] // 2, 2, 2, sizes[1] // 2), ("z", "x", "y", "c"))
    tensor = ("y", "c")
    return jax.shard_map(
        per_device,
        mesh=fine,
        in_specs=(
            P(None, tensor, DP, None),
            P(None, tensor, DP, None),
            P(DP, tensor),
            P(DP, tensor),
            P(DP, tensor),
            P(DP, tensor),
            P(DP, tensor),
            P(DP, tensor),
            P(DP, tensor),
            P(DP, tensor),
            P(DP),
            P(DP),
            P(tensor, None, None),
            P(tensor, None, None),
            P(tensor, None, None),
            P(tensor, None, None),
            P(),
            P(),
        ),
        out_specs=(
            P(None, tensor, DP, None),
            P(None, tensor, DP, None),
            P(DP, tensor),
            P(DP, tensor),
            P(DP, tensor),
            P(DP, tensor),
            P(DP, tensor),
            P(DP, tensor),
            P(DP, tensor),
            P(DP, tensor),
            P(),
            P(),
            P(tensor, None, None),
            P(tensor, None, None),
            P(tensor, None, None),
            P(tensor, None, None),
        ),
        check_vma=False,
    )
```

```python
from functools import partial

import jax
import jax.numpy as jnp
from jax import lax
from jax.experimental import pallas as pl
from jax.experimental.pallas import tpu as pltpu
from jax.sharding import Mesh
from jax.sharding import PartitionSpec as P

CH = 64
WINDOW = 256
EPS = 1e-06
NEG = -1e30
BF = jnp.bfloat16
F32 = jnp.float32


def _nn(a, b):
    return lax.dot_general(a, b, (((1,), (0,)), ((), ())), preferred_element_type=F32)


def _nt(a, b):
    return lax.dot_general(a, b, (((1,), (1,)), ((), ())), preferred_element_type=F32)


def _tn(a, b):
    return lax.dot_general(a, b, (((0,), (0,)), ((), ())), preferred_element_type=F32)


def _sig(v):
    return 1.0 / (1.0 + jnp.exp(-v))


def _scale_of(v):
    return lax.rsqrt(jnp.mean(v * v, axis=-1, keepdims=True) + EPS)


def _lane(shape, dim):
    return lax.broadcasted_iota(jnp.int32, shape, dim)


def _masks():
    rows = _lane((128, 128), 0)
    cols = _lane((128, 128), 1)
    return cols > rows, cols <= rows, (rows // CH) == (cols // CH)


def _scores(qs, near_keys, read_b, pkey, block, length, masks):
    older, newer, same_span = masks
    read_ok = same_span & (block * 128 + _lane((128, 128), 1) < length)
    parts = [_nt(qs, pkey), jnp.where(read_ok, _nt(qs, read_b), NEG)]
    for back, keys in near_keys:
        part = _nt(qs, keys)
        if back == 2:
            part = jnp.where(older, part, NEG)
        elif back == 0:
            part = jnp.where(newer, part, NEG)
        parts.append(part)
    return parts


def _spot(place, quarter):
    there = place ^ quarter
    return pl.multiple_of((((there & 1) << 1) | (there >> 1)) * 128, 128)


def _load_rows(place, length, qkv_ref, heads, qn_s, kn_s, qs_s, kb_s, v_s, vb_s, w_s, r_s):
    width = heads * 128
    for quarter in range(4):
        source = pl.ds(_spot(place, quarter), 128)
        here = pl.ds(quarter * 128, 128)
        live = (quarter * 128 + _lane((128, 1), 0) < length).astype(F32)
        rates = _sig(qkv_ref[source, 3 * width : 3 * width + 128].astype(F32))
        r_s[here, :] = rates
        for head in range(heads):
            at = slice(head * 128, (head + 1) * 128)
            q = qkv_ref[source, head * 128 : (head + 1) * 128].astype(F32)
            k = qkv_ref[source, width + head * 128 : width + (head + 1) * 128].astype(F32)
            v = qkv_ref[source, 2 * width + head * 128 : 2 * width + (head + 1) * 128].astype(F32)
            qn_s[here, at] = (q * _scale_of(q)).astype(BF)
            kn_s[here, at] = (k * _scale_of(k)).astype(BF)
            qs_s[here, at] = (q * (128 ** (-0.5))).astype(BF)
            kb_s[here, at] = k.astype(BF)
            v_s[here, at] = v
            vb_s[here, at] = v.astype(BF)
            weighting = rates[:, 3 * head : 3 * head + 1] * live * (2.0 / (CH * 128))
            w_s[here, at] = jnp.broadcast_to(weighting, (128, 128))


def _block(block, pick, rows, cols):
    return block.at[rows, cols] if pick is None else block.at[pick, rows, cols]


def _copies(blocks, rows, cols, target, sems, picks=None):
    made = []
    for k, block in enumerate(blocks):
        copy = pltpu.make_async_copy(
            _block(block, picks[k] if picks else None, rows, cols),
            target.at[pl.ds(k * rows.size, rows.size), :],
            sems.at[k],
        )
        copy.start()
        made.append(copy)
    return made


def _fwd_kernel(
    heads,
    blocks,
    batch,
    where_ref,
    own_ref,
    ypart_ref,
    cpart_ref,
    far_ref,
    pk_ref,
    pv_ref,
    m1_ref,
    m2_ref,
    *rest,
):
    weight_refs = rest[:blocks]
    extra_ref, token_ref, mixed_ref, lse_ref, keep_ref, send_ref = rest[blocks : blocks + 6]
    first_hbm, qkv_hbm, reads_hbm, states_hbm = rest[blocks + 6 : blocks + 10]
    (
        pieces_s,
        first_s,
        qkv_s,
        low_s,
        reads_s,
        states_s,
        project_s,
        rates_s,
        out_s,
        sems,
        piece_sems,
        out_sems,
        state_sems,
    ) = rest[blocks + 10 : blocks + 23]
    scratch = rest[blocks + 23 :]
    step = weight_refs[0].shape[0] - 16
    wide = heads * 128
    every = pl.ds(0, step)
    piece_copies = []
    for quarter, ref in enumerate((own_ref, ypart_ref, cpart_ref, far_ref)):
        copy = pltpu.make_async_copy(
            ref.at[:, batch], pieces_s.at[quarter], piece_sems.at[quarter]
        )
        copy.start()
        piece_copies.append(copy)
    rates_s[16:128, :] = jnp.zeros((112, rates_s.shape[1]), BF)
    extra = []
    for k, block in enumerate(weight_refs):
        copy = pltpu.make_async_copy(
            block.at[pl.ds(step, 16), pl.ds(0, step)],
            rates_s.at[pl.ds(0, 16), pl.ds(k * step, step)],
            sems.at[2, k],
        )
        copy.start()
        extra.append(copy)
    project_copies = _copies(weight_refs, every, pl.ds(0, 3 * wide), project_s, sems.at[0])
    out_copies = _copies(weight_refs, every, pl.ds(3 * wide, wide), out_s, sems.at[1])
    for copy in extra:
        copy.wait()
    extra_rows = rates_s[0:16, :].astype(F32)
    extra_ref[...] = extra_rows
    gain = extra_rows[3 * heads : 3 * heads + 1, :]
    width = blocks * step
    for quarter in range(4):
        piece_copies[quarter].wait()
        raw = pieces_s[quarter].reshape(128, width).astype(F32)
        inverse = _scale_of(raw)
        for k in range(blocks):
            source = pl.ds(pl.multiple_of(where_ref[2 + k] * step, step), step)
            piece = pieces_s[quarter, :, :, source].reshape(128, step).astype(F32)
            at = slice(k * step, (k + 1) * step)
            if quarter == 0:
                token_ref[:, at] = piece
            first_s[quarter * 128 : (quarter + 1) * 128, at] = (
                piece * inverse * gain[:, at]
            ).astype(BF)
    outgoing = [pltpu.make_async_copy(first_s, first_hbm, out_sems.at[0])]
    outgoing[0].start()
    for copy in project_copies:
        copy.wait()
    for quarter in range(4):
        rows = slice(quarter * 128, (quarter + 1) * 128)
        left = first_s[rows, :]
        qkv_s[rows, : 3 * wide] = _nn(left, project_s[...])
        qkv_s[rows, 3 * wide :] = _nt(left, rates_s[...])
    low_s[...] = qkv_s[...].astype(BF)
    outgoing.append(pltpu.make_async_copy(low_s, qkv_hbm, out_sems.at[1]))
    outgoing[1].start()

    def send_state(span):
        copy = pltpu.make_async_copy(
            states_s.at[span], states_hbm.at[span], state_sems.at[span]
        )
        copy.start()
        outgoing.append(copy)

    def send_reads():
        copy = pltpu.make_async_copy(reads_s, reads_hbm, out_sems.at[2])
        copy.start()
        outgoing.append(copy)

    _mix_forward(
        heads,
        send_state,
        send_reads,
        where_ref,
        qkv_s,
        pk_ref,
        pv_ref,
        m1_ref,
        m2_ref,
        mixed_ref,
        reads_s,
        lse_ref,
        states_s,
        *scratch,
    )
    for copy in out_copies:
        copy.wait()
    send_ref[...] = _nt(mixed_ref[256:512, :], out_s[...]).astype(BF)
    keep_ref[...] = _nt(mixed_ref[0:256, :], out_s[...]).astype(BF)
    for copy in outgoing:
        copy.wait()


def _mix_forward(
    heads,
    send_state,
    send_reads,
    where_ref,
    qkv_ref,
    pk_ref,
    pv_ref,
    m1_ref,
    m2_ref,
    mixed_ref,
    reads_ref,
    lse_ref,
    states_ref,
    qn_s,
    kn_s,
    qs_s,
    kb_s,
    v_s,
    vb_s,
    w_s,
    r_s,
):
    place = where_ref[0]
    length = where_ref[1]
    _load_rows(place, length, qkv_ref, heads, qn_s, kn_s, qs_s, kb_s, v_s, vb_s, w_s, r_s)
    carry = [
        [m1_ref[h], m2_ref[h], jnp.zeros((128, 128), F32), jnp.zeros((128, 128), F32)]
        for h in range(heads)
    ]
    for span in range(8):
        rows = slice(span * CH, (span + 1) * CH)
        means = jnp.mean(r_s[rows, :], axis=0, keepdims=True)
        for head in range(heads):
            at = slice(head * 128, (head + 1) * 128)
            first, second, s1, s2 = carry[head]
            first_b, second_b = first.astype(BF), second.astype(BF)
            states_ref[span, 0, head] = first_b
            states_ref[span, 1, head] = second_b
            states_ref[span, 2, head] = s1.astype(BF)
            states_ref[span, 3, head] = s2.astype(BF)
            kn = kn_s[rows, at]
            qn = qn_s[rows, at]
            both = _nn(jnp.concatenate([kn, qn], axis=0), first_b)
            both = both * _sig(both) if span == 7 else both
            if span < 7:
                pre = both[:CH]
                sig = _sig(both)
                act_both = both * sig
                sig_k = sig[:CH]
            else:
                act_both = both
            out_both = _nn(act_both.astype(BF), second_b)
            reads_ref[rows, at] = out_both[CH:].astype(BF)
            if span < 7:
                act = act_both[:CH]
                miss = (out_both[:CH] - v_s[rows, at]) * w_s[rows, at]
                miss_b = miss.astype(BF)
                grad_second = _tn(act.astype(BF), miss_b)
                grad_pre = _nt(miss_b, second_b) * sig_k * (1.0 + pre * (1.0 - sig_k))
                grad_first = _tn(kn, grad_pre.astype(BF))
                eta = means[:, 3 * head + 1 : 3 * head + 2]
                keep = 1.0 - 0.5 * means[:, 3 * head + 2 : 3 * head + 3]
                s1 = eta * s1 - grad_first
                s2 = eta * s2 - grad_second
                carry[head] = [keep * first + s1, keep * second + s2, s1, s2]
        send_state(span)
    send_reads()
    masks = _masks()
    for block in range(4):
        rows = slice(block * 128, (block + 1) * 128)
        target = pl.ds(_spot(place, block), 128)
        lse_all = jnp.zeros((128, 128), F32)
        for head in range(heads):
            at = slice(head * 128, (head + 1) * 128)
            qs = qs_s[rows, at]
            near = [
                (back, slice((block - back) * 128, (block - back + 1) * 128))
                for back in (2, 1, 0)
                if block - back >= 0
            ]
            read_b = reads_ref[rows, at]
            parts = _scores(
                qs, [(b, kb_s[r, at]) for b, r in near], read_b, pk_ref[head], block, length, masks
            )
            top = jnp.max(parts[0], axis=1, keepdims=True)
            wide = parts[1]
            for part in parts[2:]:
                wide = jnp.maximum(wide, part)
            top = jnp.maximum(top, jnp.max(wide, axis=1, keepdims=True))
            exps = [jnp.exp(part - top) for part in parts]
            wide = exps[1]
            for part in exps[2:]:
                wide = wide + part
            total = jnp.sum(exps[0], axis=1, keepdims=True) + jnp.sum(wide, axis=1, keepdims=True)
            acc = _nn(exps[0].astype(BF), pv_ref[head]) + _nn(exps[1].astype(BF), read_b)
            for (_, r), part in zip(near, exps[2:]):
                acc = acc + _nn(part.astype(BF), vb_s[r, at])
            mixed_ref[target, at] = (acc * (1.0 / total)).astype(BF)
            lse_all = jnp.where(
                _lane((128, 128), 1) == head, jnp.broadcast_to(top + jnp.log(total), (128, 128)), lse_all
            )
        lse_ref[rows, :] = lse_all


def _bwd_kernel(heads, blocks, where_ref, *rest):
    cots = rest[:4]
    qkv_hbm, pk_ref, pv_ref, mixed_ref, reads_ref, lse_ref, states_hbm = rest[4:11]
    weight_refs = rest[11 : 11 + blocks]
    rest = rest[11 + blocks :]
    dqkv_hbm, dpk_ref, dpv_ref, dm1_ref, dm2_ref, keep_ref, send_ref = rest[:7]
    cots_s, qkv_s, states_s, dqkv_s, dmix_s, project_s, rates_s, out_s, sems, more_sems = rest[7:17]
    scratch = rest[17:]
    step = weight_refs[0].shape[0] - 16
    wide = heads * 128
    every = pl.ds(0, step)
    out_copies = _copies(weight_refs, every, pl.ds(3 * wide, wide), out_s, sems.at[1])
    cot_copies = []
    for quarter, ref in enumerate(cots):
        copy = pltpu.make_async_copy(ref, cots_s.at[quarter], more_sems.at[quarter])
        copy.start()
        cot_copies.append(copy)
    qkv_copy = pltpu.make_async_copy(qkv_hbm, qkv_s, more_sems.at[4])
    qkv_copy.start()
    states_copy = pltpu.make_async_copy(states_hbm, states_s, more_sems.at[5])
    states_copy.start()
    project_copies = _copies(weight_refs, every, pl.ds(0, 3 * wide), project_s, sems.at[0])
    rates_s[16:128, :] = jnp.zeros((112, rates_s.shape[1]), BF)
    for k, block in enumerate(weight_refs):
        copy = pltpu.make_async_copy(
            block.at[pl.ds(step, 16), pl.ds(0, step)],
            rates_s.at[pl.ds(0, 16), pl.ds(k * step, step)],
            sems.at[2, k],
        )
        copy.start()
        project_copies.append(copy)
    for copy in out_copies:
        copy.wait()
    for quarter in range(4):
        cot_copies[quarter].wait()
        dmix_s[quarter * 128 : (quarter + 1) * 128, :] = _nn(cots_s[quarter], out_s[...])
    qkv_copy.wait()
    _mix_backward(
        heads,
        states_copy.wait,
        where_ref,
        qkv_s,
        pk_ref,
        pv_ref,
        mixed_ref,
        reads_ref,
        lse_ref,
        states_s,
        dmix_s,
        dqkv_s,
        dpk_ref,
        dpv_ref,
        dm1_ref,
        dm2_ref,
        *scratch,
    )
    dqkv_copy = pltpu.make_async_copy(dqkv_s, dqkv_hbm, more_sems.at[6])
    dqkv_copy.start()
    for copy in project_copies:
        copy.wait()
    for rows in (slice(256, 512), slice(0, 256)):
        grad = _nt(dqkv_s[rows, : 3 * wide], project_s[...])
        grad = grad + _nn(dqkv_s[rows, 3 * wide :], rates_s[...])
        if rows.start:
            send_ref[...] = grad.astype(BF)
        else:
            keep_ref[...] = grad.astype(BF)
    dqkv_copy.wait()


def _mix_backward(
    heads,
    wait_states,
    where_ref,
    qkv_ref,
    pk_ref,
    pv_ref,
    mixed_ref,
    reads_ref,
    lse_ref,
    states_ref,
    dmix_ref,
    dqkv_ref,
    dpk_ref,
    dpv_ref,
    dm1_ref,
    dm2_ref,
    qn_s,
    kn_s,
    qs_s,
    kb_s,
    v_s,
    vb_s,
    w_s,
    r_s,
    dq_s,
    dk_s,
    dv_s,
    dr_s,
    dqn_s,
    dkn_s,
    dz_s,
):
    place = where_ref[0]
    length = where_ref[1]
    width = heads * 128
    _load_rows(place, length, qkv_ref, heads, qn_s, kn_s, qs_s, kb_s, v_s, vb_s, w_s, r_s)
    masks = _masks()
    scale = 128 ** (-0.5)
    for head in range(heads):
        at = slice(head * 128, (head + 1) * 128)
        dpk = jnp.zeros((16, 128), F32)
        dpv = jnp.zeros((16, 128), F32)
        dk = [jnp.zeros((128, 128), F32)] * 4
        dv = [jnp.zeros((128, 128), F32)] * 4
        for block in range(4):
            rows = slice(block * 128, (block + 1) * 128)
            source = pl.ds(_spot(place, block), 128)
            qs = qs_s[rows, at]
            near = [
                (back, slice((block - back) * 128, (block - back + 1) * 128))
                for back in (2, 1, 0)
                if block - back >= 0
            ]
            read_b = reads_ref[rows, at]
            parts = _scores(
                qs, [(b, kb_s[r, at]) for b, r in near], read_b, pk_ref[head], block, length, masks
            )
            lse = lse_ref[rows, head : head + 1]
            probs = [jnp.exp(part - lse) for part in parts]
            dout = dmix_ref[source, at]
            dout_b = dout.astype(BF)
            dot = jnp.sum(dout * mixed_ref[source, at].astype(F32), axis=1, keepdims=True)
            values = [pv_ref[head], read_b] + [vb_s[r, at] for _, r in near]
            keys = [pk_ref[head], read_b] + [kb_s[r, at] for _, r in near]
            ds_b = [
                (p * (_nt(dout_b, val) - dot)).astype(BF) for p, val in zip(probs, values)
            ]
            probs_b = [p.astype(BF) for p in probs]
            dq = _nn(ds_b[0], keys[0])
            for d, key in zip(ds_b[1:], keys[1:]):
                dq = dq + _nn(d, key)
            dq_s[rows, at] = dq * scale
            dpk = dpk + _tn(ds_b[0], qs)
            dpv = dpv + _tn(probs_b[0], dout_b)
            dr_s[rows, at] = _tn(ds_b[1], qs) + _tn(probs_b[1], dout_b)
            for (back, _), d, p in zip(near, ds_b[2:], probs_b[2:]):
                dk[block - back] = dk[block - back] + _tn(d, qs)
                dv[block - back] = dv[block - back] + _tn(p, dout_b)
            if block >= 2:
                dk_s[(block - 2) * 128 : (block - 1) * 128, at] = dk[block - 2]
                dv_s[(block - 2) * 128 : (block - 1) * 128, at] = dv[block - 2]
        for block in (2, 3):
            rows = slice(block * 128, (block + 1) * 128)
            dk_s[rows, at] = dk[block]
            dv_s[rows, at] = dv[block]
        dpk_ref[head] = dpk
        dpv_ref[head] = dpv
    wait_states()
    zero = jnp.zeros((128, 128), F32)
    carry = [[zero, zero, zero, zero] for _ in range(heads)]
    lanes = _lane((CH, 128), 1)
    for span in range(7, -1, -1):
        rows = slice(span * CH, (span + 1) * CH)
        means = jnp.mean(r_s[rows, :], axis=0, keepdims=True)
        dr_row = jnp.zeros((CH, 128), F32)
        live = (span * CH + _lane((CH, 1), 0) < length).astype(F32)
        for head in range(heads):
            at = slice(head * 128, (head + 1) * 128)
            a1, a2, b1, b2 = carry[head]
            first_b = states_ref[span, 0, head]
            second_b = states_ref[span, 1, head]
            kn = kn_s[rows, at]
            qn = qn_s[rows, at]
            dread_b = dr_s[rows, at].astype(BF)
            both = _nn(jnp.concatenate([kn, qn], axis=0), first_b)
            sig_both = _sig(both)
            act_both = both * sig_both
            slope_both = sig_both * (1.0 + both * (1.0 - sig_both))
            act_b = act_both.astype(BF)
            db_b = (_nt(dread_b, second_b) * slope_both[CH:]).astype(BF)
            if span == 7:
                dqn_s[rows, at] = _nt(db_b, first_b)
                dkn_s[rows, at] = jnp.zeros((CH, 128), F32)
                carry[head] = [_tn(qn, db_b), _tn(act_b[CH:], dread_b), zero, zero]
                continue
            eta = means[:, 3 * head + 1 : 3 * head + 2]
            keep = 1.0 - 0.5 * means[:, 3 * head + 2 : 3 * head + 3]
            pre, sig, slope = both[:CH], sig_both[:CH], slope_both[:CH]
            bend = sig * (1.0 - sig) * (2.0 + pre * (1.0 - 2.0 * sig))
            u_b = act_b[:CH]
            w = w_s[rows, at]
            e = _nn(u_b, second_b) - v_s[rows, at]
            m_b = (e * w).astype(BF)
            p = _nt(m_b, second_b)
            g_b = (p * slope).astype(BF)
            ds1 = b1 + a1
            ds2 = b2 + a2
            dg1_b = (-ds1).astype(BF)
            dg2_b = (-ds2).astype(BF)
            x1 = _nn(kn, dg1_b)
            dp_b = (x1 * slope).astype(BF)
            dm = _nn(dp_b, second_b) + _nn(u_b, dg2_b)
            de = dm * w
            de_b = de.astype(BF)
            du = _nt(m_b, dg2_b) + _nt(de_b, second_b)
            da = x1 * p * bend + du * slope
            da_b = da.astype(BF)
            back = _nt(jnp.concatenate([da_b, db_b], axis=0), first_b)
            dkn_s[rows, at] = _nt(g_b, dg1_b) + back[:CH]
            dqn_s[rows, at] = back[CH:]
            dv_s[rows, at] = dv_s[rows, at] - de
            new1 = keep * a1 + _tn(
                jnp.concatenate([kn, qn], axis=0), jnp.concatenate([da_b, db_b], axis=0)
            )
            new2 = (
                keep * a2
                + _tn(act_b, jnp.concatenate([de_b, dread_b], axis=0))
                + _tn(dp_b, m_b)
            )
            prev1 = states_ref[span, 2, head].astype(F32)
            prev2 = states_ref[span, 3, head].astype(F32)
            deta = jnp.sum(
                jnp.sum(ds1 * prev1 + ds2 * prev2, axis=0, keepdims=True), axis=1, keepdims=True
            )
            dkeep = jnp.sum(
                jnp.sum(a1 * first_b.astype(F32) + a2 * second_b.astype(F32), axis=0, keepdims=True),
                axis=1,
                keepdims=True,
            )
            dw = jnp.sum(dm * e, axis=1, keepdims=True) * live * (2.0 / (CH * 128))
            dr_row = jnp.where(lanes == 3 * head, jnp.broadcast_to(dw, (CH, 128)), dr_row)
            dr_row = jnp.where(
                lanes == 3 * head + 1, jnp.broadcast_to(deta * (1.0 / CH), (CH, 128)), dr_row
            )
            dr_row = jnp.where(
                lanes == 3 * head + 2, jnp.broadcast_to(dkeep * (-0.5 / CH), (CH, 128)), dr_row
            )
            carry[head] = [new1, new2, eta * ds1, eta * ds2]
        rates = r_s[rows, :]
        dz_s[rows, :] = dr_row * rates * (1.0 - rates)
    for head in range(heads):
        dm1_ref[head] = carry[head][0]
        dm2_ref[head] = carry[head][1]
    for quarter in range(4):
        source = pl.ds(_spot(place, quarter), 128)
        here = slice(quarter * 128, (quarter + 1) * 128)
        dqkv_ref[source, 3 * width :] = dz_s[here, :].astype(BF)
        for head in range(heads):
            at = slice(head * 128, (head + 1) * 128)
            for part, grad_s, norm_s in ((0, dq_s, dqn_s), (1, dk_s, dkn_s)):
                col = slice(part * width + head * 128, part * width + (head + 1) * 128)
                raw = qkv_ref[source, col].astype(F32)
                inverse = _scale_of(raw)
                normed = raw * inverse
                dn = norm_s[here, at]
                inner = jnp.mean(dn * normed, axis=-1, keepdims=True)
                dqkv_ref[source, col] = (
                    grad_s[here, at] + inverse * (dn - normed * inner)
                ).astype(BF)
            col = slice(2 * width + head * 128, 2 * width + (head + 1) * 128)
            dqkv_ref[source, col] = dv_s[here, at].astype(BF)


def _row_scratch(heads):
    wide = heads * 128
    return [
        pltpu.VMEM((512, wide), BF),
        pltpu.VMEM((512, wide), BF),
        pltpu.VMEM((512, wide), BF),
        pltpu.VMEM((512, wide), BF),
        pltpu.VMEM((512, wide), F32),
        pltpu.VMEM((512, wide), BF),
        pltpu.VMEM((512, wide), F32),
        pltpu.VMEM((512, 128), F32),
    ]


_VM = pl.BlockSpec(memory_space=pltpu.VMEM)
_SM = pl.BlockSpec(memory_space=pltpu.SMEM)


def _any(count):
    return [pl.BlockSpec(memory_space=pl.ANY)] * count


def _call(kernel, operands, in_specs, after, **settings):
    count = len(operands)
    more = len(after)

    def body(*refs):
        kernel(*refs[:count], *refs[count + more :])

    return pl.pallas_call(body, in_specs=[*in_specs, *_any(more)], **settings)(*operands, *after)


def mix_forward(where, quarters, batch, weights, pk, pv, m1, m2, after=()):
    heads = pk.shape[0]
    wide = heads * 128
    blocks = len(weights)
    step = weights[0].shape[0] - 16
    width = blocks * step
    local = quarters[0].shape[2]
    extra, token, mixed, lse, keep, send, first, qkv, reads, states = _call(
        partial(_fwd_kernel, heads, blocks, batch),
        (where, *quarters, pk, pv, m1, m2, *weights),
        [_SM] + _any(4) + [_VM] * 4 + _any(blocks),
        after,
        name="mix_forward",
        out_shape=(
            _f32(16, width),
            _f32(128, width),
            _bf16(512, wide),
            _f32(512, 128),
            _bf16(256, width),
            _bf16(256, width),
            _bf16(512, width),
            _bf16(512, 3 * wide + 128),
            _bf16(512, wide),
            _bf16(8, 4, heads, 128, 128),
        ),
        out_specs=(*[_VM] * 6, *_any(4)),
        scratch_shapes=[
            pltpu.VMEM((4, blocks, local, width), BF),
            pltpu.VMEM((512, width), BF),
            pltpu.VMEM((512, 3 * wide + 128), F32),
            pltpu.VMEM((512, 3 * wide + 128), BF),
            pltpu.VMEM((512, wide), BF),
            pltpu.VMEM((8, 4, heads, 128, 128), BF),
            pltpu.VMEM((width, 3 * wide), BF),
            pltpu.VMEM((128, width), BF),
            pltpu.VMEM((width, wide), BF),
            pltpu.SemaphoreType.DMA((3, blocks)),
            pltpu.SemaphoreType.DMA((4,)),
            pltpu.SemaphoreType.DMA((3,)),
            pltpu.SemaphoreType.DMA((8,)),
        ]
        + _row_scratch(heads),
        compiler_params=pltpu.CompilerParams(vmem_limit_bytes=60 * 1024 * 1024),
        cost_estimate=pl.CostEstimate(flops=10**5, bytes_accessed=10**4, transcendentals=0),
    )
    return first, extra, token, qkv, mixed, reads, lse, states, keep, send


def mix_backward(where, cots, saved, weights, after=()):
    pk = saved[1]
    heads = pk.shape[0]
    wide = heads * 128
    blocks = len(weights)
    step = weights[0].shape[0] - 16
    width = blocks * step
    return _call(
        partial(_bwd_kernel, heads, blocks),
        (where, *cots, *saved, *weights),
        [_SM] + _any(5) + [_VM] * 5 + _any(1 + blocks),
        after,
        name="mix_backward",
        out_shape=(
            _bf16(512, 3 * wide + 128),
            _f32(heads, 16, 128),
            _f32(heads, 16, 128),
            _f32(heads, 128, 128),
            _f32(heads, 128, 128),
            _bf16(256, width),
            _bf16(256, width),
        ),
        out_specs=(*_any(1), *[_VM] * 6),
        scratch_shapes=[
            pltpu.VMEM((4, 128, width), BF),
            pltpu.VMEM((512, 3 * wide + 128), BF),
            pltpu.VMEM((8, 4, heads, 128, 128), BF),
            pltpu.VMEM((512, 3 * wide + 128), BF),
            pltpu.VMEM((512, wide), F32),
            pltpu.VMEM((width, 3 * wide), BF),
            pltpu.VMEM((128, width), BF),
            pltpu.VMEM((width, wide), BF),
            pltpu.SemaphoreType.DMA((3, blocks)),
            pltpu.SemaphoreType.DMA((7,)),
        ]
        + _row_scratch(heads)
        + [pltpu.VMEM((512, wide), F32)] * 6
        + [pltpu.VMEM((512, 128), F32)],
        compiler_params=pltpu.CompilerParams(vmem_limit_bytes=60 * 1024 * 1024),
        cost_estimate=pl.CostEstimate(flops=7 * 10**9, bytes_accessed=10**4, transcendentals=0),
    )


def _feed_kernel(blocks, picks, cols, batch, *rest):
    seconds = rest[:4]
    cots = rest[4:8]
    weight_refs = rest[8 : 8 + blocks]
    (
        hidden_ref,
        gate_ref,
        up_ref,
        keep_ref,
        send_ref,
        feed_keep_ref,
        feed_send_ref,
        gate_s,
        up_s,
        down_s,
        sems,
    ) = rest[8 + blocks :]
    step = weight_refs[0].shape[-2]
    copies = [
        _copies(weight_refs, pl.ds(0, step), pl.ds(w * cols, cols), target, sems.at[w], picks)
        for w, target in enumerate((gate_s, up_s, down_s))
    ]
    for part in range(2):
        rows = slice(part * 256, (part + 1) * 256)
        left = jnp.concatenate([seconds[2 * part][...], seconds[2 * part + 1][...]], axis=0)
        cot = jnp.concatenate([cots[2 * part][batch], cots[2 * part + 1][batch]], axis=0)
        if part == 0:
            for copy in copies[0]:
                copy.wait()
        gate = _nn(left, gate_s[...])
        if part == 0:
            for copy in copies[1]:
                copy.wait()
        up = _nn(left, up_s[...])
        if part == 0:
            for copy in copies[2]:
                copy.wait()
        grad = _nn(cot, down_s[...])
        sig = _sig(gate)
        act = gate * sig
        hidden = (act * up).astype(BF)
        gate_grad = (grad * up * (sig + act * (1.0 - sig))).astype(BF)
        up_grad = (grad * act).astype(BF)
        hidden_ref[rows, :] = hidden
        gate_ref[rows, :] = gate_grad
        up_ref[rows, :] = up_grad
        back = _nt(gate_grad, gate_s[...]) + _nt(up_grad, up_s[...])
        feed = _nt(hidden, down_s[...])
        if part == 0:
            keep_ref[...] = back.astype(BF)
            feed_keep_ref[...] = feed.astype(BF)
        else:
            send_ref[...] = back.astype(BF)
            feed_send_ref[...] = feed.astype(BF)


def feed_forward(seconds, cots, batch, weights, after=()):
    blocks = len(weights)
    picks = tuple(pick for _, pick in weights)
    weights = [array for array, _ in weights]
    step = weights[0].shape[-2]
    cols = weights[0].shape[-1] // 3
    width = blocks * step
    return _call(
        partial(_feed_kernel, blocks, picks, cols, batch),
        (*seconds, *cots, *weights),
        [_VM] * 8 + _any(blocks),
        after,
        name="feed_forward",
        out_shape=(
            jax.ShapeDtypeStruct((512, cols), BF),
            jax.ShapeDtypeStruct((512, cols), BF),
            jax.ShapeDtypeStruct((512, cols), BF),
            jax.ShapeDtypeStruct((256, width), BF),
            jax.ShapeDtypeStruct((256, width), BF),
            jax.ShapeDtypeStruct((256, width), BF),
            jax.ShapeDtypeStruct((256, width), BF),
        ),
        out_specs=(_VM,) * 7,
        scratch_shapes=[pltpu.VMEM((width, cols), BF)] * 3
        + [pltpu.SemaphoreType.DMA((3, blocks))],
        compiler_params=pltpu.CompilerParams(vmem_limit_bytes=48 * 1024 * 1024),
        cost_estimate=pl.CostEstimate(flops=35 * 10**8, bytes_accessed=10**4, transcendentals=0),
    )


def _grad_kernel(groups, counts, picks, keep, sends, *rest):
    total = sum(counts)
    row_refs = rest[:total]
    grad_refs = rest[total : total + len(counts)]
    outs = rest[total + len(counts) :]
    keep_refs, send_refs = outs[: len(keep)], outs[len(keep) :]
    targets = [
        (k, ref, place) for ref, some in zip(send_refs, sends) for place, k in enumerate(some)
    ]
    targets += [(k, ref, None) for ref, k in zip(keep_refs, keep)]
    step = outs[0].shape[-2]
    for k, out_ref, place in targets:
        at = slice(k * step, (k + 1) * step)
        start = 0
        index = 0
        term_at = 0
        for terms in groups:
            value = None
            for count, grad_ref in zip(
                counts[term_at : term_at + terms], grad_refs[term_at : term_at + terms]
            ):
                pieces = []
                for i in range(index, index + count):
                    ref, pick = row_refs[i], picks[i]
                    pieces.append(ref[:, at] if pick is None else ref[pick, :, at])
                index += count
                left = pieces[0] if count == 1 else jnp.concatenate(pieces, axis=0)
                term = _tn(left, grad_ref[...])
                value = term if value is None else value + term
            cols = slice(start, start + grad_refs[term_at].shape[1])
            start = cols.stop
            term_at += terms
            if place is None:
                out_ref[:, cols] = value.astype(BF)
            else:
                out_ref[place, :, cols] = value.astype(BF)


def weight_gradient(groups, blocks, keep, sends, flops=None, after=()):
    terms = [term for group in groups for term in group]
    width = terms[0][0][0][0].shape[-1]
    cols = sum(group[0][1].shape[1] for group in groups)
    step = width // blocks
    pieces = [piece for rows, _ in terms for piece in rows]
    grads = [grad for _, grad in terms]
    return _call(
        partial(
            _grad_kernel,
            tuple(len(group) for group in groups),
            tuple(len(rows) for rows, _ in terms),
            tuple(pick for _, pick in pieces),
            tuple(keep),
            tuple(sends),
        ),
        (*[array for array, _ in pieces], *grads),
        [_VM] * (len(pieces) + len(grads)),
        after,
        name="weight_gradient",
        out_shape=(
            *[_bf16(step, cols)] * len(keep),
            *[_bf16(len(some), step, cols) for some in sends],
        ),
        out_specs=(_VM,) * (len(keep) + len(sends)),
        compiler_params=pltpu.CompilerParams(vmem_limit_bytes=48 * 1024 * 1024),
        cost_estimate=pl.CostEstimate(
            flops=flops or 4 * 10**8 * (len(keep) + sum(len(some) for some in sends)),
            bytes_accessed=10**4,
            transcendentals=0,
        ),
    )


def _small(name, function, shapes, scalars, values, after, flops=10**5):
    return _call(
        function,
        (*scalars, *values),
        [_SM] * len(scalars) + [_VM] * len(values),
        after,
        name=name,
        out_shape=shapes,
        out_specs=(_VM,) * len(shapes),
        cost_estimate=pl.CostEstimate(flops=flops, bytes_accessed=10**4, transcendentals=0),
        compiler_params=pltpu.CompilerParams(vmem_limit_bytes=32 * 1024 * 1024),
    )


def _f32(*shape):
    return jax.ShapeDtypeStruct(shape, F32)


def _bf16(*shape):
    return jax.ShapeDtypeStruct(shape, BF)


def _add_kernel(keep_ref, got_ref, own_ref, other_ref):
    total = keep_ref[...].astype(F32) + got_ref[...].astype(F32)
    own_ref[...] = total[0:128, :]
    other_ref[...] = total[128:256, :].astype(BF)


def add_core(keep, got, after=()):
    width = keep.shape[1]
    return _small("add_core", _add_kernel, (_f32(128, width), _bf16(128, width)), (), (keep, got), after)


def _norm_kernel(rows_ref, own_ref, column_ref, gain_ref, second_ref, residual_ref, inverse_ref):
    residual = rows_ref[...] + own_ref[...] + column_ref[...].astype(F32)
    inverse = _scale_of(residual)
    second_ref[...] = (residual * inverse * gain_ref[...]).astype(BF)
    residual_ref[...] = residual
    inverse_ref[...] = jnp.broadcast_to(inverse, (128, 128))


def second_norm(rows, own, column, gain, flops=10**5, after=()):
    width = rows.shape[1]
    return _small(
        "second_norm",
        _norm_kernel,
        (_bf16(128, width), _f32(128, width), _f32(128, 128)),
        (),
        (rows, own, column, gain),
        after,
        flops,
    )


def _norm_grad(grad, normed, inverse, gain):
    scaled = grad * gain
    return inverse * (scaled - normed * jnp.mean(scaled * normed, axis=-1, keepdims=True))


def _second_back_kernel(batch, own_ref, column_ref, cot_ref, residual_ref, inverse_ref, gain_ref, low_ref, out_ref, sum_ref):
    grad = own_ref[...] + column_ref[...].astype(F32)
    inverse = inverse_ref[:, 0:1]
    normed = residual_ref[...] * inverse
    out = cot_ref[batch] + _norm_grad(grad, normed, inverse, gain_ref[...])
    low_ref[...] = out.astype(BF)
    out_ref[...] = out
    sum_ref[...] = jnp.sum(grad * normed, axis=0, keepdims=True)


def second_back(batch, own, column, cots, residual, inverse, gain, after=()):
    width = own.shape[1]
    return _small(
        "second_back",
        partial(_second_back_kernel, batch),
        (_bf16(128, width), _f32(128, width), _f32(1, width)),
        (),
        (own, column, cots, residual, inverse, gain),
        after,
        3 * 10**9,
    )


def _place(where_ref, k, step):
    return pl.ds(pl.multiple_of(where_ref[2 + k] * step, step), step)


def _live(where_ref):
    return (where_ref[0] * 128 + _lane((128, 1), 0) < where_ref[1]).astype(F32)


def _cots_kernel(blocks, where_a, where_b, scale_ref, got_ref, rows_ref, low_ref):
    width = got_ref.shape[3]
    step = width // blocks
    for b, where_ref in enumerate((where_a, where_b)):
        factor = _live(where_ref) * scale_ref[b]
        for k in range(blocks):
            piece = got_ref[:, b, :, _place(where_ref, k, step)].reshape(128, step).astype(F32)
            piece = piece * factor
            rows_ref[b, :, k * step : (k + 1) * step] = piece
            low_ref[b, :, k * step : (k + 1) * step] = piece.astype(BF)


def take_cots(wheres, scales, got, flops=10**5, after=()):
    blocks, batches, _, width = got.shape
    return _small(
        "take_cots",
        partial(_cots_kernel, blocks),
        (_f32(batches, 128, width), _bf16(batches, 128, width)),
        (*wheres, scales),
        (got,),
        after,
        flops,
    )


def _finish_kernel(blocks, where_a, where_b, own_a, own_b, column_ref, res_a, res_b, out_ref):
    width = column_ref.shape[2]
    step = width // blocks
    for b, (where_ref, own, res) in enumerate(((where_a, own_a, res_a), (where_b, own_b, res_b))):
        rows = _live(where_ref) * (res[...] + own[...] + column_ref[b].astype(F32))
        rows = rows.astype(BF)
        for k in range(blocks):
            piece = rows[:, k * step : (k + 1) * step].reshape(blocks, 128 // blocks, step)
            out_ref[:, b, :, _place(where_ref, k, step)] = piece


def finish_rows(blocks, wheres, owns, column, residuals, flops=10**5, after=()):
    width = column.shape[2]
    return _small(
        "finish_rows",
        partial(_finish_kernel, blocks),
        (_bf16(blocks, 2, 128 // blocks, width),),
        wheres,
        (*owns, column, *residuals),
        after,
        flops,
    )[0]


def _token_grad(own_ref, column_ref, rows_ref, back_ref, gain_ref):
    grad = own_ref[...] + column_ref[...].astype(F32)
    rows = rows_ref[...]
    inverse = _scale_of(rows)
    normed = rows * inverse
    out = back_ref[...] + _norm_grad(grad, normed, inverse, gain_ref[...])
    return out.astype(BF), jnp.sum(grad * normed, axis=0, keepdims=True)


def _first_back_kernel(own_ref, column_ref, rows_ref, back_ref, gain_ref, low_ref, sum_ref):
    low_ref[...], sum_ref[...] = _token_grad(own_ref, column_ref, rows_ref, back_ref, gain_ref)


def first_back(own, column, rows, back, gain, after=()):
    width = own.shape[1]
    return _small(
        "first_back",
        _first_back_kernel,
        (_bf16(128, width), _f32(1, width)),
        (),
        (own, column, rows, back, gain),
        after,
    )


def _last_kernel(blocks, where_ref, own_ref, column_ref, rows_ref, back_ref, gain_ref, low_ref, sum_a, two_a, two_b, out_ref, gains_ref):
    width = own_ref.shape[1]
    step = width // blocks
    low, total = _token_grad(own_ref, column_ref, rows_ref, back_ref, gain_ref)
    total = total + sum_a[...]
    two = two_a[...] + two_b[...]
    first = low_ref[...]
    gains_ref[...] = jnp.zeros((8, width), F32)
    for k in range(blocks):
        at = slice(k * step, (k + 1) * step)
        place = _place(where_ref, k, step)
        out_ref[:, 0, :, place] = first[:, at].reshape(blocks, 128 // blocks, step)
        out_ref[:, 1, :, place] = low[:, at].reshape(blocks, 128 // blocks, step)
        gains_ref[0:1, place] = total[:, at]
        gains_ref[1:2, place] = two[:, at]


def last_rows(blocks, where, own, column, rows, back, gain, low, sum_a, two_a, two_b, after=()):
    width = own.shape[1]
    return _small(
        "last_rows",
        partial(_last_kernel, blocks),
        (_bf16(blocks, 2, 128 // blocks, width), _f32(8, width)),
        (where,),
        (own, column, rows, back, gain, low, sum_a, two_a, two_b),
        after,
    )


def _ring_kernel(indices, passing, splits, *rest):
    count = len(indices)
    keeps, gots = rest[:count], rest[count : 2 * count]
    passed_ref = rest[2 * count] if passing else None
    outs = rest[2 * count + passing :]
    start = 0
    done = 0
    for keep, got, index, sizes in zip(keeps, gots, indices, splits):
        cols = keep.shape[1]
        total = keep[...].astype(F32) + got[index].astype(F32)
        if passing:
            total = total + passed_ref[:, start : start + cols].astype(F32)
        if sizes is None:
            outs[0][:, start : start + cols] = total.astype(BF)
        else:
            for offset, size, turned in sizes:
                piece = total[:, offset : offset + -(-size // 128) * 128]
                if turned:
                    outs[done][...] = piece.T[:size]
                else:
                    outs[done][...] = piece[:, :size]
                done += 1
        start += cols


def ring_step(keeps, gots, indices, passed, splits=None, after=()):
    step = keeps[0].shape[0]
    cols = sum(k.shape[1] for k in keeps)
    if splits is None:
        shapes = (_bf16(step, cols),)
        splits = (None,) * len(keeps)
    else:
        shapes = tuple(
            _f32(size, step) if turned else _f32(step, size)
            for sizes in splits
            for _, size, turned in sizes
        )
    return _small(
        "ring_step",
        partial(_ring_kernel, tuple(indices), len(passed), tuple(splits)),
        shapes,
        (),
        (*keeps, *gots, *passed),
        after,
    )


def _hop_kernel(value_ref, got_ref, out_ref):
    out_ref[...] = value_ref[...] + got_ref[...].astype(F32)


def add_hop(value, got, after=()):
    return _small("add_hop", _hop_kernel, (_f32(*value.shape),), (), (value, got), after)[0]


def _join_kernel(*refs):
    *grads, out_ref = refs
    count = len(grads) // 2
    start = 0
    for one, two in zip(grads[:count], grads[count:]):
        for head in range(one.shape[0]):
            rows = one.shape[1]
            out_ref[start : start + rows, :] = one[head] + two[head]
            start += rows


def join_sums(one, two, after=()):
    rows = sum(g.shape[0] * g.shape[1] for g in one)
    return _small("join_sums", _join_kernel, (_f32(rows, 128),), (), (*one, *two), after)[0]


def _tick_kernel(out_ref):
    out_ref[...] = jnp.zeros((8, 128), F32)


def tick(after=()):
    return _small("tick", _tick_kernel, (_f32(8, 128),), (), (), after, 4 * 10**9)[0]


DP = ("z", "x")


def _swap(value, axis):
    return lax.ppermute(value, axis, [(0, 1), (1, 0)])


BLOCKS = 8
LONG = 4 * 10**9
STEP = 128
DOWN = (1, 2, 3, 0)
RING = [(0, 1), (1, 2), (2, 3), (3, 0)]
BACK = [(1, 0), (2, 1), (3, 2), (0, 3)]


def _ring_sized():
    return lax.axis_size("z") == 4


def _block_ids():
    if not _ring_sized():
        return jnp.arange(BLOCKS, dtype=jnp.int32)
    z = lax.axis_index("z")
    x = lax.axis_index("x")
    zs = jnp.stack([(z + 4 - i) % 4 for i in DOWN])
    return jnp.concatenate([2 * zs + x, 2 * zs + (1 - x)]).astype(jnp.int32)


class _Order:
    def __init__(self):
        self.last = []

    def __call__(self, function, *values, need=()):
        result = function(*values, after=(*self.last, *need))
        self.last = [min(jax.tree.leaves(result), key=lambda leaf: leaf.size)]
        return result


def _ring(block):
    return lax.ppermute(block, "z", RING)


def _in_order(ring, across):
    return [ring[i] for i in DOWN] + [across[i] for i in DOWN]


def _scatter_whole(keep, *sends):
    whole = jnp.concatenate([keep, *sends]).reshape(BLOCKS * STEP, -1)
    return lax.psum_scatter(whole, DP, scatter_dimension=0, tiled=True).astype(F32)


def _quarters(own):
    column = _swap(own, "y")
    return [own, column, _swap(own, "c"), _swap(column, "c")]


def per_device(
    tokens,
    grad_output,
    query_weight,
    key_weight,
    value_weight,
    rates_weight,
    out_weight,
    gate_weight,
    up_weight,
    down_weight,
    norm1_gain,
    norm2_gain,
    persist_key,
    persist_value,
    memory_first,
    memory_second,
    seq_lengths,
    deal,
):
    devices = lax.axis_size("z") * lax.axis_size("x")
    dp_index = lax.axis_index("z") * lax.axis_size("x") + lax.axis_index("x")
    place = lax.axis_index("y") * 2 + lax.axis_index("c")
    seq_count = seq_lengths.shape[0]
    batches = seq_count // devices
    local_rows = tokens.shape[2]
    width = tokens.shape[3]
    quarter = local_rows * devices
    rows_of = query_weight.shape[0]
    head_cols = query_weight.shape[1]
    rate_cols = rates_weight.shape[1]
    hidden_cols = gate_weight.shape[1]

    batch_of = deal // devices
    batch_ids = jnp.arange(batches, dtype=jnp.int32)
    batch_tokens = jnp.sum(
        jnp.where(batch_of[None, :] == batch_ids[:, None], seq_lengths[None, :], 0), axis=1
    ).astype(F32)
    batch_scale = jnp.sum(seq_lengths).astype(F32) / (batches * batch_tokens)
    span = range(batches)
    my_seqs = [batches * dp_index + b for b in span]
    lengths = [seq_lengths[s] for s in my_seqs]
    scales = [batch_scale[batch_of[s]] for s in my_seqs]
    ring_sized = _ring_sized()
    ids = _block_ids()
    where = [
        jnp.concatenate([jnp.stack([place, lengths[b]]).astype(jnp.int32), ids]) for b in span
    ]
    scale = jnp.stack(scales)

    def deal_in(array):
        part = array.reshape(devices, batches, local_rows, width)
        part = lax.all_to_all(part, DP, split_axis=0, concat_axis=0, tiled=True)
        if local_rows * BLOCKS == quarter:
            return part
        part = part.transpose(1, 0, 2, 3).reshape(batches, BLOCKS, quarter // BLOCKS, width)
        return part.transpose(1, 0, 2, 3)

    def deal_out(part):
        if local_rows * BLOCKS != quarter:
            part = part.transpose(1, 0, 2, 3).reshape(batches, devices, local_rows, width)
            part = part.transpose(1, 0, 2, 3)
        part = lax.all_to_all(part, DP, split_axis=0, concat_axis=0, tiled=True)
        return part.reshape(seq_count, 1, local_rows, width)

    mix_shard = jnp.concatenate([query_weight, key_weight, value_weight, out_weight], axis=1)
    extra = jnp.concatenate(
        [
            rates_weight.T,
            norm1_gain[None],
            norm2_gain[None],
            jnp.zeros((16 - rate_cols - 2, rows_of), BF),
        ]
    )
    pad = -hidden_cols % 128
    feed_shard = jnp.concatenate(
        [jnp.pad(w, ((0, 0), (0, pad))) for w in (gate_weight, up_weight, down_weight)], axis=1
    )
    got_tokens = deal_in(tokens)

    run = _Order()

    def mix_of(b, wheres, need=()):
        return run(
            mix_forward,
            wheres[b],
            quarters,
            b,
            mix_weights,
            persist_key,
            persist_value,
            memory_first,
            memory_second,
            need=need,
        )

    if ring_sized:
        extra = jnp.pad(extra, ((0, 0), (0, mix_shard.shape[1] - rows_of)))
        mix0 = jnp.concatenate([mix_shard, extra], axis=0)
        mix1 = _ring(mix0)
        mix_across0 = _swap(mix0, "x")
        mix1, mix_across0, feed0, scale, *where = lax.optimization_barrier(
            (mix1, mix_across0, feed_shard, scale, *where)
        )
        mix2 = _ring(mix1)
        mix_across1 = _swap(mix1, "x")
        mix2, mix_across1 = lax.optimization_barrier((mix2, mix_across1))
        mix3 = _ring(mix2)
        mix_across2 = _swap(mix2, "x")
        quarters = _quarters(got_tokens)
        mix3, mix_across2, feed0, cots_in = lax.optimization_barrier(
            (mix3, mix_across2, feed0, grad_output)
        )
        got_cots = deal_in(cots_in)
        mix_across3 = _swap(mix3, "x")
        feed1 = _ring(feed0)
        feed3 = lax.ppermute(feed0, "z", BACK)
        feed0, mix_across3 = lax.optimization_barrier((feed0, mix_across3))
        feed_across0 = _swap(feed0, "x")
        mix_weights = _in_order(
            [mix0, mix1, mix2, mix3], [mix_across0, mix_across1, mix_across2, mix_across3]
        )
    else:
        mix_full = lax.all_gather(mix_shard, DP, axis=0, tiled=True)
        extra = lax.all_gather(extra, DP, axis=1, tiled=True)
        extra = jnp.pad(
            extra.reshape(16, BLOCKS, STEP), ((0, 0), (0, 0), (0, mix_shard.shape[1] - STEP))
        )
        mix_weights = [
            jnp.concatenate([mix_full[k * STEP : (k + 1) * STEP], extra[:, k]])
            for k in range(BLOCKS)
        ]
        feed_full = lax.all_gather(feed_shard, DP, axis=0, tiled=True)
        feed_weights = [(feed_full[k * STEP : (k + 1) * STEP], None) for k in range(BLOCKS)]
        quarters = _quarters(got_tokens)
        got_cots = deal_in(grad_output)

    mix_a = mix_of(0, where)
    if ring_sized:
        feed1, feed3, *mix_a = lax.optimization_barrier((feed1, feed3, *mix_a))
    gain_one = mix_a[1][rate_cols : rate_cols + 1]
    gain_two = mix_a[1][rate_cols + 1 : rate_cols + 2]
    core_a = _swap(mix_a[9], "c")
    early = []
    cot_rows, cot_own = run(
        take_cots, where, scale, got_cots, LONG, need=[feed_across0] if ring_sized else []
    )
    if ring_sized:
        feed2 = _ring(feed1)
        feed_across13 = _swap(jnp.stack([feed1, feed3]), "x")
        early = [feed2, feed_across13]
    own_a, other_a = run(add_core, mix_a[8], core_a)
    column_a = _swap(other_a, "y")
    cot_column = _swap(cot_own, "y")
    cot_core = _swap(cot_own, "c")
    mix_b = mix_of(1, where)
    mixes = [mix_a, mix_b]
    core_b = _swap(mix_b[9], "c")
    token_rows = [m[2] for m in mixes]
    second_a, residual_a, inverse_a = run(
        second_norm, token_rows[0], own_a, column_a, gain_two, LONG, need=[*early, cot_column]
    )
    early = []
    if ring_sized:
        feed_across2 = _swap(feed2, "x")
        feed_weights = _in_order(
            [(feed0, None), (feed1, None), (feed2, None), (feed3, None)],
            [(feed_across0, None), (feed_across13, 0), (feed_across2, None), (feed_across13, 1)],
        )
    second_a = _quarters(second_a)
    own_b, other_b = run(add_core, mix_b[8], core_b, need=[second_a[2]])
    column_b = _swap(other_b, "y")
    cots = [cot_own, cot_column, cot_core, _swap(cot_column, "c")]
    second_b, residual_b, inverse_b = run(
        second_norm, token_rows[1], own_b, column_b, gain_two, need=[*early, cots[3]]
    )
    second_b = _quarters(second_b)
    second = [second_a, second_b]
    residual = [residual_a, residual_b]

    def feed_of(b, need=()):
        return run(feed_forward, second[b], cots, b, feed_weights, need=need)

    feed_a = feed_of(0)
    core_a = _swap(feed_a[4], "c")
    run(tick, need=second_b[1:2])
    own_a, other_a = run(add_core, feed_a[3], core_a)
    column_a = _swap(other_a, "y")
    feed_b = feed_of(1)
    feeds = [feed_a, feed_b]
    core_b = _swap(feed_b[4], "c")
    def plain(pieces):
        return [(piece, None) for piece in pieces]

    def across(part):
        return _swap(part, "x") if ring_sized else part

    feed_groups = [
        [(plain(second[b]), feeds[b][1]) for b in span],
        [(plain(second[b]), feeds[b][2]) for b in span],
        [([(piece, b) for piece in cots], feeds[b][0]) for b in span],
    ]
    class Sum:
        def __init__(self, keeps, gots, splits):
            self.keeps = keeps
            self.gots = gots
            self.splits = splits
            self.place = 0
            self.passed = []
            self.results = None

        def step(self, need=()):
            place = self.place
            self.place += 1
            final = place == 3
            if not ring_sized:
                if final:
                    self.results = [
                        whole[:, at : at + size].T if turned else whole[:, at : at + size]
                        for keep, got, sizes in zip(self.keeps, self.gots, self.splits)
                        for whole in [_scatter_whole(jnp.stack(keep), *got)]
                        for at, size, turned in sizes
                    ]
                return
            keeps = [keep[place] for keep in self.keeps]
            pieces = [
                [(part, i) for part in got for i in range(part.shape[0])][place]
                for got in self.gots
            ]
            gots = [part for part, _ in pieces]
            indices = [i for _, i in pieces]
            results = run(
                ring_step, keeps, gots, indices, self.passed, self.splits if final else None, need=need
            )
            if final:
                self.results = results
            else:
                self.passed = [_ring(results[0])]

    class AllSum:
        def __init__(self, value, axes, sent):
            self.value = value
            self.sent = sent
            self.hops = []
            for axis in axes:
                size = lax.axis_size(axis)
                step = 1
                while step < size:
                    self.hops.append((axis, [(i, i ^ step) for i in range(size)]))
                    step *= 2
            self.start()

        def start(self):
            if self.hops:
                axis, pairs = self.hops.pop(0)
                self.got = lax.ppermute(self.value.astype(self.sent), axis, pairs)

        def step(self, need=()):
            self.value = run(add_hop, self.value, self.got, need=need)
            self.got = None
            self.start()

        def rest(self):
            while self.got is not None:
                self.step()
            return self.value

    first_sends = run(
        weight_gradient, feed_groups, BLOCKS, (), ((4,),), LONG, need=[column_a]
    )
    feed_got = [across(first_sends[0])]
    mixer_a, back_a, two_a = run(
        second_back, 0, own_a, column_a, cot_rows, residual_a, inverse_a, gain_two
    )
    mixer_column = _swap(mixer_a, "y")
    mixer_core = _swap(mixer_a, "c")
    own_b, other_b = run(add_core, feed_b[3], core_b)
    column_b = _swap(other_b, "y")
    feed_core = [_swap(f[6], "c") for f in feeds]
    feed_own, feed_other = zip(
        *[run(add_core, feeds[b][5], feed_core[b], need=[mixer_core]) for b in span],
        strict=True,
    )
    feed_parts = run(weight_gradient, feed_groups, BLOCKS, range(4), ((5,), (6, 7)))
    feed_got.append(across(feed_parts[4]))
    feed_keep = feed_parts[:4]
    mixer_column, *feed_keep = lax.optimization_barrier((mixer_column, *feed_keep))
    mixer_a = [mixer_a, mixer_column, mixer_core, _swap(mixer_column, "c")]
    mixer_b, back_b, two_b = run(
        second_back, 1, own_b, column_b, cot_rows, residual_b, inverse_b, gain_two
    )
    mixer_b_column = _swap(mixer_b, "y")
    mixer_b_core = _swap(mixer_b, "c")
    feed_column = _swap(jnp.stack(feed_other), "y")
    stride = feed_keep[0].shape[1] // 3
    feed_sum = Sum(
        [feed_keep],
        [feed_got],
        [[(i * stride, hidden_cols, True) for i in range(3)]],
    )
    feed_sum.step()

    def mix_back_of(b, cots, need=()):
        saved = (mixes[b][3], persist_key, persist_value, *mixes[b][4:8])
        return run(mix_backward, where[b], cots, saved, mix_weights, need=need)

    mix_back_a = mix_back_of(0, mixer_a, need=[mixer_b_core])
    core_a = _swap(mix_back_a[6], "c")
    mixer_b_column, last_part, *mix_back_a = lax.optimization_barrier(
        (mixer_b_column, feed_parts[5], *mix_back_a)
    )
    feed_got.append(across(last_part))
    mixer_b = [mixer_b, mixer_b_column, mixer_b_core, _swap(mixer_b_column, "c")]
    feed_sum.step()
    layer_out = deal_out(run(finish_rows, BLOCKS, where, feed_own, feed_column, residual, LONG))
    own_a, other_a = run(add_core, mix_back_a[5], core_a)
    column_a = _swap(other_a, "y")
    mix_back_b = mix_back_of(1, mixer_b)
    backs = [mix_back_a, mix_back_b]
    core_b = _swap(mix_back_b[6], "c")
    feed_sum.step()
    project_groups = [
        [(plain([m[0]]), k[0]) for m, k in zip(mixes, backs)],
        [(plain(mixer), m[4]) for mixer, m in ((mixer_a, mix_a), (mixer_b, mix_b))],
    ]
    run(tick, need=[layer_out])
    first_sends = run(weight_gradient, project_groups, BLOCKS, (), ((4,),))
    project_got = [across(first_sends[0])]
    own_b, other_b = run(add_core, mix_back_b[5], core_b)
    column_b = _swap(other_b, "y")
    memory_sum = AllSum(
        run(join_sums, mix_back_a[1:5], mix_back_b[1:5]), DP[::-1], BF
    )
    project_parts = run(weight_gradient, project_groups, BLOCKS, range(4), ((5,), (6, 7)))
    project_keep = project_parts[:4]
    if ring_sized:
        project_got[0], *late = lax.optimization_barrier((project_got[0], *project_parts[4:]))
    else:
        late = project_parts[4:]
    project_got += [across(part) for part in late]
    rates_at = 3 * head_cols
    project_sum = Sum(
        [project_keep],
        [project_got],
        [
            [(i * head_cols, head_cols, False) for i in range(3)]
            + [(rates_at, rate_cols, False), (rates_at + 128, head_cols, False)]
        ],
    )
    project_sum.step()
    memory_sum.step()
    token_a, one_a = run(first_back, own_a, column_a, token_rows[0], back_a, gain_one)
    token_send, gains = run(
        last_rows,
        BLOCKS,
        where[1],
        own_b,
        column_b,
        token_rows[1],
        back_b,
        gain_one,
        token_a,
        one_a,
        two_a,
        two_b,
    )
    grad_tokens = deal_out(token_send)
    gain_sum = AllSum(gains, ("c", "y", "x", "z"), F32)
    gain_sum.step()
    project_sum.step()
    feed_sum.step()
    gain_sum.step()
    memory_sum.step()
    gain_sum.step()
    project_sum.step()
    gain_sum.step()
    flat = memory_sum.rest()
    gains = gain_sum.rest()
    project_sum.step()
    gate_total, up_total, down_total = feed_sum.results
    *project_totals, out_total = project_sum.results

    memory_out = []
    start = 0
    for m in mix_back_a[1:5]:
        size = m.size // 128
        memory_out.append(flat[start : start + size].reshape(m.shape))
        start += size

    return (
        layer_out,
        grad_tokens,
        *project_totals,
        out_total,
        gate_total.T,
        up_total.T,
        down_total.T,
        gains[0],
        gains[1],
        memory_out[0],
        memory_out[1],
        memory_out[2],
        memory_out[3],
    )


def solution(mesh):
    sizes = mesh.devices.shape
    fine = Mesh(mesh.devices.reshape(sizes[0] // 2, 2, 2, sizes[1] // 2), ("z", "x", "y", "c"))
    tensor = ("y", "c")
    return jax.shard_map(
        per_device,
        mesh=fine,
        in_specs=(
            P(None, tensor, DP, None),
            P(None, tensor, DP, None),
            P(DP, tensor),
            P(DP, tensor),
            P(DP, tensor),
            P(DP, tensor),
            P(DP, tensor),
            P(DP, tensor),
            P(DP, tensor),
            P(DP, tensor),
            P(DP),
            P(DP),
            P(tensor, None, None),
            P(tensor, None, None),
            P(tensor, None, None),
            P(tensor, None, None),
            P(),
            P(),
        ),
        out_specs=(
            P(None, tensor, DP, None),
            P(None, tensor, DP, None),
            P(DP, tensor),
            P(DP, tensor),
            P(DP, tensor),
            P(DP, tensor),
            P(DP, tensor),
            P(DP, tensor),
            P(DP, tensor),
            P(DP, tensor),
            P(),
            P(),
            P(tensor, None, None),
            P(tensor, None, None),
            P(tensor, None, None),
            P(tensor, None, None),
        ),
        check_vma=False,
    )
```
